1024 devices in a mesh: gx: 16 (over z), gy: 64 (over x, y, core).
Axes of the slice: x: 4, y: 8, z: 16, core: 2. Of those that a mesh axis runs over, the one named last changes fastest.
Arguments:
- right_side: float32 [512, 16384], P('gx', 'gy'), may hold values from -6 to 6
- class_map: int32 [512, 16384], P('gx', 'gy'), may hold values from 0 to 3
- class_perm: float32 [4], replicated, may hold values from 0.05 to 20
- eigenvectors: float32 [40, 512, 16384], P(None, 'gx', 'gy'), may hold values from -0.0625 to 0.0625
- coarse_inverse: float32 [40960, 5120], P(('gx', 'gy')), may hold values from -4 to 40, as said below
Outputs:
- solution: float32 [512, 16384], P('gx', 'gy')
- residual: float32 [512, 16384], P('gx', 'gy')
The draws below stay inside these ranges and needn't reach their ends.
Inputs may be any that keep to these rules, and one draw needn't show every extreme that they name: `coarse_inverse`: each coarse group's 5120 x 5120 block is symmetric positive definite.
All inputs are finite; a program needn't handle non-finite values.
Results may differ from the reference program's by a relative error of at most 0.0003.
Values sent between devices are 32-bit elements; how exact they have to be, the bound alone decides.
No kernel may reach another device: no remote copies, remote signals or barrier semaphores. Data moves between devices by JAX's collectives and lax.ppermute only.
A program may use at most 32 MiB of HBM per device.

```python
import math
import jax
import jax.numpy as jnp
from jax import lax

CX = 32
CY = 256
NEV = 40
GROUP_ROWS = 2
NCLASS = 4
CHEB = 4
ITERS = 2
NX = 512
NY = 16384
SUBS = 1024
GROUP_DOFS = 5120
N_GX = 16
N_GY = 64


COARSE_GAIN = 8.0


def draw_coarse_inverse(key, part):
    key = jax.random.fold_in(key, 11)
    groups = SUBS * NEV // GROUP_DOFS
    spread = 0.35 / math.sqrt(GROUP_DOFS)
    entries = jax.random.truncated_normal(key, -4.0, 4.0, (groups, GROUP_DOFS, GROUP_DOFS), jnp.float32)
    symmetric = 0.5 * (entries + jnp.swapaxes(entries, 1, 2)) * spread
    identity = jnp.eye(GROUP_DOFS, dtype=jnp.float32)
    blocks = COARSE_GAIN * (identity[None] + symmetric)
    return blocks.reshape(groups * GROUP_DOFS, GROUP_DOFS)


def with_ends(values, key, smallest, high):
    spot = [jax.random.randint(jax.random.fold_in(key, axis), (), 0, length) for axis, length in enumerate(values.shape)]
    widest = values.shape.index(max(values.shape))
    next_to = spot[:widest] + [(spot[widest] + 1) % values.shape[widest]] + spot[widest + 1:]
    return values.at[tuple(spot)].set(smallest).at[tuple(next_to)].set(high)


def level_of(own_key, shape, split, smallest, top_value):
    loudness = 1.0
    for dim, blocks in split:
        draws = jax.random.uniform(jax.random.fold_in(jax.random.fold_in(own_key, 6), dim), (blocks,), jnp.float32, smallest / len(split), top_value / len(split))
        loudness = loudness * jnp.repeat(jnp.exp(draws), shape[dim] // blocks).reshape((-1,) + (1,) * (len(shape) - 1 - dim))
    return loudness


def bell_draw(key, shape, scale, reach, shards=(), kind=jnp.bfloat16):
    values = jax.random.normal(key, shape, jnp.float32) * scale
    if len(shards) > 0:
        values = level_of(key, shape, shards, -0.22, 0.18) * values
    return jnp.clip(values, min=-reach, max=reach).astype(kind)


def setup_inputs(seed: int = 0) -> dict:
    streams_of = jax.random.split(jax.random.key(seed), 6)
    return {
        "right_side": bell_draw(streams_of[0], (NX, NY), 1.0, 6.0, ((0, 16), (1, 64)), jnp.float32),
        "class_map": with_ends(jax.random.randint(streams_of[1], (NX, NY), 0, NCLASS), jax.random.fold_in(streams_of[1], 1), 0, NCLASS - 1).astype(jnp.int32),
        "class_perm": jnp.clip(jnp.exp(jax.random.uniform(streams_of[2], (NCLASS,), jnp.float32, math.log(0.05), math.log(20.0))), 0.05, 20.0),
        "eigenvectors": bell_draw(streams_of[3], (NEV, NX, NY), (CX * CY) ** -0.5, 0.0625, ((1, 16), (2, 64)), jnp.float32),
        "coarse_inverse": draw_coarse_inverse(jax.random.fold_in(streams_of[5], 71), 0),
    }


REACTION = 0.05
EIGEN_TOP = 2.0
EIGEN_LOW = 0.1
HIGHEST = lax.Precision.HIGHEST


def shifted(padded):
    return (padded[:-2, 1:-1], padded[2:, 1:-1], padded[1:-1, :-2], padded[1:-1, 2:])


def harmonic(centre, beside):
    return jnp.where(beside > 0.0, 2.0 * centre * beside / (centre + beside), centre)


def coefficients_of(centre, padded):
    face_terms = tuple(harmonic(centre, beside) for beside in shifted(padded))
    diagonal = REACTION + face_terms[0] + face_terms[1] + face_terms[2] + face_terms[3]
    return face_terms, diagonal


def operate(vector, neighbours, face_terms, diagonal):
    result = diagonal * vector
    for weight, beside in zip(face_terms, neighbours):
        result = result - weight * beside
    return result


def chebyshev(source, local_apply, diagonal):
    centre = 0.5 * (EIGEN_TOP + EIGEN_LOW)
    radius = 0.5 * (EIGEN_TOP - EIGEN_LOW)
    ratio_start = centre / radius
    factor = 1.0 / ratio_start
    update = (source / diagonal) / centre
    smoothed = update
    for degree in range(1, CHEB):
        defect = source - local_apply(smoothed)
        factor_next = 1.0 / (2.0 * ratio_start - factor)
        update = factor_next * factor * update + (2.0 * factor_next / radius) * (defect / diagonal)
        smoothed = smoothed + update
        factor = factor_next
    return smoothed


def reference(right_side, class_map, class_perm, eigenvectors, coarse_inverse):
    permeability = class_perm[class_map]
    face_terms, diagonal = coefficients_of(permeability, jnp.pad(permeability, 1))
    row_index = lax.broadcasted_iota(jnp.int32, (NX, NY), 0) % CX
    column_index = lax.broadcasted_iota(jnp.int32, (NX, NY), 1) % CY
    inside = (row_index != 0, row_index != CX - 1, column_index != 0, column_index != CY - 1)
    groups = N_GX // GROUP_ROWS
    blocks = eigenvectors.reshape(NEV, N_GX, CX, N_GY, CY)
    matrices = coarse_inverse.reshape(groups, GROUP_DOFS, GROUP_DOFS)

    def global_apply(vector):
        return operate(vector, shifted(jnp.pad(vector, 1)), face_terms, diagonal)

    def local_apply(vector):
        beside = shifted(jnp.pad(vector, 1))
        masked = tuple(jnp.where(keep_mask, near_cell, 0.0) for keep_mask, near_cell in zip(inside, beside))
        return operate(vector, masked, face_terms, diagonal)

    def precondition(source):
        smoothed = chebyshev(source, local_apply, diagonal)
        tiles = source.reshape(N_GX, CX, N_GY, CY)
        projected = jnp.einsum('eaxby,axby->abe', blocks, tiles, precision=HIGHEST)
        grouped = projected.reshape(groups, GROUP_DOFS)
        coarse = jnp.einsum('grc,gc->gr', matrices, grouped, precision=HIGHEST)
        coarse = coarse.reshape(N_GX, N_GY, NEV)
        prolonged = jnp.einsum('abe,eaxby->axby', coarse, blocks, precision=HIGHEST)
        return smoothed + prolonged.reshape(NX, NY)

    solution = jnp.zeros_like(right_side)
    residual = right_side
    preconditioned = precondition(residual)
    direction = preconditioned
    product_rz = jnp.sum(residual * preconditioned)
    for iteration in range(ITERS):
        operated = global_apply(direction)
        step_size = product_rz / jnp.sum(direction * operated)
        solution = solution + step_size * direction
        residual = residual - step_size * operated
        if iteration + 1 < ITERS:
            preconditioned = precondition(residual)
            product_next = jnp.sum(residual * preconditioned)
            direction = preconditioned + (product_next / product_rz) * direction
            product_rz = product_next
    return solution, residual
```

```python
import jax
import jax.numpy as jnp
from jax import lax
from jax.sharding import Mesh, PartitionSpec as P

CHEB = 4
REACTION = 0.05
EIGEN_TOP = 2.0
EIGEN_LOW = 0.1
HIGHEST = lax.Precision.HIGHEST

ROWS = ("zh", "zl")
COLS = ("xy", "core")
GROUP = ("zl", "xy", "core")
STACK = ("zh", "zl", "core")
PLANE = ("xy",)
FINE = ("zh", "zl", "xy", "core")


def spread(message, axes):
    count = 1
    for axis in axes:
        count *= lax.axis_size(axis)
    copies = jnp.broadcast_to(message[None], (count,) + message.shape)
    return lax.all_to_all(copies, axes, 0, 0, tiled=True)


def moved(x, axes, by):
    count = lax.axis_size(axes)
    pairs = [(i, i + by) for i in range(count) if 0 <= i + by < count]
    return lax.ppermute(x, axes, pairs)


def harmonic(centre, beside):
    return jnp.where(beside > 0.0, 2.0 * centre * beside / (centre + beside), centre)


def beside(v, up, down, left, right):
    return (
        jnp.concatenate([up, v[:-1]], axis=0),
        jnp.concatenate([v[1:], down], axis=0),
        jnp.concatenate([left, v[:, :-1]], axis=1),
        jnp.concatenate([v[:, 1:], right], axis=1),
    )


def beside_inside(v):
    row, column = jnp.zeros_like(v[:1]), jnp.zeros_like(v[:, :1])
    return beside(v, row, row, column, column)


def operate(vector, neighbours, face_terms, diagonal):
    result = diagonal * vector
    for weight, near in zip(face_terms, neighbours):
        result = result - weight * near
    return result


def chebyshev(source, local_apply, diagonal):
    centre = 0.5 * (EIGEN_TOP + EIGEN_LOW)
    radius = 0.5 * (EIGEN_TOP - EIGEN_LOW)
    ratio_start = centre / radius
    factor = 1.0 / ratio_start
    update = source / diagonal / centre
    smoothed = update
    for degree in range(1, CHEB):
        defect = source - local_apply(smoothed)
        factor_next = 1.0 / (2.0 * ratio_start - factor)
        update = factor_next * factor * update + 2.0 * factor_next / radius * (defect / diagonal)
        smoothed = smoothed + update
        factor = factor_next
    return smoothed


def padded(parts, width):
    used = sum(p.shape[0] for p in parts)
    return jnp.concatenate(parts + [jnp.zeros((width - used,), jnp.float32)])


def local(right_side, class_map, class_perm, eigenvectors, coarse_inverse):
    rows, columns = right_side.shape
    nev = eigenvectors.shape[0]
    z_count, z = lax.axis_size(ROWS), lax.axis_index(ROWS)
    b_count, b = lax.axis_size(COLS), lax.axis_index(COLS)
    zl = lax.axis_index("zl")
    xy_count, xy = lax.axis_size("xy"), lax.axis_index("xy")
    core = lax.axis_index("core")

    classes = jnp.arange(class_perm.shape[0], dtype=jnp.int32)
    perm = jnp.sum(
        jnp.where(class_map[None] == classes[:, None, None], class_perm[:, None, None], 0.0), axis=0
    )
    perm_up = moved(perm[-1:], ROWS, 1)
    perm_down = moved(perm[:1], ROWS, -1)

    def project(v):
        return jnp.einsum("eij,ij->e", eigenvectors, v, precision=HIGHEST)

    def prolong(gathered):
        grouped = gathered[:, :nev].reshape(-1)
        coarse = jnp.dot(coarse_inverse, grouped, precision=HIGHEST)
        return jnp.einsum("e,eij->ij", coarse, eigenvectors, precision=HIGHEST)

    first = spread(padded([project(right_side), perm[:, 0], perm[:, -1]], 128), GROUP)
    place = zl * b_count + b
    at_left = lax.dynamic_index_in_dim(first, jnp.maximum(place - 1, 0), 0, keepdims=False)
    at_right = lax.dynamic_index_in_dim(
        first, jnp.minimum(place + 1, first.shape[0] - 1), 0, keepdims=False
    )
    perm_left = jnp.where(b > 0, at_left[nev + rows : nev + 2 * rows], 0.0)[:, None]
    perm_right = jnp.where(b < b_count - 1, at_right[nev : nev + rows], 0.0)[:, None]
    near = beside(perm, perm_up, perm_down, perm_left, perm_right)
    faces = tuple(harmonic(perm, n) for n in near)
    diagonal = REACTION + faces[0] + faces[1] + faces[2] + faces[3]

    def local_apply(vector):
        return operate(vector, beside_inside(vector), faces, diagonal)

    z0 = chebyshev(right_side, local_apply, diagonal) + prolong(first)
    halo = (
        moved(z0[-1:], ROWS, 1),
        moved(z0[:1], ROWS, -1),
        moved(z0[:, -1:], COLS, 1),
        moved(z0[:, :1], COLS, -1),
    )
    q0 = operate(z0, beside(z0, *halo), faces, diagonal)
    second = spread(padded([project(q0)], 128), GROUP)
    w = chebyshev(q0, local_apply, diagonal) + prolong(second)
    inner = local_apply(w)

    scalars = jnp.stack([
        jnp.sum(right_side * z0),
        jnp.sum(z0 * q0),
        jnp.sum(right_side * w),
        jnp.sum(q0 * w),
        jnp.sum(w * inner),
    ])
    low = (faces[1] * w)[-1]
    right = (faces[3] * w)[:, -1]
    s = 2 * columns
    t = s + 2 * rows
    third = spread(padded([low, w[0], w[:, 0], right, scalars], t + 128 - t % 128), STACK)
    third = third.reshape(z_count, 2, -1)
    lows, tops = third[:, :, :columns], third[:, :, columns:s]
    lefts, rights = third[:, :, s : s + rows], third[:, :, s + rows : t]
    between = jnp.sum(lows[:-1] * tops[1:]) + jnp.sum(rights[:, 0] * lefts[:, 1])
    sums = jnp.sum(third[:, :, t : t + 5], axis=(0, 1)) - 2.0 * between * (jnp.arange(5) == 4)
    own = lax.dynamic_index_in_dim(third, core, 1, keepdims=False)
    from_up = lax.dynamic_index_in_dim(own, jnp.maximum(z - 1, 0), 0, keepdims=False)[:columns]
    from_down = lax.dynamic_index_in_dim(own, jnp.minimum(z + 1, z_count - 1), 0, keepdims=False)[
        columns:s
    ]
    mine = lax.dynamic_index_in_dim(third, z, 0, keepdims=False)

    wide = z_count * rows
    fourth = spread(
        padded([lefts[:, 0].reshape(-1), rights[:, 1].reshape(-1), sums], 2 * wide + 128), PLANE
    )
    outer_lefts, outer_rights = fourth[:, :wide], fourth[:, wide : 2 * wide]
    totals = jnp.sum(fourth[:, 2 * wide : 2 * wide + 5], axis=0)
    across = jnp.sum(outer_rights[:-1] * outer_lefts[1:])
    outer_left = lax.dynamic_slice(
        outer_rights, (jnp.maximum(xy - 1, 0), z * rows), (1, rows)
    )[0]
    outer_right = lax.dynamic_slice(
        outer_lefts, (jnp.minimum(xy + 1, xy_count - 1), z * rows), (1, rows)
    )[0]
    up = jnp.where(z > 0, from_up, 0.0)
    down = jnp.where(z < z_count - 1, from_down, 0.0) * faces[1][-1]
    left = jnp.where(core == 1, mine[0, s + rows : t], jnp.where(xy > 0, outer_left, 0.0))
    right_in = jnp.where(
        core == 0, mine[1, s : s + rows], jnp.where(xy < xy_count - 1, outer_right, 0.0)
    )
    right_in = right_in * faces[3][:, -1]
    row_id = lax.broadcasted_iota(jnp.int32, (rows, columns), 0)
    column_id = lax.broadcasted_iota(jnp.int32, (rows, columns), 1)
    v = inner - jnp.where(row_id == 0, up[None], 0.0) - jnp.where(row_id == rows - 1, down[None], 0.0)
    v = v - jnp.where(column_id == 0, left[:, None], 0.0)
    v = v - jnp.where(column_id == columns - 1, right_in[:, None], 0.0)

    rz, zq, rw, qw = totals[0], totals[1], totals[2], totals[3]
    wv = totals[4] - 2.0 * across
    step = rz / zq
    rz_new = rz - step * ((rw + zq) - step * qw)
    beta = rz_new / rz
    grow = 1.0 + beta
    curve = grow * grow * zq - 2.0 * grow * step * qw + step * step * wv
    step_next = rz_new / curve
    on_z = step + step_next * grow
    on_w = step_next * step
    solution = on_z * z0 - on_w * w
    residual = right_side - on_z * q0 + on_w * v
    return (solution, residual)


def solution(mesh):
    n_gx, n_gy = mesh.devices.shape
    fine = Mesh(mesh.devices.reshape(n_gx // 2, 2, n_gy // 2, 2), FINE)
    in_specs = (P(ROWS, COLS), P(ROWS, COLS), P(), P(None, ROWS, COLS), P(FINE, None))
    out_specs = (P(ROWS, COLS), P(ROWS, COLS))
    return jax.shard_map(local, mesh=fine, in_specs=in_specs, out_specs=out_specs, check_vma=False)
```

```python
import functools

import jax
import jax.numpy as jnp
from jax import lax
from jax.experimental import pallas as pl
from jax.experimental.pallas import tpu as pltpu
from jax.sharding import Mesh, PartitionSpec as P

CHEB = 4
REACTION = 0.05
EIGEN_TOP = 2.0
EIGEN_LOW = 0.1
LANES = 128

ROWS = ("zh", "zl")
COLS = ("xy", "core")
GROUP = ("zl", "xy", "core")
STACK = ("zh", "zl", "core")
PLANE = ("xy",)
FINE = ("zh", "zl", "xy", "core")
VMEM_LIMIT = 24 * 1024 * 1024


def iota(shape, dim):
    return lax.broadcasted_iota(jnp.int32, shape, dim)


def harmonic(centre, beside):
    return jnp.where(beside > 0.0, 2.0 * centre * beside / (centre + beside), centre)


def shifts(v):
    rows, columns = v.shape
    return (
        pltpu.roll(v, 1, 0),
        pltpu.roll(v, rows - 1, 0),
        pltpu.roll(v, 1, 1),
        pltpu.roll(v, columns - 1, 1),
    )


def edges_of(shape):
    row, column = iota(shape, 0), iota(shape, 1)
    return (row == 0, row == shape[0] - 1, column == 0, column == shape[1] - 1)


class Stencil:
    def __init__(self, coef):
        self.faces = tuple(coef[k] for k in range(4))
        self.diagonal, self.inverse = coef[4], coef[5]
        self.edges = edges_of(self.diagonal.shape)
        self.inner = tuple(
            jnp.where(edge, 0.0, face) for edge, face in zip(self.edges, self.faces)
        )

    def apply(self, v):
        result = self.diagonal * v
        for weight, near in zip(self.inner, shifts(v)):
            result = result - weight * near
        return result

    def smooth(self, source):
        centre = 0.5 * (EIGEN_TOP + EIGEN_LOW)
        radius = 0.5 * (EIGEN_TOP - EIGEN_LOW)
        ratio_start = centre / radius
        factor = 1.0 / ratio_start
        update = source * self.inverse * (1.0 / centre)
        smoothed = update
        for _ in range(1, CHEB):
            defect = source - self.apply(smoothed)
            factor_next = 1.0 / (2.0 * ratio_start - factor)
            update = factor_next * factor * update + (2.0 * factor_next / radius) * (
                defect * self.inverse
            )
            smoothed = smoothed + update
            factor = factor_next
        return smoothed


def to_lanes(column, start):
    n = column.shape[0]
    want = lax.rem(iota((n, LANES), 1) - start + 8 * LANES, LANES)
    hit = want == iota((n, LANES), 0)
    return jnp.sum(jnp.where(hit, column, 0.0), axis=0, keepdims=True)


def to_column(row, start, n):
    want = lax.rem(iota((n, LANES), 1) - start + 8 * LANES, LANES)
    hit = want == iota((n, LANES), 0)
    return jnp.sum(jnp.where(hit, row, 0.0), axis=1, keepdims=True)


def project(e_ref, v, rows_ref):
    nev, rows, columns = e_ref.shape
    for e in range(nev):
        p = e_ref[e] * v
        q = p[:, :LANES]
        for k in range(1, columns // LANES):
            q = q + p[:, k * LANES : (k + 1) * LANES]
        s = q[:8]
        for k in range(1, rows // 8):
            s = s + q[8 * k : 8 * k + 8]
        rows_ref[e : e + 1, :] = jnp.sum(s, axis=0, keepdims=True)
    return jnp.sum(rows_ref[...], axis=1, keepdims=True)


def coarse(c_ref, gathered_ref, nev):
    dofs = c_ref.shape[1]
    lane = iota((1, LANES), 1)
    total = None
    for r in range(dofs // LANES):
        low = r * LANES // nev
        high = (r * LANES + LANES - 1) // nev
        flat = gathered_ref[low : low + 1, :]
        for d in range(low + 1, high + 1):
            flat = jnp.where(lane >= d * nev - r * LANES, gathered_ref[d : d + 1, :], flat)
        term = c_ref[:, r * LANES : (r + 1) * LANES] * flat
        total = term if total is None else total + term
    return jnp.sum(total, axis=1, keepdims=True)


def prolong(e_ref, y, rows_ref):
    nev = e_ref.shape[0]
    rows_ref[...] = jnp.broadcast_to(y, (nev, LANES))
    reps = e_ref.shape[2] // LANES
    result = None
    for e in range(nev):
        weight = jnp.concatenate([rows_ref[e : e + 1, :]] * reps, axis=1)
        term = weight * e_ref[e]
        result = term if result is None else result + term
    return result


def total_of(v):
    return jnp.sum(jnp.sum(v, axis=0, keepdims=True), axis=1, keepdims=True)


def group_place():
    return (lax.axis_index("zl") * lax.axis_size("xy") + lax.axis_index("xy")) * 2 + lax.axis_index(
        "core"
    )


def lane_start(place, nev):
    return lax.rem(place * nev, LANES)


def opening_kernel(kinds_ref, r_ref, map_ref, e_ref, perm_ref, over_ref, in_ref, out_ref, rows_ref):
    nev, rows, _ = e_ref.shape
    classes = map_ref[...]
    perm = jnp.full(classes.shape, kinds_ref[0])
    for k in range(1, kinds_ref.shape[0]):
        perm = jnp.where(classes == k, kinds_ref[k], perm)
    perm_ref[...] = perm
    upper = lax.axis_index("zl") == 0
    over_ref[...] = jnp.where(upper, perm[:1], perm[-1:])
    in_ref[...] = jnp.where(upper, perm[-1:], perm[:1])
    c = project(e_ref, r_ref[...], rows_ref)
    start = lane_start(group_place(), nev)
    message = to_lanes(c, start) + to_lanes(perm[:, :1], start + nev)
    message = message + to_lanes(perm[:, -1:], start + nev + rows)
    out_ref[...] = jnp.broadcast_to(message, out_ref.shape)


def first_kernel(
    got_ref, over_ref, in_ref, perm_ref, r_ref, e_ref, c_ref,
    z_ref, coef_ref, z_over_ref, z_in_ref, y_over_ref, y_in_ref, rows_ref,
):
    nev, rows, columns = e_ref.shape
    xy, core = lax.axis_index("xy"), lax.axis_index("core")
    b = xy * 2 + core
    b_count = lax.axis_size("xy") * 2
    upper = lax.axis_index("zl") == 0
    place = group_place()
    before, after = jnp.maximum(place - 1, 0), jnp.minimum(place + 1, got_ref.shape[0] - 1)
    left = to_column(got_ref[pl.ds(before, 1), :], lane_start(before, nev) + nev + rows, rows)
    right = to_column(got_ref[pl.ds(after, 1), :], lane_start(after, nev) + nev, rows)
    left = jnp.where(b > 0, left, 0.0)
    right = jnp.where(b < b_count - 1, right, 0.0)
    over, within = over_ref[...], in_ref[...]
    halo = (jnp.where(upper, over, within), jnp.where(upper, within, over), left, right)
    perm = perm_ref[...]
    edges = edges_of(perm.shape)
    faces = []
    for edge, near, outside in zip(edges, shifts(perm), halo):
        faces.append(harmonic(perm, jnp.where(edge, outside, near)))
    diagonal = REACTION + faces[0] + faces[1] + faces[2] + faces[3]
    coef = faces + [diagonal, 1.0 / diagonal]
    for k in range(6):
        coef_ref[k] = coef[k]
    stencil = Stencil(coef)
    y = coarse(c_ref, got_ref, nev)
    z = stencil.smooth(r_ref[...]) + prolong(e_ref, y, rows_ref)
    z_ref[...] = z
    top, low = (faces[0] * z)[:1], (faces[1] * z)[-1:]
    z_over_ref[...] = jnp.where(upper, top, low)
    z_in_ref[...] = jnp.where(upper, low, top)
    lefts, rights = to_lanes((faces[2] * z)[:, :1], 0), to_lanes((faces[3] * z)[:, -1:], 0)
    y_over_ref[...] = jnp.where(core == 0, lefts, rights)
    y_in_ref[...] = jnp.where(core == 0, rights, lefts)


def second_kernel(
    z_over_ref, z_in_ref, y_over_ref, y_in_ref, z_ref, coef_ref, e_ref, q_ref, out_ref, rows_ref
):
    nev, rows, _ = e_ref.shape
    upper = lax.axis_index("zl") == 0
    first = lax.axis_index("core") == 0
    stencil = Stencil(coef_ref)
    over, within = z_over_ref[...], z_in_ref[...]
    y_over, y_in = to_column(y_over_ref[...], 0, rows), to_column(y_in_ref[...], 0, rows)
    halo = (
        jnp.where(upper, over, within),
        jnp.where(upper, within, over),
        jnp.where(first, y_over, y_in),
        jnp.where(first, y_in, y_over),
    )
    q = stencil.apply(z_ref[...])
    for edge, outside in zip(stencil.edges, halo):
        q = q - jnp.where(edge, outside, 0.0)
    q_ref[...] = q
    message = to_lanes(project(e_ref, q, rows_ref), lane_start(group_place(), nev))
    out_ref[...] = jnp.broadcast_to(message, out_ref.shape)


def third_kernel(
    got_ref, q_ref, z_ref, r_ref, coef_ref, e_ref, c_ref, w_ref, v_ref, out_ref, rows_ref, block_ref
):
    nev, rows, columns = e_ref.shape
    half = columns // LANES
    stencil = Stencil(coef_ref)
    q, z, r = q_ref[...], z_ref[...], r_ref[...]
    y = coarse(c_ref, got_ref, nev)
    w = stencil.smooth(q) + prolong(e_ref, y, rows_ref)
    v = stencil.apply(w)
    w_ref[...] = w
    v_ref[...] = v
    position = lax.rem(lax.axis_index("zh") * 2 + lax.axis_index("zl"), LANES // rows) * rows
    low = (stencil.faces[1] * w)[-1:]
    block_ref[...] = jnp.zeros_like(block_ref)
    for k in range(half):
        block_ref[k : k + 1, :] = low[:, k * LANES : (k + 1) * LANES]
        block_ref[half + k : half + k + 1, :] = w[:1, k * LANES : (k + 1) * LANES]
    block_ref[2 * half : 2 * half + 1, :] = to_lanes(w[:, :1], position)
    block_ref[2 * half + 1 : 2 * half + 2, :] = to_lanes(
        (stencil.faces[3] * w)[:, -1:], position
    )
    lane = iota((1, LANES), 1)
    sums = jnp.zeros((1, LANES), jnp.float32)
    for k, product in enumerate((r * z, z * q, r * w, q * w, w * v)):
        sums = jnp.where(lane == k, total_of(product), sums)
    block_ref[2 * half + 2 : 2 * half + 3, :] = sums
    out_ref[...] = jnp.broadcast_to(block_ref[...][None], out_ref.shape)


def fourth_kernel(got_ref, v_ref, coef_ref, v_out_ref, out_ref, block_ref):
    count, height, _ = got_ref.shape
    rows, columns = v_ref.shape
    half = columns // LANES
    z_count = count // 2
    z = lax.axis_index("zh") * 2 + lax.axis_index("zl")
    core = lax.axis_index("core")
    sub = iota((height, LANES), 0)
    lane = iota((1, LANES), 1)
    total = jnp.zeros((height, LANES), jnp.float32)
    flat = jnp.zeros((1, LANES), jnp.float32)
    for i in range(count):
        total = total + got_ref[i]
    for i in range(z_count - 1):
        for c in range(2):
            for k in range(half):
                here = got_ref[2 * i + c, k : k + 1, :]
                below = got_ref[2 * i + 2 + c, half + k : half + k + 1, :]
                flat = flat + here * below
    for i in range(z_count):
        flat = flat + (
            got_ref[2 * i, 2 * half + 1 : 2 * half + 2, :]
            * got_ref[2 * i + 1, 2 * half : 2 * half + 1, :]
        )
    between = jnp.sum(flat, axis=1, keepdims=True)
    sums = total[2 * half + 2 : 2 * half + 3]
    sums = jnp.where(lane == 4, sums - 2.0 * between, sums)
    pack = LANES // rows
    zr = z_count // pack
    for g in range(zr):
        lefts, rights = None, None
        for i in range(g * pack, (g + 1) * pack):
            a = got_ref[2 * i, 2 * half : 2 * half + 1, :]
            d = got_ref[2 * i + 1, 2 * half + 1 : 2 * half + 2, :]
            lefts = a if lefts is None else lefts + a
            rights = d if rights is None else rights + d
        block_ref[g : g + 1, :] = lefts
        block_ref[zr + g : zr + g + 1, :] = rights
    block_ref[2 * zr : 2 * zr + 1, :] = sums
    message = block_ref[...]
    size = block_ref.shape[0]
    for i in range(out_ref.shape[0] // size):
        out_ref[i * size : (i + 1) * size, :] = message

    above = got_ref[jnp.maximum(2 * z - 2 + core, 0)]
    below = got_ref[jnp.minimum(2 * z + 2 + core, count - 1)]
    up = jnp.concatenate([above[k : k + 1] for k in range(half)], axis=1)
    down = jnp.concatenate([below[half + k : half + k + 1] for k in range(half)], axis=1)
    up = jnp.where(z > 0, up, 0.0)
    down = jnp.where(z < z_count - 1, down, 0.0) * coef_ref[1, rows - 1 : rows, :]
    partner = got_ref[2 * z + 1 - core]
    position = lax.rem(z, pack) * rows
    left = to_column(partner[2 * half + 1 : 2 * half + 2], position, rows)
    right = to_column(partner[2 * half : 2 * half + 1], position, rows)
    edges = edges_of((rows, columns))
    v = v_ref[...]
    v = v - jnp.where(edges[0], up, 0.0) - jnp.where(edges[1], down, 0.0)
    v = v - jnp.where(edges[2], jnp.where(core == 1, left, 0.0), 0.0)
    v = v - jnp.where(edges[3], jnp.where(core == 0, right, 0.0) * coef_ref[3], 0.0)
    v_out_ref[...] = v


def closing_kernel(got_ref, v_ref, z_ref, w_ref, q_ref, r_ref, coef_ref, x_ref, res_ref):
    rows, columns = v_ref.shape
    pack = LANES // rows
    zr = lax.axis_size("zh") * 2 // pack
    size = 2 * zr + 1
    count = got_ref.shape[0] // size
    z = lax.axis_index("zh") * 2 + lax.axis_index("zl")
    xy, core = lax.axis_index("xy"), lax.axis_index("core")
    sums = got_ref[2 * zr : 2 * zr + 1, :]
    flat = jnp.zeros((zr, LANES), jnp.float32)
    for i in range(1, count):
        at = i * size
        sums = sums + got_ref[at + 2 * zr : at + 2 * zr + 1, :]
        flat = flat + got_ref[at - size + zr : at - size + 2 * zr, :] * got_ref[at : at + zr, :]
    across = total_of(flat)
    lane = iota((1, LANES), 1)
    rz, zq, rw, qw, wv = (
        jnp.sum(jnp.where(lane == k, sums, 0.0), axis=1, keepdims=True) for k in range(5)
    )
    wv = wv - 2.0 * across
    step = rz / zq
    rz_new = rz - step * ((rw + zq) - step * qw)
    grow = 1.0 + rz_new / rz
    curve = grow * grow * zq - 2.0 * grow * step * qw + step * step * wv
    step_next = rz_new / curve
    on_z = step + step_next * grow
    on_w = step_next * step

    left_of, right_of = jnp.maximum(xy - 1, 0), jnp.minimum(xy + 1, count - 1)
    row = z // pack
    position = lax.rem(z, pack) * rows
    left = to_column(got_ref[pl.ds(left_of * size + zr + row, 1), :], position, rows)
    right = to_column(got_ref[pl.ds(right_of * size + row, 1), :], position, rows)
    left = jnp.where((core == 0) & (xy > 0), left, 0.0)
    right = jnp.where((core == 1) & (xy < count - 1), right, 0.0)
    edges = edges_of((rows, columns))
    v = v_ref[...]
    v = v - jnp.where(edges[2], left, 0.0) - jnp.where(edges[3], right * coef_ref[3], 0.0)
    x_ref[...] = on_z * z_ref[...] - on_w * w_ref[...]
    res_ref[...] = r_ref[...] - on_z * q_ref[...] + on_w * v


def call(kernel, name, args, outs, scratch=(), smem=()):
    whole = pl.BlockSpec(memory_space=pltpu.VMEM)
    scalar = pl.BlockSpec(memory_space=pltpu.SMEM)
    return pl.pallas_call(
        kernel,
        out_shape=[jax.ShapeDtypeStruct(shape, jnp.float32) for shape in outs],
        in_specs=[scalar if k in smem else whole for k in range(len(args))],
        out_specs=[whole] * len(outs),
        scratch_shapes=[pltpu.VMEM(shape, jnp.float32) for shape in scratch],
        compiler_params=pltpu.CompilerParams(vmem_limit_bytes=VMEM_LIMIT),
        name=name,
    )(*args)


def exchanged(x, axes):
    return lax.all_to_all(x, axes, 0, 0, tiled=True)


def swap_in(x, axis):
    return lax.ppermute(x, axis, [(0, 1), (1, 0)])


def swap_over(x, axes):
    count = lax.axis_size(axes)
    pairs = [(i, i + 1) for i in range(1, count - 1, 2)]
    return lax.ppermute(x, axes, pairs + [(j, i) for i, j in pairs])


def local(right_side, class_map, class_perm, eigenvectors, coarse_inverse):
    rows, columns = right_side.shape
    nev = eigenvectors.shape[0]
    field = (rows, columns)
    group = 2 * lax.axis_size(COLS)
    z_count, chips = lax.axis_size(ROWS), lax.axis_size("xy")
    size = 2 * (z_count * rows // LANES) + 1
    per_vector = (nev, LANES)

    perm, over, within, message = call(
        opening_kernel, "opening", (class_perm, right_side, class_map, eigenvectors),
        [field, (1, columns), (1, columns), (group, LANES)], [per_vector], smem=(0,),
    )
    over, within = swap_over(over, ROWS), swap_in(within, "zl")
    got = exchanged(message, GROUP)
    z0, coef, z_over, z_in, y_over, y_in = call(
        first_kernel, "first",
        (got, over, within, perm, right_side, eigenvectors, coarse_inverse),
        [field, (6,) + field, (1, columns), (1, columns), (1, LANES), (1, LANES)], [per_vector],
    )
    z_over, z_in = swap_over(z_over, ROWS), swap_in(z_in, "zl")
    y_over, y_in = swap_over(y_over, COLS), swap_in(y_in, "core")
    q0, message = call(
        second_kernel, "second", (z_over, z_in, y_over, y_in, z0, coef, eigenvectors),
        [field, (group, LANES)], [per_vector],
    )
    got = exchanged(message, GROUP)
    w, v, message = call(
        third_kernel, "third", (got, q0, z0, right_side, coef, eigenvectors, coarse_inverse),
        [field, field, (2 * z_count, 8, LANES)], [per_vector, (8, LANES)],
    )
    got = exchanged(message, STACK)
    v, message = call(
        fourth_kernel, "fourth", (got, v, coef),
        [field, (chips * size, LANES)], [(size, LANES)],
    )
    got = exchanged(message.reshape(chips, size * LANES), PLANE).reshape(chips * size, LANES)
    return tuple(
        call(
            closing_kernel, "closing", (got, v, z0, w, q0, right_side, coef), [field, field]
        )
    )


def solution(mesh):
    n_gx, n_gy = mesh.devices.shape
    fine = Mesh(mesh.devices.reshape(n_gx // 2, 2, n_gy // 2, 2), FINE)
    in_specs = (P(ROWS, COLS), P(ROWS, COLS), P(), P(None, ROWS, COLS), P(FINE, None))
    out_specs = (P(ROWS, COLS), P(ROWS, COLS))
    return jax.shard_map(local, mesh=fine, in_specs=in_specs, out_specs=out_specs, check_vma=False)
```

```python
import jax
import jax.numpy as jnp
from jax import lax
from jax.experimental import pallas as pl
from jax.experimental.pallas import tpu as pltpu
from jax.sharding import Mesh, PartitionSpec as P

CHEB = 4
REACTION = 0.05
EIGEN_TOP = 2.0
EIGEN_LOW = 0.1
LANES = 128

ROWS = ("zh", "zl")
COLS = ("xy", "core")
GROUP = ("zl", "xy", "core")
STACK = ("zh", "zl", "core")
PLANE = ("xy",)
FINE = ("zh", "zl", "xy", "core")
VMEM_LIMIT = 24 * 1024 * 1024
PIECES = 5


def iota(shape, dim):
    return lax.broadcasted_iota(jnp.int32, shape, dim)


def harmonic(centre, beside):
    return jnp.where(beside > 0.0, 2.0 * centre * beside / (centre + beside), centre)


def shifts(v):
    rows, columns = v.shape
    return (
        pltpu.roll(v, 1, 0),
        pltpu.roll(v, rows - 1, 0),
        pltpu.roll(v, 1, 1),
        pltpu.roll(v, columns - 1, 1),
    )


def edges_of(shape):
    row, column = iota(shape, 0), iota(shape, 1)
    return (row == 0, row == shape[0] - 1, column == 0, column == shape[1] - 1)


class Stencil:
    def __init__(self, coef):
        self.faces = tuple(coef[k] for k in range(4))
        self.diagonal, self.inverse = coef[4], coef[5]
        self.edges = edges_of(self.diagonal.shape)
        self.inner = tuple(
            jnp.where(edge, 0.0, face) for edge, face in zip(self.edges, self.faces)
        )

    def apply(self, v):
        result = self.diagonal * v
        for weight, near in zip(self.inner, shifts(v)):
            result = result - weight * near
        return result

    def smooth(self, source):
        centre = 0.5 * (EIGEN_TOP + EIGEN_LOW)
        radius = 0.5 * (EIGEN_TOP - EIGEN_LOW)
        ratio_start = centre / radius
        factor = 1.0 / ratio_start
        update = source * self.inverse * (1.0 / centre)
        smoothed = update
        for _ in range(1, CHEB):
            defect = source - self.apply(smoothed)
            factor_next = 1.0 / (2.0 * ratio_start - factor)
            update = factor_next * factor * update + (2.0 * factor_next / radius) * (
                defect * self.inverse
            )
            smoothed = smoothed + update
            factor = factor_next
        return smoothed


def to_lanes(column, start):
    n = column.shape[0]
    want = lax.rem(iota((n, LANES), 1) - start + 8 * LANES, LANES)
    hit = want == iota((n, LANES), 0)
    return jnp.sum(jnp.where(hit, column, 0.0), axis=0, keepdims=True)


def to_column(row, start, n):
    want = lax.rem(iota((n, LANES), 1) - start + 8 * LANES, LANES)
    hit = want == iota((n, LANES), 0)
    return jnp.sum(jnp.where(hit, row, 0.0), axis=1, keepdims=True)


def project_one(own, v, rows_ref, e):
    rows, columns = v.shape
    p = own * v
    q = p[:, :LANES]
    for k in range(1, columns // LANES):
        q = q + p[:, k * LANES : (k + 1) * LANES]
    s = q[:8]
    for k in range(1, rows // 8):
        s = s + q[8 * k : 8 * k + 8]
    rows_ref[e : e + 1, :] = jnp.sum(s, axis=0, keepdims=True)


def project(e_ref, v, rows_ref):
    for e in range(e_ref.shape[0]):
        project_one(e_ref[e], v, rows_ref, e)
    return jnp.sum(rows_ref[...], axis=1, keepdims=True)


def coarse(c_ref, gathered_ref, nev):
    dofs = c_ref.shape[1]
    lane = iota((1, LANES), 1)
    total = None
    for r in range(dofs // LANES):
        low = r * LANES // nev
        high = (r * LANES + LANES - 1) // nev
        flat = gathered_ref[low : low + 1, :]
        for d in range(low + 1, high + 1):
            flat = jnp.where(lane >= d * nev - r * LANES, gathered_ref[d : d + 1, :], flat)
        term = c_ref[:, r * LANES : (r + 1) * LANES] * flat
        total = term if total is None else total + term
    return jnp.sum(total, axis=1, keepdims=True)


def prolong(e_ref, y, rows_ref):
    nev = e_ref.shape[0]
    rows_ref[...] = jnp.broadcast_to(y, (nev, LANES))
    reps = e_ref.shape[2] // LANES
    result = None
    for e in range(nev):
        weight = jnp.concatenate([rows_ref[e : e + 1, :]] * reps, axis=1)
        term = weight * e_ref[e]
        result = term if result is None else result + term
    return result


def total_of(v):
    return jnp.sum(jnp.sum(v, axis=0, keepdims=True), axis=1, keepdims=True)


def group_place():
    return (lax.axis_index("zl") * lax.axis_size("xy") + lax.axis_index("xy")) * 2 + lax.axis_index(
        "core"
    )


def column_place():
    return lax.axis_index("xy") * 2 + lax.axis_index("core")


def lane_start(place, nev):
    return lax.rem(place * nev, LANES)


def opening_kernel(
    kinds_hbm, r_hbm, map_hbm, e_hbm, c_hbm,
    perm_ref, over_ref, in_ref, e_over_ref, e_in_ref, out_ref, r_ref, e_ref, c_ref,
    kinds_ref, map_ref, rows_ref, sems,
):
    nev, rows, columns = e_ref.shape
    steps = sems.shape[0] - 4
    chunk = nev // steps
    small = [
        pltpu.make_async_copy(source, target, sems.at[k])
        for k, (source, target) in enumerate(
            ((kinds_hbm, kinds_ref), (map_hbm, map_ref), (r_hbm, r_ref))
        )
    ]
    parts = [
        pltpu.make_async_copy(
            e_hbm.at[pl.ds(k * chunk, chunk)], e_ref.at[pl.ds(k * chunk, chunk)], sems.at[4 + k]
        )
        for k in range(steps)
    ]
    matrix = pltpu.make_async_copy(c_hbm, c_ref, sems.at[3])
    for copy in small + parts + [matrix]:
        copy.start()
    for copy in small:
        copy.wait()
    classes = map_ref[...]
    perm = jnp.full(classes.shape, kinds_ref[0])
    for k in range(1, kinds_ref.shape[0]):
        perm = jnp.where(classes == k, kinds_ref[k], perm)
    perm_ref[...] = perm
    upper = lax.axis_index("zl") == 0
    first = lax.axis_index("core") == 0
    over_ref[...] = jnp.where(upper, perm[:1], perm[-1:])
    in_ref[...] = jnp.where(upper, perm[-1:], perm[:1])
    r = r_ref[...]
    lane = iota((rows, LANES), 1)
    lefts = jnp.zeros((rows, LANES), jnp.float32)
    rights = lefts
    for k in range(steps):
        parts[k].wait()
        for e in range(k * chunk, (k + 1) * chunk):
            own = e_ref[e]
            project_one(own, r, rows_ref, e)
            lefts = jnp.where(lane == e, own[:, :1], lefts)
            rights = jnp.where(lane == e, own[:, columns - 1 :], rights)
    e_over_ref[...] = jnp.where(first, lefts, rights)
    e_in_ref[...] = jnp.where(first, rights, lefts)
    c = jnp.sum(rows_ref[...], axis=1, keepdims=True)
    start = lane_start(group_place(), nev)
    message = to_lanes(c, start) + to_lanes(perm[:, :1], start + nev)
    message = message + to_lanes(perm[:, -1:], start + nev + rows)
    out_ref[...] = jnp.broadcast_to(message, out_ref.shape)
    matrix.wait()


def beside_columns(got_ref, stride, nev, rows):
    place, b, b_count = group_place(), column_place(), lax.axis_size("xy") * 2
    last = got_ref.shape[0] // stride - 1
    before, after = jnp.maximum(place - 1, 0), jnp.minimum(place + 1, last)
    left = to_column(
        got_ref[pl.ds(before * stride, 1), :], lane_start(before, nev) + nev + rows, rows
    )
    right = to_column(got_ref[pl.ds(after * stride, 1), :], lane_start(after, nev) + nev, rows)
    return jnp.where(b > 0, left, 0.0), jnp.where(b < b_count - 1, right, 0.0)


def first_kernel(
    got_ref, over_ref, in_ref, perm_ref, r_ref, e_ref, c_ref,
    z_ref, coef_ref, z_over_ref, z_in_ref, rows_ref,
):
    nev, rows, columns = e_ref.shape
    upper = lax.axis_index("zl") == 0
    left, right = beside_columns(got_ref, 1, nev, rows)
    over, within = over_ref[...], in_ref[...]
    halo = (jnp.where(upper, over, within), jnp.where(upper, within, over), left, right)
    perm = perm_ref[...]
    edges = edges_of(perm.shape)
    faces = []
    for edge, near, outside in zip(edges, shifts(perm), halo):
        faces.append(harmonic(perm, jnp.where(edge, outside, near)))
    diagonal = REACTION + faces[0] + faces[1] + faces[2] + faces[3]
    coef = faces + [diagonal, 1.0 / diagonal]
    for k in range(6):
        coef_ref[k] = coef[k]
    stencil = Stencil(coef)
    y = coarse(c_ref, got_ref, nev)
    z = stencil.smooth(r_ref[...]) + prolong(e_ref, y, rows_ref)
    z_ref[...] = z
    top, low = (faces[0] * z)[:1], (faces[1] * z)[-1:]
    z_over_ref[...] = jnp.where(upper, top, low)
    z_in_ref[...] = jnp.where(upper, low, top)


def second_kernel(
    z_over_ref, z_in_ref, e_over_ref, e_in_ref, z_ref, coef_ref, e_ref, q_ref, out_ref, rows_ref
):
    nev, rows, _ = e_ref.shape
    upper = lax.axis_index("zl") == 0
    first = lax.axis_index("core") == 0
    stencil = Stencil(coef_ref)
    over, within = z_over_ref[...], z_in_ref[...]
    z = z_ref[...]
    q = stencil.apply(z)
    q = q - jnp.where(stencil.edges[0], jnp.where(upper, over, within), 0.0)
    q = q - jnp.where(stencil.edges[1], jnp.where(upper, within, over), 0.0)
    q_ref[...] = q
    left, right = (stencil.faces[2] * z)[:, :1], (stencil.faces[3] * z)[:, -1:]
    start = lane_start(group_place(), nev)
    own = to_lanes(project(e_ref, q, rows_ref), start)
    own = own + to_lanes(left, start + nev) + to_lanes(right, start + nev + rows)
    e_over, e_in = e_over_ref[...], e_in_ref[...]
    to_left = jnp.sum(jnp.where(first, e_over, e_in) * left, axis=0, keepdims=True)
    to_right = jnp.sum(jnp.where(first, e_in, e_over) * right, axis=0, keepdims=True)
    added = pltpu.roll(to_left, lax.rem(start - nev + LANES, LANES), 1)
    added = added + pltpu.roll(to_right, lax.rem(start + nev, LANES), 1)
    sub = iota((8, LANES), 0)
    pair = jnp.where(lax.rem(sub, 2) == 0, own, -added)
    for k in range(out_ref.shape[0] // 8):
        out_ref[8 * k : 8 * k + 8, :] = pair


def third_kernel(
    got_ref, q_ref, z_ref, r_ref, coef_ref, e_ref, c_ref,
    q_out_ref, w_ref, v_ref, out_ref, rows_ref, block_ref, group_ref,
):
    nev, rows, columns = e_ref.shape
    half = columns // LANES
    count = group_ref.shape[0]
    stencil = Stencil(coef_ref)
    z, r = z_ref[...], r_ref[...]
    left, right = beside_columns(got_ref, 2, nev, rows)
    q = q_ref[...] - jnp.where(stencil.edges[2], left, 0.0)
    q = q - jnp.where(stencil.edges[3], right, 0.0)
    q_out_ref[...] = q
    added = got_ref[pl.ds(1, count, stride=2), :]
    group_ref[...] = (
        got_ref[pl.ds(0, count, stride=2), :]
        + pltpu.roll(added, 1, 0)
        + pltpu.roll(added, count - 1, 0)
    )
    y = coarse(c_ref, group_ref, nev)
    w = stencil.smooth(q) + prolong(e_ref, y, rows_ref)
    v = stencil.apply(w)
    w_ref[...] = w
    v_ref[...] = v
    low = (stencil.faces[1] * w)[-1:]
    for k in range(half):
        block_ref[k : k + 1, :] = low[:, k * LANES : (k + 1) * LANES]
        block_ref[half + k : half + k + 1, :] = w[:1, k * LANES : (k + 1) * LANES]
    last = to_lanes(w[:, :1], 0) + to_lanes((stencil.faces[3] * w)[:, -1:], rows)
    lane = iota((1, LANES), 1)
    for k, product in enumerate((r * z, z * q, r * w, q * w, w * v)):
        last = jnp.where(lane == 2 * rows + k, total_of(product), last)
    size = block_ref.shape[0]
    block_ref[size - 1 : size, :] = last
    message = block_ref[...]
    for i in range(out_ref.shape[0] // size):
        out_ref[i * size : (i + 1) * size, :] = message


def fourth_kernel(got_ref, v_ref, coef_ref, v_out_ref, out_ref, block_ref):
    rows, columns = v_ref.shape
    half = columns // LANES
    size = 2 * half + 1
    count = got_ref.shape[0] // size
    z_count = count // 2
    z = lax.axis_index("zh") * 2 + lax.axis_index("zl")
    core = lax.axis_index("core")
    flat = jnp.zeros((half, LANES), jnp.float32)
    for i in range(count - 2):
        at, below = i * size, (i + 2) * size
        flat = flat + got_ref[at : at + half, :] * got_ref[below + half : below + 2 * half, :]
    west = got_ref[pl.ds(2 * half, z_count, stride=2 * size), :]
    east = got_ref[pl.ds(2 * half + size, z_count, stride=2 * size), :]
    facing = jnp.where(iota((z_count, LANES), 1) < rows, pltpu.roll(west, LANES - rows, 1) * east, 0.0)
    between = total_of(flat) + total_of(facing)
    lane = iota((1, LANES), 1)
    sums = jnp.sum(west + east, axis=0, keepdims=True)
    sums = jnp.where(lane == 2 * rows + 4, sums - 2.0 * between, sums)
    pack = LANES // rows
    zr = z_count // pack
    wide = iota((zr, LANES), 1)
    lefts = jnp.zeros((zr, LANES), jnp.float32)
    rights = lefts
    for j in range(pack):
        a = got_ref[pl.ds(2 * half + 2 * size * j, zr, stride=2 * size * pack), :]
        d = got_ref[pl.ds(2 * half + size + 2 * size * j, zr, stride=2 * size * pack), :]
        a = jnp.where(wide < rows, a, 0.0)
        d = jnp.where((wide >= rows) & (wide < 2 * rows), d, 0.0)
        if j > 0:
            a = pltpu.roll(a, rows * j, 1)
        if j != 1:
            d = pltpu.roll(d, (rows * (j - 1)) % LANES, 1)
        lefts, rights = lefts + a, rights + d
    block_ref[:zr, :] = lefts
    block_ref[zr : 2 * zr, :] = rights
    block_ref[2 * zr : 2 * zr + 1, :] = sums
    message = block_ref[...]
    height = block_ref.shape[0]
    for i in range(out_ref.shape[0] // height):
        out_ref[i * height : (i + 1) * height, :] = message

    above = jnp.maximum(2 * z - 2 + core, 0) * size
    below = jnp.minimum(2 * z + 2 + core, count - 1) * size + half
    up = jnp.concatenate([got_ref[pl.ds(above + k, 1), :] for k in range(half)], axis=1)
    down = jnp.concatenate([got_ref[pl.ds(below + k, 1), :] for k in range(half)], axis=1)
    up = jnp.where(z > 0, up, 0.0)
    down = jnp.where(z < z_count - 1, down, 0.0) * coef_ref[1, rows - 1 : rows, :]
    partner = got_ref[pl.ds((2 * z + 1 - core) * size + 2 * half, 1), :]
    left, right = to_column(partner, rows, rows), to_column(partner, 0, rows)
    edges = edges_of((rows, columns))
    v = v_ref[...]
    v = v - jnp.where(edges[0], up, 0.0) - jnp.where(edges[1], down, 0.0)
    v = v - jnp.where(edges[2], jnp.where(core == 1, left, 0.0), 0.0)
    v = v - jnp.where(edges[3], jnp.where(core == 0, right, 0.0) * coef_ref[3], 0.0)
    v_out_ref[...] = v


def closing_kernel(got_ref, v_ref, z_ref, w_ref, q_ref, r_ref, coef_ref, x_ref, res_ref):
    rows, columns = v_ref.shape
    pack = LANES // rows
    zr = lax.axis_size("zh") * 2 // pack
    size = 2 * zr + 1
    count = got_ref.shape[0] // size
    z = lax.axis_index("zh") * 2 + lax.axis_index("zl")
    xy, core = lax.axis_index("xy"), lax.axis_index("core")
    sums = got_ref[2 * zr : 2 * zr + 1, :]
    flat = jnp.zeros((zr, LANES), jnp.float32)
    for i in range(1, count):
        at = i * size
        sums = sums + got_ref[at + 2 * zr : at + 2 * zr + 1, :]
        flat = flat + got_ref[at - size + zr : at - size + 2 * zr, :] * got_ref[at : at + zr, :]
    across = total_of(flat)
    lane = iota((1, LANES), 1)
    rz, zq, rw, qw, wv = (
        jnp.sum(jnp.where(lane == 2 * rows + k, sums, 0.0), axis=1, keepdims=True)
        for k in range(5)
    )
    wv = wv - 2.0 * across
    step = rz / zq
    rz_new = rz - step * ((rw + zq) - step * qw)
    grow = 1.0 + rz_new / rz
    curve = grow * grow * zq - 2.0 * grow * step * qw + step * step * wv
    step_next = rz_new / curve
    on_z = step + step_next * grow
    on_w = step_next * step

    left_of, right_of = jnp.maximum(xy - 1, 0), jnp.minimum(xy + 1, count - 1)
    row = z // pack
    position = lax.rem(z, pack) * rows
    left = to_column(got_ref[pl.ds(left_of * size + zr + row, 1), :], position, rows)
    right = to_column(got_ref[pl.ds(right_of * size + row, 1), :], position, rows)
    left = jnp.where((core == 0) & (xy > 0), left, 0.0)
    right = jnp.where((core == 1) & (xy < count - 1), right, 0.0)
    edges = edges_of((rows, columns))
    v = v_ref[...]
    v = v - jnp.where(edges[2], left, 0.0) - jnp.where(edges[3], right * coef_ref[3], 0.0)
    x_ref[...] = on_z * z_ref[...] - on_w * w_ref[...]
    res_ref[...] = r_ref[...] - on_z * q_ref[...] + on_w * v


def call(kernel, name, args, outs, scratch=(), by_hand=False):
    whole = pl.BlockSpec(memory_space=pltpu.VMEM)
    scratch = [pltpu.VMEM(x, jnp.float32) if isinstance(x, tuple) else x for x in scratch]
    return pl.pallas_call(
        kernel,
        out_shape=[jax.ShapeDtypeStruct(shape, jnp.float32) for shape in outs],
        in_specs=[pl.BlockSpec(memory_space=pl.ANY) if by_hand else whole] * len(args),
        out_specs=[whole] * len(outs),
        scratch_shapes=scratch,
        compiler_params=pltpu.CompilerParams(vmem_limit_bytes=VMEM_LIMIT),
        name=name,
    )(*args)


def exchanged(x, axes, rows):
    flat = x.reshape(x.shape[0] // rows, rows * LANES)
    return lax.all_to_all(flat, axes, 0, 0, tiled=True).reshape(x.shape)


def swap_in(x, axis):
    return lax.ppermute(x, axis, [(0, 1), (1, 0)])


def swap_over(x, axes):
    count = lax.axis_size(axes)
    pairs = [(i, i + 1) for i in range(1, count - 1, 2)]
    return lax.ppermute(x, axes, pairs + [(j, i) for i, j in pairs])


def local(right_side, class_map, class_perm, eigenvectors, coarse_inverse):
    rows, columns = right_side.shape
    nev = eigenvectors.shape[0]
    field = (rows, columns)
    group = 2 * lax.axis_size(COLS)
    z_count, chips = lax.axis_size(ROWS), lax.axis_size("xy")
    size = 2 * (columns // LANES) + 1
    size_next = 2 * (z_count * rows // LANES) + 1
    per_vector = (nev, LANES)

    perm, over, within, e_over, e_in, message, r, vectors, matrix = call(
        opening_kernel, "opening",
        (class_perm, right_side, class_map, eigenvectors, coarse_inverse),
        [field, (1, columns), (1, columns), (rows, LANES), (rows, LANES), (group, LANES),
         field, eigenvectors.shape, coarse_inverse.shape],
        [pltpu.SMEM(class_perm.shape, jnp.float32), pltpu.VMEM(field, jnp.int32), per_vector,
         pltpu.SemaphoreType.DMA((4 + PIECES,))],
        by_hand=True,
    )
    over, within = swap_over(over, ROWS), swap_in(within, "zl")
    e_over, e_in = swap_over(e_over, COLS), swap_in(e_in, "core")
    got = exchanged(message, GROUP, 1)
    z0, coef, z_over, z_in = call(
        first_kernel, "first", (got, over, within, perm, r, vectors, matrix),
        [field, (6,) + field, (1, columns), (1, columns)], [per_vector],
    )
    z_over, z_in = swap_over(z_over, ROWS), swap_in(z_in, "zl")
    q0, message = call(
        second_kernel, "second", (z_over, z_in, e_over, e_in, z0, coef, vectors),
        [field, (2 * group, LANES)], [per_vector],
    )
    got = exchanged(message, GROUP, 2)
    q0, w, v, message = call(
        third_kernel, "third", (got, q0, z0, r, coef, vectors, matrix),
        [field, field, field, (2 * z_count * size, LANES)],
        [per_vector, (size, LANES), (group, LANES)],
    )
    got = exchanged(message, STACK, size)
    v, message = call(
        fourth_kernel, "fourth", (got, v, coef),
        [field, (chips * size_next, LANES)], [(size_next, LANES)],
    )
    got = exchanged(message, PLANE, size_next)
    return tuple(call(closing_kernel, "closing", (got, v, z0, w, q0, r, coef), [field, field]))


def solution(mesh):
    n_gx, n_gy = mesh.devices.shape
    fine = Mesh(mesh.devices.reshape(n_gx // 2, 2, n_gy // 2, 2), FINE)
    in_specs = (P(ROWS, COLS), P(ROWS, COLS), P(), P(None, ROWS, COLS), P(FINE, None))
    out_specs = (P(ROWS, COLS), P(ROWS, COLS))
    return jax.shard_map(local, mesh=fine, in_specs=in_specs, out_specs=out_specs, check_vma=False)
```

```python
import jax
import jax.numpy as jnp
from jax import lax
from jax.experimental import pallas as pl
from jax.experimental.pallas import tpu as pltpu
from jax.sharding import Mesh, PartitionSpec as P

CHEB = 4
REACTION = 0.05
EIGEN_TOP = 2.0
EIGEN_LOW = 0.1
LANES = 128

ROWS = ("zh", "zl")
COLS = ("xy", "core")
GROUP = ("zl", "xy", "core")
STACK = ("zh", "zl", "core")
PLANE = ("xy",)
FINE = ("zh", "zl", "xy", "core")
VMEM_LIMIT = 24 * 1024 * 1024
PIECES = 5


def iota(shape, dim):
    return lax.broadcasted_iota(jnp.int32, shape, dim)


def harmonic(centre, beside):
    return jnp.where(beside > 0.0, 2.0 * centre * beside / (centre + beside), centre)


def shifts(v):
    rows, columns = v.shape
    return (
        pltpu.roll(v, 1, 0),
        pltpu.roll(v, rows - 1, 0),
        pltpu.roll(v, 1, 1),
        pltpu.roll(v, columns - 1, 1),
    )


def edges_of(shape):
    row, column = iota(shape, 0), iota(shape, 1)
    return (row == 0, row == shape[0] - 1, column == 0, column == shape[1] - 1)


class Stencil:
    def __init__(self, coef):
        self.faces = tuple(coef[k] for k in range(4))
        self.diagonal, self.inverse = coef[4], coef[5]
        self.edges = edges_of(self.diagonal.shape)
        self.inner = tuple(
            jnp.where(edge, 0.0, face) for edge, face in zip(self.edges, self.faces)
        )

    def apply(self, v):
        result = self.diagonal * v
        for weight, near in zip(self.inner, shifts(v)):
            result = result - weight * near
        return result

    def smooth(self, source):
        centre = 0.5 * (EIGEN_TOP + EIGEN_LOW)
        radius = 0.5 * (EIGEN_TOP - EIGEN_LOW)
        ratio_start = centre / radius
        factor = 1.0 / ratio_start
        update = source * self.inverse * (1.0 / centre)
        smoothed = update
        for _ in range(1, CHEB):
            defect = source - self.apply(smoothed)
            factor_next = 1.0 / (2.0 * ratio_start - factor)
            update = factor_next * factor * update + (2.0 * factor_next / radius) * (
                defect * self.inverse
            )
            smoothed = smoothed + update
            factor = factor_next
        return smoothed


def to_lanes(column, start):
    n = column.shape[0]
    want = lax.rem(iota((n, LANES), 1) - start + 8 * LANES, LANES)
    hit = want == iota((n, LANES), 0)
    return jnp.sum(jnp.where(hit, column, 0.0), axis=0, keepdims=True)


def to_column(row, start, n):
    want = lax.rem(iota((n, LANES), 1) - start + 8 * LANES, LANES)
    hit = want == iota((n, LANES), 0)
    return jnp.sum(jnp.where(hit, row, 0.0), axis=1, keepdims=True)


def project_one(own, v, rows_ref, e):
    rows, columns = v.shape
    p = own * v
    q = p[:, :LANES]
    for k in range(1, columns // LANES):
        q = q + p[:, k * LANES : (k + 1) * LANES]
    s = q[:8]
    for k in range(1, rows // 8):
        s = s + q[8 * k : 8 * k + 8]
    rows_ref[e : e + 1, :] = jnp.sum(s, axis=0, keepdims=True)


def project(e_ref, v, rows_ref):
    for e in range(e_ref.shape[0]):
        project_one(e_ref[e], v, rows_ref, e)
    return jnp.sum(rows_ref[...], axis=1, keepdims=True)


def coarse(c_ref, gathered_ref, nev, stride):
    dofs = c_ref.shape[1]
    lane = iota((1, LANES), 1)
    total = None
    for r in range(dofs // LANES):
        low = r * LANES // nev
        high = (r * LANES + LANES - 1) // nev
        flat = gathered_ref[low * stride : low * stride + 1, :]
        for d in range(low + 1, high + 1):
            row = gathered_ref[d * stride : d * stride + 1, :]
            flat = jnp.where(lane >= d * nev - r * LANES, row, flat)
        term = c_ref[:, r * LANES : (r + 1) * LANES] * flat
        total = term if total is None else total + term
    return jnp.sum(total, axis=1, keepdims=True)


def prolong(e_ref, y, rows_ref):
    nev = e_ref.shape[0]
    rows_ref[...] = jnp.broadcast_to(y, (nev, LANES))
    reps = e_ref.shape[2] // LANES
    result = None
    for e in range(nev):
        weight = jnp.concatenate([rows_ref[e : e + 1, :]] * reps, axis=1)
        term = weight * e_ref[e]
        result = term if result is None else result + term
    return result


def total_of(v):
    return jnp.sum(jnp.sum(v, axis=0, keepdims=True), axis=1, keepdims=True)


def group_place():
    return (lax.axis_index("zl") * lax.axis_size("xy") + lax.axis_index("xy")) * 2 + lax.axis_index(
        "core"
    )


def column_place():
    return lax.axis_index("xy") * 2 + lax.axis_index("core")


def lane_start(place, nev):
    return lax.rem(place * nev, LANES)


def opening_kernel(
    kinds_hbm, r_hbm, map_hbm, e_hbm, c_hbm,
    perm_ref, over_ref, out_ref, r_ref, e_ref, c_ref,
    kinds_ref, map_ref, rows_ref, block_ref, sems,
):
    nev, rows, columns = e_ref.shape
    steps = sems.shape[0] - 4
    chunk = nev // steps
    small = [
        pltpu.make_async_copy(source, target, sems.at[k])
        for k, (source, target) in enumerate(
            ((kinds_hbm, kinds_ref), (map_hbm, map_ref), (r_hbm, r_ref))
        )
    ]
    parts = [
        pltpu.make_async_copy(
            e_hbm.at[pl.ds(k * chunk, chunk)], e_ref.at[pl.ds(k * chunk, chunk)], sems.at[4 + k]
        )
        for k in range(steps)
    ]
    matrix = pltpu.make_async_copy(c_hbm, c_ref, sems.at[3])
    for copy in small + parts + [matrix]:
        copy.start()
    for copy in small:
        copy.wait()
    classes = map_ref[...]
    perm = jnp.full(classes.shape, kinds_ref[0])
    for k in range(1, kinds_ref.shape[0]):
        perm = jnp.where(classes == k, kinds_ref[k], perm)
    perm_ref[...] = perm
    upper = lax.axis_index("zl") == 0
    over_ref[...] = jnp.where(upper, perm[:1], perm[-1:])
    within = jnp.where(upper, perm[-1:], perm[:1])
    r = r_ref[...]
    for k in range(steps):
        parts[k].wait()
        for e in range(k * chunk, (k + 1) * chunk):
            project_one(e_ref[e], r, rows_ref, e)
    c = jnp.sum(rows_ref[...], axis=1, keepdims=True)
    start = lane_start(group_place(), nev)
    size = block_ref.shape[0]
    block_ref[:1, :] = (
        to_lanes(c, start)
        + to_lanes(perm[:, :1], start + nev)
        + to_lanes(perm[:, -1:], start + nev + rows)
    )
    for k in range(size - 1):
        block_ref[k + 1 : k + 2, :] = within[:, k * LANES : (k + 1) * LANES]
    message = block_ref[...]
    for i in range(out_ref.shape[0] // size):
        out_ref[i * size : (i + 1) * size, :] = message
    matrix.wait()


def beside_columns(got_ref, stride, nev, rows):
    place, b, b_count = group_place(), column_place(), lax.axis_size("xy") * 2
    last = got_ref.shape[0] // stride - 1
    before, after = jnp.maximum(place - 1, 0), jnp.minimum(place + 1, last)
    left = to_column(
        got_ref[pl.ds(before * stride, 1), :], lane_start(before, nev) + nev + rows, rows
    )
    right = to_column(got_ref[pl.ds(after * stride, 1), :], lane_start(after, nev) + nev, rows)
    return jnp.where(b > 0, left, 0.0), jnp.where(b < b_count - 1, right, 0.0)


def first_kernel(
    got_ref, over_ref, perm_ref, r_ref, e_ref, c_ref,
    z_ref, coef_ref, z_over_ref, z_in_ref, y_over_ref, y_in_ref, rows_ref,
):
    nev, rows, columns = e_ref.shape
    size = columns // LANES + 1
    upper = lax.axis_index("zl") == 0
    first = lax.axis_index("core") == 0
    left, right = beside_columns(got_ref, size, nev, rows)
    across = lax.axis_size("xy") * 2
    partner = (group_place() + jnp.where(upper, across, -across)) * size
    over = over_ref[...]
    within = jnp.concatenate(
        [got_ref[pl.ds(partner + 1 + k, 1), :] for k in range(size - 1)], axis=1
    )
    halo = (jnp.where(upper, over, within), jnp.where(upper, within, over), left, right)
    perm = perm_ref[...]
    edges = edges_of(perm.shape)
    faces = []
    for edge, near, outside in zip(edges, shifts(perm), halo):
        faces.append(harmonic(perm, jnp.where(edge, outside, near)))
    diagonal = REACTION + faces[0] + faces[1] + faces[2] + faces[3]
    coef = faces + [diagonal, 1.0 / diagonal]
    for k in range(6):
        coef_ref[k] = coef[k]
    stencil = Stencil(coef)
    y = coarse(c_ref, got_ref, nev, size)
    z = stencil.smooth(r_ref[...]) + prolong(e_ref, y, rows_ref)
    z_ref[...] = z
    top, low = (faces[0] * z)[:1], (faces[1] * z)[-1:]
    z_over_ref[...] = jnp.where(upper, top, low)
    z_in_ref[...] = jnp.where(upper, low, top)
    lefts, rights = to_lanes((faces[2] * z)[:, :1], 0), to_lanes((faces[3] * z)[:, -1:], 0)
    y_over_ref[...] = jnp.where(first, lefts, rights)
    y_in_ref[...] = jnp.where(first, rights, lefts)


def second_kernel(
    z_in_ref, y_over_ref, y_in_ref, z_over_ref, z_ref, coef_ref, e_ref, q_ref, out_ref, rows_ref
):
    nev, rows, _ = e_ref.shape
    upper = lax.axis_index("zl") == 0
    first = lax.axis_index("core") == 0
    stencil = Stencil(coef_ref)
    over, within = z_over_ref[...], z_in_ref[...]
    y_over, y_in = to_column(y_over_ref[...], 0, rows), to_column(y_in_ref[...], 0, rows)
    halo = (
        jnp.where(upper, over, within),
        jnp.where(upper, within, over),
        jnp.where(first, y_over, y_in),
        jnp.where(first, y_in, y_over),
    )
    q = stencil.apply(z_ref[...])
    for edge, outside in zip(stencil.edges, halo):
        q = q - jnp.where(edge, outside, 0.0)
    q_ref[...] = q
    message = to_lanes(project(e_ref, q, rows_ref), lane_start(group_place(), nev))
    out_ref[...] = jnp.broadcast_to(message, out_ref.shape)


def third_kernel(
    got_ref, q_ref, z_ref, r_ref, coef_ref, e_ref, c_ref,
    w_ref, v_ref, out_ref, rows_ref, block_ref,
):
    nev, rows, columns = e_ref.shape
    half = columns // LANES
    stencil = Stencil(coef_ref)
    q, z, r = q_ref[...], z_ref[...], r_ref[...]
    y = coarse(c_ref, got_ref, nev, 1)
    w = stencil.smooth(q) + prolong(e_ref, y, rows_ref)
    v = stencil.apply(w)
    w_ref[...] = w
    v_ref[...] = v
    low = (stencil.faces[1] * w)[-1:]
    for k in range(half):
        block_ref[k : k + 1, :] = low[:, k * LANES : (k + 1) * LANES]
        block_ref[half + k : half + k + 1, :] = w[:1, k * LANES : (k + 1) * LANES]
    last = to_lanes(w[:, :1], 0) + to_lanes((stencil.faces[3] * w)[:, -1:], rows)
    lane = iota((1, LANES), 1)
    for k, product in enumerate((r * z, z * q, r * w, q * w, w * v)):
        last = jnp.where(lane == 2 * rows + k, total_of(product), last)
    size = block_ref.shape[0]
    block_ref[size - 1 : size, :] = last
    message = block_ref[...]
    for i in range(out_ref.shape[0] // size):
        out_ref[i * size : (i + 1) * size, :] = message


def fourth_kernel(got_ref, v_ref, coef_ref, v_out_ref, out_ref, block_ref):
    rows, columns = v_ref.shape
    half = columns // LANES
    size = 2 * half + 1
    count = got_ref.shape[0] // size
    z_count = count // 2
    z = lax.axis_index("zh") * 2 + lax.axis_index("zl")
    core = lax.axis_index("core")
    flat = jnp.zeros((half, LANES), jnp.float32)
    for i in range(count - 2):
        at, below = i * size, (i + 2) * size
        flat = flat + got_ref[at : at + half, :] * got_ref[below + half : below + 2 * half, :]
    west = got_ref[pl.ds(2 * half, z_count, stride=2 * size), :]
    east = got_ref[pl.ds(2 * half + size, z_count, stride=2 * size), :]
    facing = jnp.where(iota((z_count, LANES), 1) < rows, pltpu.roll(west, LANES - rows, 1) * east, 0.0)
    between = total_of(flat) + total_of(facing)
    lane = iota((1, LANES), 1)
    sums = jnp.sum(west + east, axis=0, keepdims=True)
    sums = jnp.where(lane == 2 * rows + 4, sums - 2.0 * between, sums)
    pack = LANES // rows
    zr = z_count // pack
    wide = iota((zr, LANES), 1)
    lefts = jnp.zeros((zr, LANES), jnp.float32)
    rights = lefts
    for j in range(pack):
        a = got_ref[pl.ds(2 * half + 2 * size * j, zr, stride=2 * size * pack), :]
        d = got_ref[pl.ds(2 * half + size + 2 * size * j, zr, stride=2 * size * pack), :]
        a = jnp.where(wide < rows, a, 0.0)
        d = jnp.where((wide >= rows) & (wide < 2 * rows), d, 0.0)
        if j > 0:
            a = pltpu.roll(a, rows * j, 1)
        if j != 1:
            d = pltpu.roll(d, (rows * (j - 1)) % LANES, 1)
        lefts, rights = lefts + a, rights + d
    block_ref[:zr, :] = lefts
    block_ref[zr : 2 * zr, :] = rights
    block_ref[2 * zr : 2 * zr + 1, :] = sums
    message = block_ref[...]
    height = block_ref.shape[0]
    for i in range(out_ref.shape[0] // height):
        out_ref[i * height : (i + 1) * height, :] = message

    above = jnp.maximum(2 * z - 2 + core, 0) * size
    below = jnp.minimum(2 * z + 2 + core, count - 1) * size + half
    up = jnp.concatenate([got_ref[pl.ds(above + k, 1), :] for k in range(half)], axis=1)
    down = jnp.concatenate([got_ref[pl.ds(below + k, 1), :] for k in range(half)], axis=1)
    up = jnp.where(z > 0, up, 0.0)
    down = jnp.where(z < z_count - 1, down, 0.0) * coef_ref[1, rows - 1 : rows, :]
    partner = got_ref[pl.ds((2 * z + 1 - core) * size + 2 * half, 1), :]
    left, right = to_column(partner, rows, rows), to_column(partner, 0, rows)
    edges = edges_of((rows, columns))
    v = v_ref[...]
    v = v - jnp.where(edges[0], up, 0.0) - jnp.where(edges[1], down, 0.0)
    v = v - jnp.where(edges[2], jnp.where(core == 1, left, 0.0), 0.0)
    v = v - jnp.where(edges[3], jnp.where(core == 0, right, 0.0) * coef_ref[3], 0.0)
    v_out_ref[...] = v


def closing_kernel(got_ref, v_ref, z_ref, w_ref, q_ref, r_ref, coef_ref, x_ref, res_ref):
    rows, columns = v_ref.shape
    pack = LANES // rows
    zr = lax.axis_size("zh") * 2 // pack
    size = 2 * zr + 1
    count = got_ref.shape[0] // size
    z = lax.axis_index("zh") * 2 + lax.axis_index("zl")
    xy, core = lax.axis_index("xy"), lax.axis_index("core")
    sums = got_ref[2 * zr : 2 * zr + 1, :]
    flat = jnp.zeros((zr, LANES), jnp.float32)
    for i in range(1, count):
        at = i * size
        sums = sums + got_ref[at + 2 * zr : at + 2 * zr + 1, :]
        flat = flat + got_ref[at - size + zr : at - size + 2 * zr, :] * got_ref[at : at + zr, :]
    across = total_of(flat)
    lane = iota((1, LANES), 1)
    rz, zq, rw, qw, wv = (
        jnp.sum(jnp.where(lane == 2 * rows + k, sums, 0.0), axis=1, keepdims=True)
        for k in range(5)
    )
    wv = wv - 2.0 * across
    step = rz / zq
    rz_new = rz - step * ((rw + zq) - step * qw)
    grow = 1.0 + rz_new / rz
    curve = grow * grow * zq - 2.0 * grow * step * qw + step * step * wv
    step_next = rz_new / curve
    on_z = step + step_next * grow
    on_w = step_next * step

    left_of, right_of = jnp.maximum(xy - 1, 0), jnp.minimum(xy + 1, count - 1)
    row = z // pack
    position = lax.rem(z, pack) * rows
    left = to_column(got_ref[pl.ds(left_of * size + zr + row, 1), :], position, rows)
    right = to_column(got_ref[pl.ds(right_of * size + row, 1), :], position, rows)
    left = jnp.where((core == 0) & (xy > 0), left, 0.0)
    right = jnp.where((core == 1) & (xy < count - 1), right, 0.0)
    edges = edges_of((rows, columns))
    v = v_ref[...]
    v = v - jnp.where(edges[2], left, 0.0) - jnp.where(edges[3], right * coef_ref[3], 0.0)
    x_ref[...] = on_z * z_ref[...] - on_w * w_ref[...]
    res_ref[...] = r_ref[...] - on_z * q_ref[...] + on_w * v


def call(kernel, name, args, outs, scratch=(), by_hand=False):
    whole = pl.BlockSpec(memory_space=pltpu.VMEM)
    scratch = [pltpu.VMEM(x, jnp.float32) if isinstance(x, tuple) else x for x in scratch]
    return pl.pallas_call(
        kernel,
        out_shape=[jax.ShapeDtypeStruct(shape, jnp.float32) for shape in outs],
        in_specs=[pl.BlockSpec(memory_space=pl.ANY) if by_hand else whole] * len(args),
        out_specs=[whole] * len(outs),
        scratch_shapes=scratch,
        compiler_params=pltpu.CompilerParams(vmem_limit_bytes=VMEM_LIMIT),
        name=name,
    )(*args)


def exchanged(x, axes, rows):
    flat = x.reshape(x.shape[0] // rows, rows * LANES)
    return lax.all_to_all(flat, axes, 0, 0, tiled=True).reshape(x.shape)


def swap_in(x, axis):
    return lax.ppermute(x, axis, [(0, 1), (1, 0)])


def swap_over(x, axes):
    count = lax.axis_size(axes)
    pairs = [(i, i + 1) for i in range(1, count - 1, 2)]
    return lax.ppermute(x, axes, pairs + [(j, i) for i, j in pairs])


def local(right_side, class_map, class_perm, eigenvectors, coarse_inverse):
    rows, columns = right_side.shape
    nev = eigenvectors.shape[0]
    field = (rows, columns)
    group = 2 * lax.axis_size(COLS)
    z_count, chips = lax.axis_size(ROWS), lax.axis_size("xy")
    size = 2 * (columns // LANES) + 1
    size_next = 2 * (z_count * rows // LANES) + 1
    per_vector = (nev, LANES)

    size_first = columns // LANES + 1
    given = (class_perm, right_side, class_map, eigenvectors, coarse_inverse)
    perm, over, message, r, vectors, matrix = call(
        opening_kernel, "opening",
        tuple(pltpu.with_memory_space_constraint(x, pltpu.HBM) for x in given),
        [field, (1, columns), (size_first * group, LANES),
         field, eigenvectors.shape, coarse_inverse.shape],
        [pltpu.SMEM(class_perm.shape, jnp.float32), pltpu.VMEM(field, jnp.int32), per_vector,
         (size_first, LANES), pltpu.SemaphoreType.DMA((4 + PIECES,))],
        by_hand=True,
    )
    over = swap_over(over, ROWS)
    got = exchanged(message, GROUP, size_first)
    z0, coef, z_over, z_in, y_over, y_in = call(
        first_kernel, "first", (got, over, perm, r, vectors, matrix),
        [field, (6,) + field, (1, columns), (1, columns), (1, LANES), (1, LANES)], [per_vector],
    )
    y_over, z_in = swap_over(y_over, COLS), swap_in(z_in, "zl")
    y_in, z_over = swap_in(y_in, "core"), swap_over(z_over, ROWS)
    q0, message = call(
        second_kernel, "second", (z_in, y_over, y_in, z_over, z0, coef, vectors),
        [field, (group, LANES)], [per_vector],
    )
    got = exchanged(message, GROUP, 1)
    w, v, message = call(
        third_kernel, "third", (got, q0, z0, r, coef, vectors, matrix),
        [field, field, (2 * z_count * size, LANES)], [per_vector, (size, LANES)],
    )
    got = exchanged(message, STACK, size)
    v, message = call(
        fourth_kernel, "fourth", (got, v, coef),
        [field, (chips * size_next, LANES)], [(size_next, LANES)],
    )
    got = exchanged(message, PLANE, size_next)
    return tuple(call(closing_kernel, "closing", (got, v, z0, w, q0, r, coef), [field, field]))


def solution(mesh):
    n_gx, n_gy = mesh.devices.shape
    fine = Mesh(mesh.devices.reshape(n_gx // 2, 2, n_gy // 2, 2), FINE)
    in_specs = (P(ROWS, COLS), P(ROWS, COLS), P(), P(None, ROWS, COLS), P(FINE, None))
    out_specs = (P(ROWS, COLS), P(ROWS, COLS))
    return jax.shard_map(local, mesh=fine, in_specs=in_specs, out_specs=out_specs, check_vma=False)
```

```python
import jax
import jax.numpy as jnp
from jax import lax
from jax.experimental import pallas as pl
from jax.experimental.pallas import tpu as pltpu
from jax.sharding import Mesh, PartitionSpec as P

CHEB = 4
REACTION = 0.05
EIGEN_TOP = 2.0
EIGEN_LOW = 0.1
LANES = 128

ROWS = ("zh", "zl")
COLS = ("xy", "core")
GROUP = ("zl", "xy", "core")
STACK = ("zh", "zl", "core")
PLANE = ("xy",)
FINE = ("zh", "zl", "xy", "core")
VMEM_LIMIT = 24 * 1024 * 1024
PIECES = 5


def iota(shape, dim):
    return lax.broadcasted_iota(jnp.int32, shape, dim)


def harmonic(centre, beside):
    return jnp.where(beside > 0.0, 2.0 * centre * beside / (centre + beside), centre)


def shifts(v):
    rows, columns = v.shape
    return (
        pltpu.roll(v, 1, 0),
        pltpu.roll(v, rows - 1, 0),
        pltpu.roll(v, 1, 1),
        pltpu.roll(v, columns - 1, 1),
    )


def edges_of(shape):
    row, column = iota(shape, 0), iota(shape, 1)
    return (row == 0, row == shape[0] - 1, column == 0, column == shape[1] - 1)


class Stencil:
    def __init__(self, coef):
        self.faces = tuple(coef[k] for k in range(4))
        self.diagonal, self.inverse = coef[4], coef[5]
        self.edges = edges_of(self.diagonal.shape)
        self.inner = tuple(
            jnp.where(edge, 0.0, face) for edge, face in zip(self.edges, self.faces)
        )

    def apply(self, v):
        result = self.diagonal * v
        for weight, near in zip(self.inner, shifts(v)):
            result = result - weight * near
        return result

    def smooth(self, source):
        centre = 0.5 * (EIGEN_TOP + EIGEN_LOW)
        radius = 0.5 * (EIGEN_TOP - EIGEN_LOW)
        ratio_start = centre / radius
        factor = 1.0 / ratio_start
        update = source * self.inverse * (1.0 / centre)
        smoothed = update
        for _ in range(1, CHEB):
            defect = source - self.apply(smoothed)
            factor_next = 1.0 / (2.0 * ratio_start - factor)
            update = factor_next * factor * update + (2.0 * factor_next / radius) * (
                defect * self.inverse
            )
            smoothed = smoothed + update
            factor = factor_next
        return smoothed


def to_lanes(column, start):
    n = column.shape[0]
    want = lax.rem(iota((n, LANES), 1) - start + 8 * LANES, LANES)
    hit = want == iota((n, LANES), 0)
    return jnp.sum(jnp.where(hit, column, 0.0), axis=0, keepdims=True)


def to_column(row, start, n):
    want = lax.rem(iota((n, LANES), 1) - start + 8 * LANES, LANES)
    hit = want == iota((n, LANES), 0)
    return jnp.sum(jnp.where(hit, row, 0.0), axis=1, keepdims=True)


def project_one(own, v, rows_ref, e):
    rows, columns = v.shape
    p = own * v
    q = p[:, :LANES]
    for k in range(1, columns // LANES):
        q = q + p[:, k * LANES : (k + 1) * LANES]
    s = q[:8]
    for k in range(1, rows // 8):
        s = s + q[8 * k : 8 * k + 8]
    rows_ref[e : e + 1, :] = jnp.sum(s, axis=0, keepdims=True)


def project(e_ref, v, rows_ref):
    for e in range(e_ref.shape[0]):
        project_one(e_ref[e], v, rows_ref, e)
    return jnp.sum(rows_ref[...], axis=1, keepdims=True)


def coarse(c_ref, gathered_ref, nev, stride):
    dofs = c_ref.shape[1]
    lane = iota((1, LANES), 1)
    total = None
    for r in range(dofs // LANES):
        low = r * LANES // nev
        high = (r * LANES + LANES - 1) // nev
        flat = gathered_ref[low * stride : low * stride + 1, :]
        for d in range(low + 1, high + 1):
            row = gathered_ref[d * stride : d * stride + 1, :]
            flat = jnp.where(lane >= d * nev - r * LANES, row, flat)
        term = c_ref[:, r * LANES : (r + 1) * LANES] * flat
        total = term if total is None else total + term
    return jnp.sum(total, axis=1, keepdims=True)


def prolong(e_ref, y, rows_ref):
    nev = e_ref.shape[0]
    rows_ref[...] = jnp.broadcast_to(y, (nev, LANES))
    reps = e_ref.shape[2] // LANES
    result = None
    for e in range(nev):
        weight = jnp.concatenate([rows_ref[e : e + 1, :]] * reps, axis=1)
        term = weight * e_ref[e]
        result = term if result is None else result + term
    return result


def total_of(v):
    return jnp.sum(jnp.sum(v, axis=0, keepdims=True), axis=1, keepdims=True)


def fill(out_ref, message):
    size = message.shape[0]
    count = out_ref.shape[0] // size
    batch = min(8, count)
    for i in range(batch):
        out_ref[i * size : (i + 1) * size, :] = message
    pattern = out_ref[: batch * size, :]
    for k in range(1, count // batch):
        out_ref[k * batch * size : (k + 1) * batch * size, :] = pattern


def group_place():
    return (lax.axis_index("zl") * lax.axis_size("xy") + lax.axis_index("xy")) * 2 + lax.axis_index(
        "core"
    )


def column_place():
    return lax.axis_index("xy") * 2 + lax.axis_index("core")


def lane_start(place, nev):
    return lax.rem(place * nev, LANES)


def opening_kernel(
    kinds_hbm, r_hbm, map_hbm, e_hbm, c_hbm,
    perm_ref, over_ref, facing_ref, out_ref, r_ref, e_ref, c_ref,
    kinds_ref, map_ref, rows_ref, block_ref, sems,
):
    nev, rows, columns = e_ref.shape
    steps = sems.shape[0] - 4
    chunk = nev // steps
    small = [
        pltpu.make_async_copy(source, target, sems.at[k])
        for k, (source, target) in enumerate(
            ((kinds_hbm, kinds_ref), (map_hbm, map_ref), (r_hbm, r_ref))
        )
    ]
    parts = [
        pltpu.make_async_copy(
            e_hbm.at[pl.ds(k * chunk, chunk)], e_ref.at[pl.ds(k * chunk, chunk)], sems.at[4 + k]
        )
        for k in range(steps)
    ]
    matrix = pltpu.make_async_copy(c_hbm, c_ref, sems.at[3])
    for copy in small + parts + [matrix]:
        copy.start()
    for copy in small:
        copy.wait()
    classes = map_ref[...]
    perm = jnp.full(classes.shape, kinds_ref[0])
    for k in range(1, kinds_ref.shape[0]):
        perm = jnp.where(classes == k, kinds_ref[k], perm)
    perm_ref[...] = perm
    upper = lax.axis_index("zl") == 0
    over_ref[...] = jnp.where(upper, perm[:1], perm[-1:])
    within = jnp.where(upper, perm[-1:], perm[:1])
    r = r_ref[...]
    first = lax.axis_index("core") == 0
    block = pl.multiple_of(jnp.where(first, 0, columns - LANES), LANES)
    turn = jnp.where(first, 0, 1)
    lane = iota((rows, LANES), 1)
    facing = jnp.zeros((rows, LANES), jnp.float32)
    for k in range(steps):
        parts[k].wait()
        for e in range(k * chunk, (k + 1) * chunk):
            project_one(e_ref[e], r, rows_ref, e)
            edge = pltpu.roll(e_ref[e, :, pl.ds(block, LANES)], e + turn, 1)
            facing = jnp.where(lane == e, edge, facing)
    facing_ref[...] = facing
    c = jnp.sum(rows_ref[...], axis=1, keepdims=True)
    start = lane_start(group_place(), nev)
    size = block_ref.shape[0]
    block_ref[:1, :] = (
        to_lanes(c, start)
        + to_lanes(perm[:, :1], start + nev)
        + to_lanes(perm[:, -1:], start + nev + rows)
    )
    for k in range(size - 1):
        block_ref[k + 1 : k + 2, :] = within[:, k * LANES : (k + 1) * LANES]
    fill(out_ref, block_ref[...])
    matrix.wait()


def beside_columns(got_ref, stride, nev, rows):
    place, b, b_count = group_place(), column_place(), lax.axis_size("xy") * 2
    last = got_ref.shape[0] // stride - 1
    before, after = jnp.maximum(place - 1, 0), jnp.minimum(place + 1, last)
    left = to_column(
        got_ref[pl.ds(before * stride, 1), :], lane_start(before, nev) + nev + rows, rows
    )
    right = to_column(got_ref[pl.ds(after * stride, 1), :], lane_start(after, nev) + nev, rows)
    return jnp.where(b > 0, left, 0.0), jnp.where(b < b_count - 1, right, 0.0)


def first_kernel(
    got_ref, over_ref, perm_ref, r_ref, e_ref, c_ref,
    z_ref, coef_ref, z_over_ref, z_in_ref, y_in_ref, rows_ref,
):
    nev, rows, columns = e_ref.shape
    size = columns // LANES + 1
    upper = lax.axis_index("zl") == 0
    first = lax.axis_index("core") == 0
    left, right = beside_columns(got_ref, size, nev, rows)
    across = lax.axis_size("xy") * 2
    partner = (group_place() + jnp.where(upper, across, -across)) * size
    over = over_ref[...]
    within = jnp.concatenate(
        [got_ref[pl.ds(partner + 1 + k, 1), :] for k in range(size - 1)], axis=1
    )
    halo = (jnp.where(upper, over, within), jnp.where(upper, within, over), left, right)
    perm = perm_ref[...]
    edges = edges_of(perm.shape)
    faces = []
    for edge, near, outside in zip(edges, shifts(perm), halo):
        faces.append(harmonic(perm, jnp.where(edge, outside, near)))
    diagonal = REACTION + faces[0] + faces[1] + faces[2] + faces[3]
    coef = faces + [diagonal, 1.0 / diagonal]
    for k in range(6):
        coef_ref[k] = coef[k]
    stencil = Stencil(coef)
    y = coarse(c_ref, got_ref, nev, size)
    z = stencil.smooth(r_ref[...]) + prolong(e_ref, y, rows_ref)
    z_ref[...] = z
    top, low = (faces[0] * z)[:1], (faces[1] * z)[-1:]
    z_over_ref[...] = jnp.where(upper, top, low)
    z_in_ref[...] = jnp.where(upper, low, top)
    lefts, rights = to_lanes((faces[2] * z)[:, :1], 0), to_lanes((faces[3] * z)[:, -1:], 0)
    y_in_ref[...] = jnp.where(first, rights, lefts)


def second_kernel(
    z_in_ref, y_in_ref, z_over_ref, facing_ref, z_ref, coef_ref, e_ref, q_ref, out_ref, rows_ref
):
    nev, rows, _ = e_ref.shape
    upper = lax.axis_index("zl") == 0
    first = lax.axis_index("core") == 0
    stencil = Stencil(coef_ref)
    over, within = z_over_ref[...], z_in_ref[...]
    y_in = to_column(y_in_ref[...], 0, rows)
    halo = (
        jnp.where(upper, over, within),
        jnp.where(upper, within, over),
        jnp.where(first, 0.0, y_in),
        jnp.where(first, y_in, 0.0),
    )
    z = z_ref[...]
    q = stencil.apply(z)
    for edge, outside in zip(stencil.edges, halo):
        q = q - jnp.where(edge, outside, 0.0)
    q_ref[...] = q
    left, right = (stencil.faces[2] * z)[:, :1], (stencil.faces[3] * z)[:, -1:]
    edge = jnp.where(first, left, right)
    start = lane_start(group_place(), nev)
    own = to_lanes(project(e_ref, q, rows_ref), start) + to_lanes(edge, start + nev)
    added = jnp.sum(facing_ref[...] * edge, axis=0, keepdims=True)
    step = jnp.where(first, LANES - nev, nev)
    added = pltpu.roll(added, lax.rem(start + step, LANES), 1)
    sub = iota((8, LANES), 0)
    pair = jnp.where(lax.rem(sub, 2) == 0, own, -added)
    for k in range(out_ref.shape[0] // 8):
        out_ref[8 * k : 8 * k + 8, :] = pair


def third_kernel(
    got_ref, q_ref, z_ref, r_ref, coef_ref, e_ref, c_ref,
    q_out_ref, w_ref, v_ref, out_ref, rows_ref, block_ref, group_ref,
):
    nev, rows, columns = e_ref.shape
    half = columns // LANES
    stencil = Stencil(coef_ref)
    z, r = z_ref[...], r_ref[...]
    first = lax.axis_index("core") == 0
    place, b, count = group_place(), column_place(), group_ref.shape[0]
    near = jnp.where(first, jnp.maximum(place - 1, 0), jnp.minimum(place + 1, count - 1))
    edge = to_column(got_ref[pl.ds(2 * near, 1), :], lane_start(near, nev) + nev, rows)
    left = jnp.where(first & (b > 0), edge, 0.0)
    right = jnp.where((~first) & (b < lax.axis_size("xy") * 2 - 1), edge, 0.0)
    q = q_ref[...] - jnp.where(stencil.edges[2], left, 0.0)
    q = q - jnp.where(stencil.edges[3], right, 0.0)
    q_out_ref[...] = q
    added = got_ref[pl.ds(1, count, stride=2), :]
    group_ref[...] = (
        got_ref[pl.ds(0, count, stride=2), :]
        + pltpu.roll(added, 1, 0)
        + pltpu.roll(added, count - 1, 0)
    )
    y = coarse(c_ref, group_ref, nev, 1)
    w = stencil.smooth(q) + prolong(e_ref, y, rows_ref)
    v = stencil.apply(w)
    w_ref[...] = w
    v_ref[...] = v
    low = (stencil.faces[1] * w)[-1:]
    for k in range(half):
        block_ref[k : k + 1, :] = low[:, k * LANES : (k + 1) * LANES]
        block_ref[half + k : half + k + 1, :] = w[:1, k * LANES : (k + 1) * LANES]
    last = to_lanes(w[:, :1], 0) + to_lanes((stencil.faces[3] * w)[:, -1:], rows)
    lane = iota((1, LANES), 1)
    for k, product in enumerate((r * z, z * q, r * w, q * w, w * v)):
        last = jnp.where(lane == 2 * rows + k, total_of(product), last)
    size = block_ref.shape[0]
    block_ref[size - 1 : size, :] = last
    fill(out_ref, block_ref[...])


def fourth_kernel(got_ref, v_ref, coef_ref, v_out_ref, out_ref, block_ref):
    rows, columns = v_ref.shape
    half = columns // LANES
    size = 2 * half + 1
    count = got_ref.shape[0] // size
    z_count = count // 2
    z = lax.axis_index("zh") * 2 + lax.axis_index("zl")
    core = lax.axis_index("core")
    flat = jnp.zeros((half, LANES), jnp.float32)
    for i in range(count - 2):
        at, below = i * size, (i + 2) * size
        flat = flat + got_ref[at : at + half, :] * got_ref[below + half : below + 2 * half, :]
    west = got_ref[pl.ds(2 * half, z_count, stride=2 * size), :]
    east = got_ref[pl.ds(2 * half + size, z_count, stride=2 * size), :]
    facing = jnp.where(iota((z_count, LANES), 1) < rows, pltpu.roll(west, LANES - rows, 1) * east, 0.0)
    between = total_of(flat) + total_of(facing)
    lane = iota((1, LANES), 1)
    sums = jnp.sum(west + east, axis=0, keepdims=True)
    sums = jnp.where(lane == 2 * rows + 4, sums - 2.0 * between, sums)
    pack = LANES // rows
    zr = z_count // pack
    wide = iota((zr, LANES), 1)
    lefts = jnp.zeros((zr, LANES), jnp.float32)
    rights = lefts
    for j in range(pack):
        a = got_ref[pl.ds(2 * half + 2 * size * j, zr, stride=2 * size * pack), :]
        d = got_ref[pl.ds(2 * half + size + 2 * size * j, zr, stride=2 * size * pack), :]
        a = jnp.where(wide < rows, a, 0.0)
        d = jnp.where((wide >= rows) & (wide < 2 * rows), d, 0.0)
        if j > 0:
            a = pltpu.roll(a, rows * j, 1)
        if j != 1:
            d = pltpu.roll(d, (rows * (j - 1)) % LANES, 1)
        lefts, rights = lefts + a, rights + d
    block_ref[:zr, :] = lefts
    block_ref[zr : 2 * zr, :] = rights
    block_ref[2 * zr : 2 * zr + 1, :] = sums
    fill(out_ref, block_ref[...])

    above = jnp.maximum(2 * z - 2 + core, 0) * size
    below = jnp.minimum(2 * z + 2 + core, count - 1) * size + half
    up = jnp.concatenate([got_ref[pl.ds(above + k, 1), :] for k in range(half)], axis=1)
    down = jnp.concatenate([got_ref[pl.ds(below + k, 1), :] for k in range(half)], axis=1)
    up = jnp.where(z > 0, up, 0.0)
    down = jnp.where(z < z_count - 1, down, 0.0) * coef_ref[1, rows - 1 : rows, :]
    partner = got_ref[pl.ds((2 * z + 1 - core) * size + 2 * half, 1), :]
    left, right = to_column(partner, rows, rows), to_column(partner, 0, rows)
    edges = edges_of((rows, columns))
    v = v_ref[...]
    v = v - jnp.where(edges[0], up, 0.0) - jnp.where(edges[1], down, 0.0)
    v = v - jnp.where(edges[2], jnp.where(core == 1, left, 0.0), 0.0)
    v = v - jnp.where(edges[3], jnp.where(core == 0, right, 0.0) * coef_ref[3], 0.0)
    v_out_ref[...] = v


def closing_kernel(got_ref, v_ref, z_ref, w_ref, q_ref, r_ref, coef_ref, x_ref, res_ref):
    rows, columns = v_ref.shape
    pack = LANES // rows
    zr = lax.axis_size("zh") * 2 // pack
    size = 2 * zr + 1
    count = got_ref.shape[0] // size
    z = lax.axis_index("zh") * 2 + lax.axis_index("zl")
    xy, core = lax.axis_index("xy"), lax.axis_index("core")
    sums = got_ref[2 * zr : 2 * zr + 1, :]
    flat = jnp.zeros((zr, LANES), jnp.float32)
    for i in range(1, count):
        at = i * size
        sums = sums + got_ref[at + 2 * zr : at + 2 * zr + 1, :]
        flat = flat + got_ref[at - size + zr : at - size + 2 * zr, :] * got_ref[at : at + zr, :]
    across = total_of(flat)
    lane = iota((1, LANES), 1)
    rz, zq, rw, qw, wv = (
        jnp.sum(jnp.where(lane == 2 * rows + k, sums, 0.0), axis=1, keepdims=True)
        for k in range(5)
    )
    wv = wv - 2.0 * across
    step = rz / zq
    rz_new = rz - step * ((rw + zq) - step * qw)
    grow = 1.0 + rz_new / rz
    curve = grow * grow * zq - 2.0 * grow * step * qw + step * step * wv
    step_next = rz_new / curve
    on_z = step + step_next * grow
    on_w = step_next * step

    left_of, right_of = jnp.maximum(xy - 1, 0), jnp.minimum(xy + 1, count - 1)
    row = z // pack
    position = lax.rem(z, pack) * rows
    left = to_column(got_ref[pl.ds(left_of * size + zr + row, 1), :], position, rows)
    right = to_column(got_ref[pl.ds(right_of * size + row, 1), :], position, rows)
    left = jnp.where((core == 0) & (xy > 0), left, 0.0)
    right = jnp.where((core == 1) & (xy < count - 1), right, 0.0)
    edges = edges_of((rows, columns))
    v = v_ref[...]
    v = v - jnp.where(edges[2], left, 0.0) - jnp.where(edges[3], right * coef_ref[3], 0.0)
    x_ref[...] = on_z * z_ref[...] - on_w * w_ref[...]
    res_ref[...] = r_ref[...] - on_z * q_ref[...] + on_w * v


def call(kernel, name, args, outs, scratch=(), by_hand=False):
    whole = pl.BlockSpec(memory_space=pltpu.VMEM)
    scratch = [pltpu.VMEM(x, jnp.float32) if isinstance(x, tuple) else x for x in scratch]
    return pl.pallas_call(
        kernel,
        out_shape=[jax.ShapeDtypeStruct(shape, jnp.float32) for shape in outs],
        in_specs=[pl.BlockSpec(memory_space=pl.ANY) if by_hand else whole] * len(args),
        out_specs=[whole] * len(outs),
        scratch_shapes=scratch,
        compiler_params=pltpu.CompilerParams(vmem_limit_bytes=VMEM_LIMIT),
        name=name,
    )(*args)


def exchanged(x, axes, rows):
    flat = x.reshape(x.shape[0] // rows, rows * LANES)
    return lax.all_to_all(flat, axes, 0, 0, tiled=True).reshape(x.shape)


def swap_in(x, axis):
    return lax.ppermute(x, axis, [(0, 1), (1, 0)])


def swap_over(x, axes):
    count = lax.axis_size(axes)
    pairs = [(i, i + 1) for i in range(1, count - 1, 2)]
    return lax.ppermute(x, axes, pairs + [(j, i) for i, j in pairs])


def local(right_side, class_map, class_perm, eigenvectors, coarse_inverse):
    rows, columns = right_side.shape
    nev = eigenvectors.shape[0]
    field = (rows, columns)
    group = 2 * lax.axis_size(COLS)
    z_count, chips = lax.axis_size(ROWS), lax.axis_size("xy")
    size = 2 * (columns // LANES) + 1
    size_next = 2 * (z_count * rows // LANES) + 1
    per_vector = (nev, LANES)

    size_first = columns // LANES + 1
    given = (class_perm, right_side, class_map, eigenvectors, coarse_inverse)
    perm, over, facing, message, r, vectors, matrix = call(
        opening_kernel, "opening",
        tuple(pltpu.with_memory_space_constraint(x, pltpu.HBM) for x in given),
        [field, (1, columns), (rows, LANES), (size_first * group, LANES),
         field, eigenvectors.shape, coarse_inverse.shape],
        [pltpu.SMEM(class_perm.shape, jnp.float32), pltpu.VMEM(field, jnp.int32), per_vector,
         (size_first, LANES), pltpu.SemaphoreType.DMA((4 + PIECES,))],
        by_hand=True,
    )
    over, facing = swap_over(over, ROWS), swap_over(facing, COLS)
    got = exchanged(message, GROUP, size_first)
    z0, coef, z_over, z_in, y_in = call(
        first_kernel, "first", (got, over, perm, r, vectors, matrix),
        [field, (6,) + field, (1, columns), (1, columns), (1, LANES)], [per_vector],
    )
    z_in, y_in = swap_in(z_in, "zl"), swap_in(y_in, "core")
    z_over = swap_over(z_over, ROWS)
    q0, message = call(
        second_kernel, "second", (z_in, y_in, z_over, facing, z0, coef, vectors),
        [field, (2 * group, LANES)], [per_vector],
    )
    got = exchanged(message, GROUP, 2)
    q0, w, v, message = call(
        third_kernel, "third", (got, q0, z0, r, coef, vectors, matrix),
        [field, field, field, (2 * z_count * size, LANES)],
        [per_vector, (size, LANES), (group, LANES)],
    )
    got = exchanged(message, STACK, size)
    v, message = call(
        fourth_kernel, "fourth", (got, v, coef),
        [field, (chips * size_next, LANES)], [(size_next, LANES)],
    )
    got = exchanged(message, PLANE, size_next)
    return tuple(call(closing_kernel, "closing", (got, v, z0, w, q0, r, coef), [field, field]))


def solution(mesh):
    n_gx, n_gy = mesh.devices.shape
    fine = Mesh(mesh.devices.reshape(n_gx // 2, 2, n_gy // 2, 2), FINE)
    in_specs = (P(ROWS, COLS), P(ROWS, COLS), P(), P(None, ROWS, COLS), P(FINE, None))
    out_specs = (P(ROWS, COLS), P(ROWS, COLS))
    return jax.shard_map(local, mesh=fine, in_specs=in_specs, out_specs=out_specs, check_vma=False)
```

```python
import jax
import jax.numpy as jnp
from jax import lax
from jax.experimental import pallas as pl
from jax.experimental.pallas import tpu as pltpu
from jax.sharding import Mesh, PartitionSpec as P

CHEB = 4
REACTION = 0.05
EIGEN_TOP = 2.0
EIGEN_LOW = 0.1
LANES = 128

ROWS = ("zh", "zl")
COLS = ("xy", "core")
GROUP = ("zl", "xy", "core")
STACK = ("zh", "zl", "core")
PLANE = ("xy",)
FINE = ("zh", "zl", "xy", "core")
VMEM_LIMIT = 24 * 1024 * 1024
PIECES = 5


def iota(shape, dim):
    return lax.broadcasted_iota(jnp.int32, shape, dim)


def harmonic(centre, beside):
    return jnp.where(beside > 0.0, 2.0 * centre * beside / (centre + beside), centre)


def shifts(v):
    rows, columns = v.shape
    return (
        pltpu.roll(v, 1, 0),
        pltpu.roll(v, rows - 1, 0),
        pltpu.roll(v, 1, 1),
        pltpu.roll(v, columns - 1, 1),
    )


def edges_of(shape):
    row, column = iota(shape, 0), iota(shape, 1)
    return (row == 0, row == shape[0] - 1, column == 0, column == shape[1] - 1)


class Stencil:
    def __init__(self, coef):
        self.faces = tuple(coef[k] for k in range(4))
        self.diagonal, self.inverse = coef[4], coef[5]
        self.edges = edges_of(self.diagonal.shape)
        self.inner = tuple(
            jnp.where(edge, 0.0, face) for edge, face in zip(self.edges, self.faces)
        )

    def apply(self, v):
        result = self.diagonal * v
        for weight, near in zip(self.inner, shifts(v)):
            result = result - weight * near
        return result

    def smooth(self, source):
        centre = 0.5 * (EIGEN_TOP + EIGEN_LOW)
        radius = 0.5 * (EIGEN_TOP - EIGEN_LOW)
        ratio_start = centre / radius
        factor = 1.0 / ratio_start
        update = source * self.inverse * (1.0 / centre)
        smoothed = update
        for _ in range(1, CHEB):
            defect = source - self.apply(smoothed)
            factor_next = 1.0 / (2.0 * ratio_start - factor)
            update = factor_next * factor * update + (2.0 * factor_next / radius) * (
                defect * self.inverse
            )
            smoothed = smoothed + update
            factor = factor_next
        return smoothed


def to_lanes(column, start):
    n = column.shape[0]
    want = lax.rem(iota((n, LANES), 1) - start + 8 * LANES, LANES)
    hit = want == iota((n, LANES), 0)
    return jnp.sum(jnp.where(hit, column, 0.0), axis=0, keepdims=True)


def to_column(row, start, n):
    want = lax.rem(iota((n, LANES), 1) - start + 8 * LANES, LANES)
    hit = want == iota((n, LANES), 0)
    return jnp.sum(jnp.where(hit, row, 0.0), axis=1, keepdims=True)


def project_one(own, v, rows_ref, e):
    rows, columns = v.shape
    p = own * v
    q = p[:, :LANES]
    for k in range(1, columns // LANES):
        q = q + p[:, k * LANES : (k + 1) * LANES]
    s = q[:8]
    for k in range(1, rows // 8):
        s = s + q[8 * k : 8 * k + 8]
    rows_ref[e : e + 1, :] = jnp.sum(s, axis=0, keepdims=True)


def project(e_ref, v, rows_ref):
    for e in range(e_ref.shape[0]):
        project_one(e_ref[e], v, rows_ref, e)
    return jnp.sum(rows_ref[...], axis=1, keepdims=True)


def coarse(c_ref, gathered_ref, nev, stride):
    dofs = c_ref.shape[1]
    lane = iota((1, LANES), 1)
    total = None
    for r in range(dofs // LANES):
        low = r * LANES // nev
        high = (r * LANES + LANES - 1) // nev
        flat = gathered_ref[low * stride : low * stride + 1, :]
        for d in range(low + 1, high + 1):
            row = gathered_ref[d * stride : d * stride + 1, :]
            flat = jnp.where(lane >= d * nev - r * LANES, row, flat)
        term = c_ref[:, r * LANES : (r + 1) * LANES] * flat
        total = term if total is None else total + term
    return jnp.sum(total, axis=1, keepdims=True)


def prolong(e_ref, y, rows_ref):
    nev = e_ref.shape[0]
    rows_ref[...] = jnp.broadcast_to(y, (nev, LANES))
    reps = e_ref.shape[2] // LANES
    result = None
    for e in range(nev):
        weight = jnp.concatenate([rows_ref[e : e + 1, :]] * reps, axis=1)
        term = weight * e_ref[e]
        result = term if result is None else result + term
    return result


def total_of(v):
    return jnp.sum(jnp.sum(v, axis=0, keepdims=True), axis=1, keepdims=True)


def fill(out_ref, message):
    size = message.shape[0]
    count = out_ref.shape[0] // size
    batch = min(8, count)
    for i in range(batch):
        out_ref[i * size : (i + 1) * size, :] = message
    pattern = out_ref[: batch * size, :]
    for k in range(1, count // batch):
        out_ref[k * batch * size : (k + 1) * batch * size, :] = pattern


def group_place():
    return (lax.axis_index("zl") * lax.axis_size("xy") + lax.axis_index("xy")) * 2 + lax.axis_index(
        "core"
    )


def column_place():
    return lax.axis_index("xy") * 2 + lax.axis_index("core")


def lane_start(place, nev):
    return lax.rem(place * nev, LANES)


def opening_kernel(
    kinds_hbm, r_hbm, map_hbm, e_hbm, c_hbm,
    perm_ref, over_ref, facing_ref, out_ref, r_ref, e_ref, c_ref,
    kinds_ref, map_ref, rows_ref, block_ref, sems,
):
    nev, rows, columns = e_ref.shape
    steps = sems.shape[0] - 4
    chunk = nev // steps
    small = [
        pltpu.make_async_copy(source, target, sems.at[k])
        for k, (source, target) in enumerate(
            ((kinds_hbm, kinds_ref), (map_hbm, map_ref), (r_hbm, r_ref))
        )
    ]
    parts = [
        pltpu.make_async_copy(
            e_hbm.at[pl.ds(k * chunk, chunk)], e_ref.at[pl.ds(k * chunk, chunk)], sems.at[4 + k]
        )
        for k in range(steps)
    ]
    matrix = pltpu.make_async_copy(c_hbm, c_ref, sems.at[3])
    for copy in parts[:2] + small + parts[2:] + [matrix]:
        copy.start()
    for copy in small:
        copy.wait()
    classes = map_ref[...]
    perm = jnp.full(classes.shape, kinds_ref[0])
    for k in range(1, kinds_ref.shape[0]):
        perm = jnp.where(classes == k, kinds_ref[k], perm)
    perm_ref[...] = perm
    upper = lax.axis_index("zl") == 0
    over_ref[...] = jnp.where(upper, perm[:1], perm[-1:])
    within = jnp.where(upper, perm[-1:], perm[:1])
    r = r_ref[...]
    first = lax.axis_index("core") == 0
    block = pl.multiple_of(jnp.where(first, 0, columns - LANES), LANES)
    turn = jnp.where(first, 0, 1)
    lane = iota((rows, LANES), 1)
    facing = jnp.zeros((rows, LANES), jnp.float32)
    for k in range(steps):
        parts[k].wait()
        for e in range(k * chunk, (k + 1) * chunk):
            project_one(e_ref[e], r, rows_ref, e)
            edge = pltpu.roll(e_ref[e, :, pl.ds(block, LANES)], e + turn, 1)
            facing = jnp.where(lane == e, edge, facing)
    facing_ref[...] = facing
    c = jnp.sum(rows_ref[...], axis=1, keepdims=True)
    start = lane_start(group_place(), nev)
    size = block_ref.shape[0]
    block_ref[:1, :] = (
        to_lanes(c, start)
        + to_lanes(perm[:, :1], start + nev)
        + to_lanes(perm[:, -1:], start + nev + rows)
    )
    for k in range(size - 1):
        block_ref[k + 1 : k + 2, :] = within[:, k * LANES : (k + 1) * LANES]
    fill(out_ref, block_ref[...])
    matrix.wait()


def beside_columns(got_ref, stride, nev, rows):
    place, b, b_count = group_place(), column_place(), lax.axis_size("xy") * 2
    last = got_ref.shape[0] // stride - 1
    before, after = jnp.maximum(place - 1, 0), jnp.minimum(place + 1, last)
    left = to_column(
        got_ref[pl.ds(before * stride, 1), :], lane_start(before, nev) + nev + rows, rows
    )
    right = to_column(got_ref[pl.ds(after * stride, 1), :], lane_start(after, nev) + nev, rows)
    return jnp.where(b > 0, left, 0.0), jnp.where(b < b_count - 1, right, 0.0)


def first_kernel(
    got_ref, over_ref, _, perm_ref, r_ref, e_ref, c_ref,
    z_ref, coef_ref, z_over_ref, z_in_ref, y_in_ref, rows_ref,
):
    nev, rows, columns = e_ref.shape
    size = columns // LANES + 1
    upper = lax.axis_index("zl") == 0
    first = lax.axis_index("core") == 0
    left, right = beside_columns(got_ref, size, nev, rows)
    across = lax.axis_size("xy") * 2
    partner = (group_place() + jnp.where(upper, across, -across)) * size
    over = over_ref[...]
    within = jnp.concatenate(
        [got_ref[pl.ds(partner + 1 + k, 1), :] for k in range(size - 1)], axis=1
    )
    halo = (jnp.where(upper, over, within), jnp.where(upper, within, over), left, right)
    perm = perm_ref[...]
    edges = edges_of(perm.shape)
    faces = []
    for edge, near, outside in zip(edges, shifts(perm), halo):
        faces.append(harmonic(perm, jnp.where(edge, outside, near)))
    diagonal = REACTION + faces[0] + faces[1] + faces[2] + faces[3]
    coef = faces + [diagonal, 1.0 / diagonal]
    for k in range(6):
        coef_ref[k] = coef[k]
    stencil = Stencil(coef)
    y = coarse(c_ref, got_ref, nev, size)
    z = stencil.smooth(r_ref[...]) + prolong(e_ref, y, rows_ref)
    z_ref[...] = z
    top, low = (faces[0] * z)[:1], (faces[1] * z)[-1:]
    z_over_ref[...] = jnp.where(upper, top, low)
    z_in_ref[...] = jnp.where(upper, low, top)
    lefts, rights = to_lanes((faces[2] * z)[:, :1], 0), to_lanes((faces[3] * z)[:, -1:], 0)
    y_in_ref[...] = jnp.where(first, rights, lefts)


def second_kernel(
    z_in_ref, y_in_ref, z_over_ref, facing_ref, z_ref, coef_ref, e_ref, q_ref, out_ref, rows_ref
):
    nev, rows, _ = e_ref.shape
    upper = lax.axis_index("zl") == 0
    first = lax.axis_index("core") == 0
    stencil = Stencil(coef_ref)
    over, within = z_over_ref[...], z_in_ref[...]
    y_in = to_column(y_in_ref[...], 0, rows)
    halo = (
        jnp.where(upper, over, within),
        jnp.where(upper, within, over),
        jnp.where(first, 0.0, y_in),
        jnp.where(first, y_in, 0.0),
    )
    z = z_ref[...]
    q = stencil.apply(z)
    for edge, outside in zip(stencil.edges, halo):
        q = q - jnp.where(edge, outside, 0.0)
    q_ref[...] = q
    left, right = (stencil.faces[2] * z)[:, :1], (stencil.faces[3] * z)[:, -1:]
    edge = jnp.where(first, left, right)
    start = lane_start(group_place(), nev)
    own = to_lanes(project(e_ref, q, rows_ref), start) + to_lanes(edge, start + nev)
    added = jnp.sum(facing_ref[...] * edge, axis=0, keepdims=True)
    step = jnp.where(first, LANES - nev, nev)
    added = pltpu.roll(added, lax.rem(start + step, LANES), 1)
    sub = iota((8, LANES), 0)
    pair = jnp.where(lax.rem(sub, 2) == 0, own, -added)
    for k in range(out_ref.shape[0] // 8):
        out_ref[8 * k : 8 * k + 8, :] = pair


def third_kernel(
    got_ref, q_ref, z_ref, r_ref, coef_ref, e_ref, c_ref,
    q_out_ref, w_ref, v_ref, out_ref, rows_ref, block_ref, group_ref,
):
    nev, rows, columns = e_ref.shape
    half = columns // LANES
    stencil = Stencil(coef_ref)
    z, r = z_ref[...], r_ref[...]
    first = lax.axis_index("core") == 0
    place, b, count = group_place(), column_place(), group_ref.shape[0]
    near = jnp.where(first, jnp.maximum(place - 1, 0), jnp.minimum(place + 1, count - 1))
    edge = to_column(got_ref[pl.ds(2 * near, 1), :], lane_start(near, nev) + nev, rows)
    left = jnp.where(first & (b > 0), edge, 0.0)
    right = jnp.where((~first) & (b < lax.axis_size("xy") * 2 - 1), edge, 0.0)
    q = q_ref[...] - jnp.where(stencil.edges[2], left, 0.0)
    q = q - jnp.where(stencil.edges[3], right, 0.0)
    q_out_ref[...] = q
    added = got_ref[pl.ds(1, count, stride=2), :]
    group_ref[...] = (
        got_ref[pl.ds(0, count, stride=2), :]
        + pltpu.roll(added, 1, 0)
        + pltpu.roll(added, count - 1, 0)
    )
    y = coarse(c_ref, group_ref, nev, 1)
    w = stencil.smooth(q) + prolong(e_ref, y, rows_ref)
    v = stencil.apply(w)
    w_ref[...] = w
    v_ref[...] = v
    low = (stencil.faces[1] * w)[-1:]
    for k in range(half):
        block_ref[k : k + 1, :] = low[:, k * LANES : (k + 1) * LANES]
        block_ref[half + k : half + k + 1, :] = w[:1, k * LANES : (k + 1) * LANES]
    last = to_lanes(w[:, :1], 0) + to_lanes((stencil.faces[3] * w)[:, -1:], rows)
    lane = iota((1, LANES), 1)
    for k, product in enumerate((r * z, z * q, r * w, q * w, w * v)):
        last = jnp.where(lane == 2 * rows + k, total_of(product), last)
    size = block_ref.shape[0]
    block_ref[size - 1 : size, :] = last
    fill(out_ref, block_ref[...])


def fourth_kernel(got_ref, v_ref, coef_ref, v_out_ref, out_ref, block_ref):
    rows, columns = v_ref.shape
    half = columns // LANES
    size = 2 * half + 1
    count = got_ref.shape[0] // size
    z_count = count // 2
    z = lax.axis_index("zh") * 2 + lax.axis_index("zl")
    core = lax.axis_index("core")
    flat = jnp.zeros((half, LANES), jnp.float32)
    for i in range(count - 2):
        at, below = i * size, (i + 2) * size
        flat = flat + got_ref[at : at + half, :] * got_ref[below + half : below + 2 * half, :]
    west = got_ref[pl.ds(2 * half, z_count, stride=2 * size), :]
    east = got_ref[pl.ds(2 * half + size, z_count, stride=2 * size), :]
    facing = jnp.where(iota((z_count, LANES), 1) < rows, pltpu.roll(west, LANES - rows, 1) * east, 0.0)
    between = total_of(flat) + total_of(facing)
    lane = iota((1, LANES), 1)
    sums = jnp.sum(west + east, axis=0, keepdims=True)
    sums = jnp.where(lane == 2 * rows + 4, sums - 2.0 * between, sums)
    pack = LANES // rows
    zr = z_count // pack
    wide = iota((zr, LANES), 1)
    lefts = jnp.zeros((zr, LANES), jnp.float32)
    rights = lefts
    for j in range(pack):
        a = got_ref[pl.ds(2 * half + 2 * size * j, zr, stride=2 * size * pack), :]
        d = got_ref[pl.ds(2 * half + size + 2 * size * j, zr, stride=2 * size * pack), :]
        a = jnp.where(wide < rows, a, 0.0)
        d = jnp.where((wide >= rows) & (wide < 2 * rows), d, 0.0)
        if j > 0:
            a = pltpu.roll(a, rows * j, 1)
        if j != 1:
            d = pltpu.roll(d, (rows * (j - 1)) % LANES, 1)
        lefts, rights = lefts + a, rights + d
    block_ref[:zr, :] = lefts
    block_ref[zr : 2 * zr, :] = rights
    block_ref[2 * zr : 2 * zr + 1, :] = sums
    fill(out_ref, block_ref[...])

    above = jnp.maximum(2 * z - 2 + core, 0) * size
    below = jnp.minimum(2 * z + 2 + core, count - 1) * size + half
    up = jnp.concatenate([got_ref[pl.ds(above + k, 1), :] for k in range(half)], axis=1)
    down = jnp.concatenate([got_ref[pl.ds(below + k, 1), :] for k in range(half)], axis=1)
    up = jnp.where(z > 0, up, 0.0)
    down = jnp.where(z < z_count - 1, down, 0.0) * coef_ref[1, rows - 1 : rows, :]
    partner = got_ref[pl.ds((2 * z + 1 - core) * size + 2 * half, 1), :]
    left, right = to_column(partner, rows, rows), to_column(partner, 0, rows)
    edges = edges_of((rows, columns))
    v = v_ref[...]
    v = v - jnp.where(edges[0], up, 0.0) - jnp.where(edges[1], down, 0.0)
    v = v - jnp.where(edges[2], jnp.where(core == 1, left, 0.0), 0.0)
    v = v - jnp.where(edges[3], jnp.where(core == 0, right, 0.0) * coef_ref[3], 0.0)
    v_out_ref[...] = v


def closing_kernel(got_ref, v_ref, z_ref, w_ref, q_ref, r_ref, coef_ref, x_ref, res_ref):
    rows, columns = v_ref.shape
    pack = LANES // rows
    zr = lax.axis_size("zh") * 2 // pack
    size = 2 * zr + 1
    count = got_ref.shape[0] // size
    z = lax.axis_index("zh") * 2 + lax.axis_index("zl")
    xy, core = lax.axis_index("xy"), lax.axis_index("core")
    sums = got_ref[2 * zr : 2 * zr + 1, :]
    flat = jnp.zeros((zr, LANES), jnp.float32)
    for i in range(1, count):
        at = i * size
        sums = sums + got_ref[at + 2 * zr : at + 2 * zr + 1, :]
        flat = flat + got_ref[at - size + zr : at - size + 2 * zr, :] * got_ref[at : at + zr, :]
    across = total_of(flat)
    lane = iota((1, LANES), 1)
    rz, zq, rw, qw, wv = (
        jnp.sum(jnp.where(lane == 2 * rows + k, sums, 0.0), axis=1, keepdims=True)
        for k in range(5)
    )
    wv = wv - 2.0 * across
    step = rz / zq
    rz_new = rz - step * ((rw + zq) - step * qw)
    grow = 1.0 + rz_new / rz
    curve = grow * grow * zq - 2.0 * grow * step * qw + step * step * wv
    step_next = rz_new / curve
    on_z = step + step_next * grow
    on_w = step_next * step

    left_of, right_of = jnp.maximum(xy - 1, 0), jnp.minimum(xy + 1, count - 1)
    row = z // pack
    position = lax.rem(z, pack) * rows
    left = to_column(got_ref[pl.ds(left_of * size + zr + row, 1), :], position, rows)
    right = to_column(got_ref[pl.ds(right_of * size + row, 1), :], position, rows)
    left = jnp.where((core == 0) & (xy > 0), left, 0.0)
    right = jnp.where((core == 1) & (xy < count - 1), right, 0.0)
    edges = edges_of((rows, columns))
    v = v_ref[...]
    v = v - jnp.where(edges[2], left, 0.0) - jnp.where(edges[3], right * coef_ref[3], 0.0)
    x_ref[...] = on_z * z_ref[...] - on_w * w_ref[...]
    res_ref[...] = r_ref[...] - on_z * q_ref[...] + on_w * v


def call(kernel, name, args, outs, scratch=(), by_hand=False):
    whole = pl.BlockSpec(memory_space=pltpu.VMEM)
    scratch = [pltpu.VMEM(x, jnp.float32) if isinstance(x, tuple) else x for x in scratch]
    return pl.pallas_call(
        kernel,
        out_shape=[jax.ShapeDtypeStruct(shape, jnp.float32) for shape in outs],
        in_specs=[pl.BlockSpec(memory_space=pl.ANY) if by_hand else whole] * len(args),
        out_specs=[whole] * len(outs),
        scratch_shapes=scratch,
        compiler_params=pltpu.CompilerParams(vmem_limit_bytes=VMEM_LIMIT),
        name=name,
    )(*args)


def exchanged(x, axes, rows):
    flat = x.reshape(x.shape[0] // rows, rows * LANES)
    return lax.all_to_all(flat, axes, 0, 0, tiled=True).reshape(x.shape)


def swap_in(x, axis):
    return lax.ppermute(x, axis, [(0, 1), (1, 0)])


def swap_over(x, axes):
    count = lax.axis_size(axes)
    pairs = [(i, i + 1) for i in range(1, count - 1, 2)]
    return lax.ppermute(x, axes, pairs + [(j, i) for i, j in pairs])


def local(right_side, class_map, class_perm, eigenvectors, coarse_inverse):
    rows, columns = right_side.shape
    nev = eigenvectors.shape[0]
    field = (rows, columns)
    group = 2 * lax.axis_size(COLS)
    z_count, chips = lax.axis_size(ROWS), lax.axis_size("xy")
    size = 2 * (columns // LANES) + 1
    size_next = 2 * (z_count * rows // LANES) + 1
    per_vector = (nev, LANES)

    size_first = columns // LANES + 1
    given = (class_perm, right_side, class_map, eigenvectors, coarse_inverse)
    perm, over, facing, message, r, vectors, matrix = call(
        opening_kernel, "opening",
        tuple(pltpu.with_memory_space_constraint(x, pltpu.HBM) for x in given),
        [field, (1, columns), (rows, LANES), (size_first * group, LANES),
         field, eigenvectors.shape, coarse_inverse.shape],
        [pltpu.SMEM(class_perm.shape, jnp.float32), pltpu.VMEM(field, jnp.int32), per_vector,
         (size_first, LANES), pltpu.SemaphoreType.DMA((4 + PIECES,))],
        by_hand=True,
    )
    over, facing = swap_over(over, ROWS), swap_over(facing, COLS)
    got = exchanged(message, GROUP, size_first)
    z0, coef, z_over, z_in, y_in = call(
        first_kernel, "first", (got, over, facing, perm, r, vectors, matrix),
        [field, (6,) + field, (1, columns), (1, columns), (1, LANES)], [per_vector],
    )
    z_in, y_in = swap_in(z_in, "zl"), swap_in(y_in, "core")
    z_over = swap_over(z_over, ROWS)
    q0, message = call(
        second_kernel, "second", (z_in, y_in, z_over, facing, z0, coef, vectors),
        [field, (2 * group, LANES)], [per_vector],
    )
    got = exchanged(message, GROUP, 2)
    q0, w, v, message = call(
        third_kernel, "third", (got, q0, z0, r, coef, vectors, matrix),
        [field, field, field, (2 * z_count * size, LANES)],
        [per_vector, (size, LANES), (group, LANES)],
    )
    got = exchanged(message, STACK, size)
    v, message = call(
        fourth_kernel, "fourth", (got, v, coef),
        [field, (chips * size_next, LANES)], [(size_next, LANES)],
    )
    got = exchanged(message, PLANE, size_next)
    return tuple(call(closing_kernel, "closing", (got, v, z0, w, q0, r, coef), [field, field]))


def solution(mesh):
    n_gx, n_gy = mesh.devices.shape
    fine = Mesh(mesh.devices.reshape(n_gx // 2, 2, n_gy // 2, 2), FINE)
    in_specs = (P(ROWS, COLS), P(ROWS, COLS), P(), P(None, ROWS, COLS), P(FINE, None))
    out_specs = (P(ROWS, COLS), P(ROWS, COLS))
    return jax.shard_map(local, mesh=fine, in_specs=in_specs, out_specs=out_specs, check_vma=False)
```

```python
import jax
import jax.numpy as jnp
from jax import lax
from jax.experimental import pallas as pl
from jax.experimental.pallas import tpu as pltpu
from jax.sharding import Mesh, PartitionSpec as P

CHEB = 4
REACTION = 0.05
EIGEN_TOP = 2.0
EIGEN_LOW = 0.1
LANES = 128

ROWS = ("zh", "zl")
COLS = ("xy", "core")
GROUP = ("zl", "xy", "core")
STACK = ("zh", "zl", "core")
PLANE = ("xy",)
FINE = ("zh", "zl", "xy", "core")
VMEM_LIMIT = 24 * 1024 * 1024
PIECES = 5


def iota(shape, dim):
    return lax.broadcasted_iota(jnp.int32, shape, dim)


def harmonic(centre, beside):
    return jnp.where(beside > 0.0, 2.0 * centre * beside / (centre + beside), centre)


def shifts(v):
    rows, columns = v.shape
    return (
        pltpu.roll(v, 1, 0),
        pltpu.roll(v, rows - 1, 0),
        pltpu.roll(v, 1, 1),
        pltpu.roll(v, columns - 1, 1),
    )


def edges_of(shape):
    row, column = iota(shape, 0), iota(shape, 1)
    return (row == 0, row == shape[0] - 1, column == 0, column == shape[1] - 1)


class Stencil:
    def __init__(self, coef):
        self.faces = tuple(coef[k] for k in range(4))
        self.diagonal, self.inverse = coef[4], coef[5]
        self.edges = edges_of(self.diagonal.shape)
        self.inner = tuple(
            jnp.where(edge, 0.0, face) for edge, face in zip(self.edges, self.faces)
        )

    def apply(self, v):
        result = self.diagonal * v
        for weight, near in zip(self.inner, shifts(v)):
            result = result - weight * near
        return result

    def smooth(self, source):
        centre = 0.5 * (EIGEN_TOP + EIGEN_LOW)
        radius = 0.5 * (EIGEN_TOP - EIGEN_LOW)
        ratio_start = centre / radius
        factor = 1.0 / ratio_start
        update = source * self.inverse * (1.0 / centre)
        smoothed = update
        for _ in range(1, CHEB):
            defect = source - self.apply(smoothed)
            factor_next = 1.0 / (2.0 * ratio_start - factor)
            update = factor_next * factor * update + (2.0 * factor_next / radius) * (
                defect * self.inverse
            )
            smoothed = smoothed + update
            factor = factor_next
        return smoothed


def to_lanes(column, start):
    n = column.shape[0]
    want = lax.rem(iota((n, LANES), 1) - start + 8 * LANES, LANES)
    hit = want == iota((n, LANES), 0)
    return jnp.sum(jnp.where(hit, column, 0.0), axis=0, keepdims=True)


def to_column(row, start, n):
    want = lax.rem(iota((n, LANES), 1) - start + 8 * LANES, LANES)
    hit = want == iota((n, LANES), 0)
    return jnp.sum(jnp.where(hit, row, 0.0), axis=1, keepdims=True)


def project_one(own, v, rows_ref, e):
    rows, columns = v.shape
    p = own * v
    q = p[:, :LANES]
    for k in range(1, columns // LANES):
        q = q + p[:, k * LANES : (k + 1) * LANES]
    s = q[:8]
    for k in range(1, rows // 8):
        s = s + q[8 * k : 8 * k + 8]
    rows_ref[e : e + 1, :] = jnp.sum(s, axis=0, keepdims=True)


def project(e_ref, v, rows_ref):
    for e in range(e_ref.shape[0]):
        project_one(e_ref[e], v, rows_ref, e)
    return jnp.sum(rows_ref[...], axis=1, keepdims=True)


def coarse(c_ref, gathered_ref, nev, stride):
    dofs = c_ref.shape[1]
    lane = iota((1, LANES), 1)
    total = None
    for r in range(dofs // LANES):
        low = r * LANES // nev
        high = (r * LANES + LANES - 1) // nev
        flat = gathered_ref[low * stride : low * stride + 1, :]
        for d in range(low + 1, high + 1):
            row = gathered_ref[d * stride : d * stride + 1, :]
            flat = jnp.where(lane >= d * nev - r * LANES, row, flat)
        term = c_ref[:, r * LANES : (r + 1) * LANES] * flat
        total = term if total is None else total + term
    return jnp.sum(total, axis=1, keepdims=True)


def prolong(e_ref, y, rows_ref):
    nev = e_ref.shape[0]
    rows_ref[...] = jnp.broadcast_to(y, (nev, LANES))
    reps = e_ref.shape[2] // LANES
    result = None
    for e in range(nev):
        weight = jnp.concatenate([rows_ref[e : e + 1, :]] * reps, axis=1)
        term = weight * e_ref[e]
        result = term if result is None else result + term
    return result


def total_of(v):
    return jnp.sum(jnp.sum(v, axis=0, keepdims=True), axis=1, keepdims=True)


def fill(out_ref, message):
    size = message.shape[0]
    count = out_ref.shape[0] // size
    batch = min(8, count)
    for i in range(batch):
        out_ref[i * size : (i + 1) * size, :] = message
    pattern = out_ref[: batch * size, :]
    for k in range(1, count // batch):
        out_ref[k * batch * size : (k + 1) * batch * size, :] = pattern


def group_place():
    return (lax.axis_index("zl") * lax.axis_size("xy") + lax.axis_index("xy")) * 2 + lax.axis_index(
        "core"
    )


def column_place():
    return lax.axis_index("xy") * 2 + lax.axis_index("core")


def lane_start(place, nev):
    return lax.rem(place * nev, LANES)


def opening_kernel(
    kinds_hbm, r_hbm, map_hbm, e_hbm, c_hbm,
    perm_ref, over_ref, facing_ref, out_ref, r_ref, e_ref, c_ref,
    kinds_ref, map_ref, rows_ref, block_ref, sems,
):
    nev, rows, columns = e_ref.shape
    steps = sems.shape[0] - 4
    chunk = nev // steps
    small = [
        pltpu.make_async_copy(source, target, sems.at[k])
        for k, (source, target) in enumerate(
            ((kinds_hbm, kinds_ref), (map_hbm, map_ref), (r_hbm, r_ref))
        )
    ]
    parts = [
        pltpu.make_async_copy(
            e_hbm.at[pl.ds(k * chunk, chunk)], e_ref.at[pl.ds(k * chunk, chunk)], sems.at[4 + k]
        )
        for k in range(steps)
    ]
    matrix = pltpu.make_async_copy(c_hbm, c_ref, sems.at[3])
    for copy in parts[:2] + small + parts[2:] + [matrix]:
        copy.start()
    for copy in small:
        copy.wait()
    classes = map_ref[...]
    perm = jnp.full(classes.shape, kinds_ref[0])
    for k in range(1, kinds_ref.shape[0]):
        perm = jnp.where(classes == k, kinds_ref[k], perm)
    perm_ref[...] = perm
    upper = lax.axis_index("zl") == 0
    over = jnp.where(upper, perm[:1], perm[-1:])
    within = jnp.where(upper, perm[-1:], perm[:1])
    over_ref[...] = jnp.zeros_like(over_ref)
    for k in range(columns // LANES):
        over_ref[k : k + 1, :] = over[:, k * LANES : (k + 1) * LANES]
    r = r_ref[...]
    first = lax.axis_index("core") == 0
    block = pl.multiple_of(jnp.where(first, 0, columns - LANES), LANES)
    turn = jnp.where(first, 0, 1)
    lane = iota((rows, LANES), 1)
    facing = jnp.zeros((rows, LANES), jnp.float32)
    for k in range(steps):
        parts[k].wait()
        for e in range(k * chunk, (k + 1) * chunk):
            project_one(e_ref[e], r, rows_ref, e)
            edge = pltpu.roll(e_ref[e, :, pl.ds(block, LANES)], e + turn, 1)
            facing = jnp.where(lane == e, edge, facing)
    facing_ref[...] = facing
    c = jnp.sum(rows_ref[...], axis=1, keepdims=True)
    start = lane_start(group_place(), nev)
    size = block_ref.shape[0]
    block_ref[:1, :] = (
        to_lanes(c, start)
        + to_lanes(perm[:, :1], start + nev)
        + to_lanes(perm[:, -1:], start + nev + rows)
    )
    for k in range(size - 1):
        block_ref[k + 1 : k + 2, :] = within[:, k * LANES : (k + 1) * LANES]
    fill(out_ref, block_ref[...])
    matrix.wait()


def beside_columns(got_ref, stride, nev, rows):
    place, b, b_count = group_place(), column_place(), lax.axis_size("xy") * 2
    last = got_ref.shape[0] // stride - 1
    before, after = jnp.maximum(place - 1, 0), jnp.minimum(place + 1, last)
    left = to_column(
        got_ref[pl.ds(before * stride, 1), :], lane_start(before, nev) + nev + rows, rows
    )
    right = to_column(got_ref[pl.ds(after * stride, 1), :], lane_start(after, nev) + nev, rows)
    return jnp.where(b > 0, left, 0.0), jnp.where(b < b_count - 1, right, 0.0)


def first_kernel(
    got_ref, over_ref, perm_ref, r_ref, e_ref, c_ref,
    z_ref, coef_ref, z_over_ref, z_in_ref, y_in_ref, rows_ref,
):
    nev, rows, columns = e_ref.shape
    size = columns // LANES + 1
    upper = lax.axis_index("zl") == 0
    first = lax.axis_index("core") == 0
    left, right = beside_columns(got_ref, size, nev, rows)
    across = lax.axis_size("xy") * 2
    partner = (group_place() + jnp.where(upper, across, -across)) * size
    over = jnp.concatenate([over_ref[k : k + 1, :] for k in range(size - 1)], axis=1)
    within = jnp.concatenate(
        [got_ref[pl.ds(partner + 1 + k, 1), :] for k in range(size - 1)], axis=1
    )
    halo = (jnp.where(upper, over, within), jnp.where(upper, within, over), left, right)
    perm = perm_ref[...]
    edges = edges_of(perm.shape)
    faces = []
    for edge, near, outside in zip(edges, shifts(perm), halo):
        faces.append(harmonic(perm, jnp.where(edge, outside, near)))
    diagonal = REACTION + faces[0] + faces[1] + faces[2] + faces[3]
    coef = faces + [diagonal, 1.0 / diagonal]
    for k in range(6):
        coef_ref[k] = coef[k]
    stencil = Stencil(coef)
    y = coarse(c_ref, got_ref, nev, size)
    z = stencil.smooth(r_ref[...]) + prolong(e_ref, y, rows_ref)
    z_ref[...] = z
    top, low = (faces[0] * z)[:1], (faces[1] * z)[-1:]
    z_over_ref[...] = jnp.where(upper, top, low)
    z_in_ref[...] = jnp.where(upper, low, top)
    lefts, rights = to_lanes((faces[2] * z)[:, :1], 0), to_lanes((faces[3] * z)[:, -1:], 0)
    y_in_ref[...] = jnp.where(first, rights, lefts)


def second_kernel(
    z_in_ref, y_in_ref, z_over_ref, facing_ref, z_ref, coef_ref, e_ref, q_ref, out_ref, rows_ref
):
    nev, rows, _ = e_ref.shape
    upper = lax.axis_index("zl") == 0
    first = lax.axis_index("core") == 0
    stencil = Stencil(coef_ref)
    over, within = z_over_ref[...], z_in_ref[...]
    y_in = to_column(y_in_ref[...], 0, rows)
    halo = (
        jnp.where(upper, over, within),
        jnp.where(upper, within, over),
        jnp.where(first, 0.0, y_in),
        jnp.where(first, y_in, 0.0),
    )
    z = z_ref[...]
    q = stencil.apply(z)
    for edge, outside in zip(stencil.edges, halo):
        q = q - jnp.where(edge, outside, 0.0)
    q_ref[...] = q
    left, right = (stencil.faces[2] * z)[:, :1], (stencil.faces[3] * z)[:, -1:]
    edge = jnp.where(first, left, right)
    start = lane_start(group_place(), nev)
    own = to_lanes(project(e_ref, q, rows_ref), start) + to_lanes(edge, start + nev)
    added = jnp.sum(facing_ref[...] * edge, axis=0, keepdims=True)
    step = jnp.where(first, LANES - nev, nev)
    added = pltpu.roll(added, lax.rem(start + step, LANES), 1)
    sub = iota((8, LANES), 0)
    pair = jnp.where(lax.rem(sub, 2) == 0, own, -added)
    for k in range(out_ref.shape[0] // 8):
        out_ref[8 * k : 8 * k + 8, :] = pair


def third_kernel(
    got_ref, q_ref, z_ref, r_ref, coef_ref, e_ref, c_ref,
    q_out_ref, w_ref, v_ref, out_ref, rows_ref, block_ref, group_ref,
):
    nev, rows, columns = e_ref.shape
    half = columns // LANES
    stencil = Stencil(coef_ref)
    z, r = z_ref[...], r_ref[...]
    first = lax.axis_index("core") == 0
    place, b, count = group_place(), column_place(), group_ref.shape[0]
    near = jnp.where(first, jnp.maximum(place - 1, 0), jnp.minimum(place + 1, count - 1))
    edge = to_column(got_ref[pl.ds(2 * near, 1), :], lane_start(near, nev) + nev, rows)
    left = jnp.where(first & (b > 0), edge, 0.0)
    right = jnp.where((~first) & (b < lax.axis_size("xy") * 2 - 1), edge, 0.0)
    q = q_ref[...] - jnp.where(stencil.edges[2], left, 0.0)
    q = q - jnp.where(stencil.edges[3], right, 0.0)
    q_out_ref[...] = q
    added = got_ref[pl.ds(1, count, stride=2), :]
    group_ref[...] = (
        got_ref[pl.ds(0, count, stride=2), :]
        + pltpu.roll(added, 1, 0)
        + pltpu.roll(added, count - 1, 0)
    )
    y = coarse(c_ref, group_ref, nev, 1)
    w = stencil.smooth(q) + prolong(e_ref, y, rows_ref)
    v = stencil.apply(w)
    w_ref[...] = w
    v_ref[...] = v
    low = (stencil.faces[1] * w)[-1:]
    for k in range(half):
        block_ref[k : k + 1, :] = low[:, k * LANES : (k + 1) * LANES]
        block_ref[half + k : half + k + 1, :] = w[:1, k * LANES : (k + 1) * LANES]
    last = to_lanes(w[:, :1], 0) + to_lanes((stencil.faces[3] * w)[:, -1:], rows)
    lane = iota((1, LANES), 1)
    for k, product in enumerate((r * z, z * q, r * w, q * w, w * v)):
        last = jnp.where(lane == 2 * rows + k, total_of(product), last)
    size = block_ref.shape[0]
    block_ref[size - 1 : size, :] = last
    fill(out_ref, block_ref[...])


def fourth_kernel(got_ref, v_ref, coef_ref, v_out_ref, out_ref, block_ref):
    rows, columns = v_ref.shape
    half = columns // LANES
    size = 2 * half + 1
    count = got_ref.shape[0] // size
    z_count = count // 2
    z = lax.axis_index("zh") * 2 + lax.axis_index("zl")
    core = lax.axis_index("core")
    flat = jnp.zeros((half, LANES), jnp.float32)
    for i in range(count - 2):
        at, below = i * size, (i + 2) * size
        flat = flat + got_ref[at : at + half, :] * got_ref[below + half : below + 2 * half, :]
    west = got_ref[pl.ds(2 * half, z_count, stride=2 * size), :]
    east = got_ref[pl.ds(2 * half + size, z_count, stride=2 * size), :]
    facing = jnp.where(iota((z_count, LANES), 1) < rows, pltpu.roll(west, LANES - rows, 1) * east, 0.0)
    between = total_of(flat) + total_of(facing)
    lane = iota((1, LANES), 1)
    sums = jnp.sum(west + east, axis=0, keepdims=True)
    sums = jnp.where(lane == 2 * rows + 4, sums - 2.0 * between, sums)
    pack = LANES // rows
    zr = z_count // pack
    wide = iota((zr, LANES), 1)
    lefts = jnp.zeros((zr, LANES), jnp.float32)
    rights = lefts
    for j in range(pack):
        a = got_ref[pl.ds(2 * half + 2 * size * j, zr, stride=2 * size * pack), :]
        d = got_ref[pl.ds(2 * half + size + 2 * size * j, zr, stride=2 * size * pack), :]
        a = jnp.where(wide < rows, a, 0.0)
        d = jnp.where((wide >= rows) & (wide < 2 * rows), d, 0.0)
        if j > 0:
            a = pltpu.roll(a, rows * j, 1)
        if j != 1:
            d = pltpu.roll(d, (rows * (j - 1)) % LANES, 1)
        lefts, rights = lefts + a, rights + d
    block_ref[:zr, :] = lefts
    block_ref[zr : 2 * zr, :] = rights
    block_ref[2 * zr : 2 * zr + 1, :] = sums
    fill(out_ref, block_ref[...])

    above = jnp.maximum(2 * z - 2 + core, 0) * size
    below = jnp.minimum(2 * z + 2 + core, count - 1) * size + half
    up = jnp.concatenate([got_ref[pl.ds(above + k, 1), :] for k in range(half)], axis=1)
    down = jnp.concatenate([got_ref[pl.ds(below + k, 1), :] for k in range(half)], axis=1)
    up = jnp.where(z > 0, up, 0.0)
    down = jnp.where(z < z_count - 1, down, 0.0) * coef_ref[1, rows - 1 : rows, :]
    partner = got_ref[pl.ds((2 * z + 1 - core) * size + 2 * half, 1), :]
    left, right = to_column(partner, rows, rows), to_column(partner, 0, rows)
    edges = edges_of((rows, columns))
    v = v_ref[...]
    v = v - jnp.where(edges[0], up, 0.0) - jnp.where(edges[1], down, 0.0)
    v = v - jnp.where(edges[2], jnp.where(core == 1, left, 0.0), 0.0)
    v = v - jnp.where(edges[3], jnp.where(core == 0, right, 0.0) * coef_ref[3], 0.0)
    v_out_ref[...] = v


def closing_kernel(got_ref, v_ref, z_ref, w_ref, q_ref, r_ref, coef_ref, x_ref, res_ref):
    rows, columns = v_ref.shape
    pack = LANES // rows
    zr = lax.axis_size("zh") * 2 // pack
    size = 2 * zr + 1
    count = got_ref.shape[0] // size
    z = lax.axis_index("zh") * 2 + lax.axis_index("zl")
    xy, core = lax.axis_index("xy"), lax.axis_index("core")
    sums = got_ref[2 * zr : 2 * zr + 1, :]
    flat = jnp.zeros((zr, LANES), jnp.float32)
    for i in range(1, count):
        at = i * size
        sums = sums + got_ref[at + 2 * zr : at + 2 * zr + 1, :]
        flat = flat + got_ref[at - size + zr : at - size + 2 * zr, :] * got_ref[at : at + zr, :]
    across = total_of(flat)
    lane = iota((1, LANES), 1)
    rz, zq, rw, qw, wv = (
        jnp.sum(jnp.where(lane == 2 * rows + k, sums, 0.0), axis=1, keepdims=True)
        for k in range(5)
    )
    wv = wv - 2.0 * across
    step = rz / zq
    rz_new = rz - step * ((rw + zq) - step * qw)
    grow = 1.0 + rz_new / rz
    curve = grow * grow * zq - 2.0 * grow * step * qw + step * step * wv
    step_next = rz_new / curve
    on_z = step + step_next * grow
    on_w = step_next * step

    left_of, right_of = jnp.maximum(xy - 1, 0), jnp.minimum(xy + 1, count - 1)
    row = z // pack
    position = lax.rem(z, pack) * rows
    left = to_column(got_ref[pl.ds(left_of * size + zr + row, 1), :], position, rows)
    right = to_column(got_ref[pl.ds(right_of * size + row, 1), :], position, rows)
    left = jnp.where((core == 0) & (xy > 0), left, 0.0)
    right = jnp.where((core == 1) & (xy < count - 1), right, 0.0)
    edges = edges_of((rows, columns))
    v = v_ref[...]
    v = v - jnp.where(edges[2], left, 0.0) - jnp.where(edges[3], right * coef_ref[3], 0.0)
    x_ref[...] = on_z * z_ref[...] - on_w * w_ref[...]
    res_ref[...] = r_ref[...] - on_z * q_ref[...] + on_w * v


def call(kernel, name, args, outs, scratch=(), by_hand=False):
    whole = pl.BlockSpec(memory_space=pltpu.VMEM)
    scratch = [pltpu.VMEM(x, jnp.float32) if isinstance(x, tuple) else x for x in scratch]
    return pl.pallas_call(
        kernel,
        out_shape=[jax.ShapeDtypeStruct(shape, jnp.float32) for shape in outs],
        in_specs=[pl.BlockSpec(memory_space=pl.ANY) if by_hand else whole] * len(args),
        out_specs=[whole] * len(outs),
        scratch_shapes=scratch,
        compiler_params=pltpu.CompilerParams(vmem_limit_bytes=VMEM_LIMIT),
        name=name,
    )(*args)


def exchanged(x, axes, rows):
    flat = x.reshape(x.shape[0] // rows, rows * LANES)
    return lax.all_to_all(flat, axes, 0, 0, tiled=True).reshape(x.shape)


def swap_in(x, axis):
    return lax.ppermute(x, axis, [(0, 1), (1, 0)])


def swap_over(x, axes):
    count = lax.axis_size(axes)
    pairs = [(i, i + 1) for i in range(1, count - 1, 2)]
    return lax.ppermute(x, axes, pairs + [(j, i) for i, j in pairs])


def local(right_side, class_map, class_perm, eigenvectors, coarse_inverse):
    rows, columns = right_side.shape
    nev = eigenvectors.shape[0]
    field = (rows, columns)
    group = 2 * lax.axis_size(COLS)
    z_count, chips = lax.axis_size(ROWS), lax.axis_size("xy")
    size = 2 * (columns // LANES) + 1
    size_next = 2 * (z_count * rows // LANES) + 1
    per_vector = (nev, LANES)

    size_first = columns // LANES + 1
    given = (class_perm, right_side, class_map, eigenvectors, coarse_inverse)
    perm, over, facing, message, r, vectors, matrix = call(
        opening_kernel, "opening",
        tuple(pltpu.with_memory_space_constraint(x, pltpu.HBM) for x in given),
        [field, (rows + 8, LANES), (rows, LANES), (size_first * group, LANES),
         field, eigenvectors.shape, coarse_inverse.shape],
        [pltpu.SMEM(class_perm.shape, jnp.float32), pltpu.VMEM(field, jnp.int32), per_vector,
         (size_first, LANES), pltpu.SemaphoreType.DMA((4 + PIECES,))],
        by_hand=True,
    )
    over, facing = swap_over(over, ROWS), swap_over(facing, COLS)
    got = exchanged(message, GROUP, size_first)
    z0, coef, z_over, z_in, y_in = call(
        first_kernel, "first", (got, over, perm, r, vectors, matrix),
        [field, (6,) + field, (1, columns), (1, columns), (1, LANES)], [per_vector],
    )
    z_in, y_in = swap_in(z_in, "zl"), swap_in(y_in, "core")
    z_over = swap_over(z_over, ROWS)
    q0, message = call(
        second_kernel, "second", (z_in, y_in, z_over, facing, z0, coef, vectors),
        [field, (2 * group, LANES)], [per_vector],
    )
    got = exchanged(message, GROUP, 2)
    q0, w, v, message = call(
        third_kernel, "third", (got, q0, z0, r, coef, vectors, matrix),
        [field, field, field, (2 * z_count * size, LANES)],
        [per_vector, (size, LANES), (group, LANES)],
    )
    got = exchanged(message, STACK, size)
    v, message = call(
        fourth_kernel, "fourth", (got, v, coef),
        [field, (chips * size_next, LANES)], [(size_next, LANES)],
    )
    got = exchanged(message, PLANE, size_next)
    return tuple(call(closing_kernel, "closing", (got, v, z0, w, q0, r, coef), [field, field]))


def solution(mesh):
    n_gx, n_gy = mesh.devices.shape
    fine = Mesh(mesh.devices.reshape(n_gx // 2, 2, n_gy // 2, 2), FINE)
    in_specs = (P(ROWS, COLS), P(ROWS, COLS), P(), P(None, ROWS, COLS), P(FINE, None))
    out_specs = (P(ROWS, COLS), P(ROWS, COLS))
    return jax.shard_map(local, mesh=fine, in_specs=in_specs, out_specs=out_specs, check_vma=False)
```

```python
import jax
import jax.numpy as jnp
from jax import lax
from jax.experimental import pallas as pl
from jax.experimental.pallas import tpu as pltpu
from jax.sharding import Mesh, PartitionSpec as P

CHEB = 4
REACTION = 0.05
EIGEN_TOP = 2.0
EIGEN_LOW = 0.1
LANES = 128

ROWS = ("zh", "zl")
COLS = ("xy", "core")
GROUP = ("zl", "xy", "core")
STACK = ("zh", "zl", "core")
PLANE = ("xy",)
FINE = ("zh", "zl", "xy", "core")
VMEM_LIMIT = 24 * 1024 * 1024
PIECES = 5


def iota(shape, dim):
    return lax.broadcasted_iota(jnp.int32, shape, dim)


def harmonic(centre, beside):
    return jnp.where(beside > 0.0, 2.0 * centre * beside / (centre + beside), centre)


def shifts(v):
    rows, columns = v.shape
    return (
        pltpu.roll(v, 1, 0),
        pltpu.roll(v, rows - 1, 0),
        pltpu.roll(v, 1, 1),
        pltpu.roll(v, columns - 1, 1),
    )


def edges_of(shape):
    row, column = iota(shape, 0), iota(shape, 1)
    return (row == 0, row == shape[0] - 1, column == 0, column == shape[1] - 1)


class Stencil:
    def __init__(self, coef):
        self.faces = tuple(coef[k] for k in range(4))
        self.diagonal, self.inverse = coef[4], coef[5]
        self.edges = edges_of(self.diagonal.shape)
        self.inner = tuple(
            jnp.where(edge, 0.0, face) for edge, face in zip(self.edges, self.faces)
        )

    def apply(self, v):
        result = self.diagonal * v
        for weight, near in zip(self.inner, shifts(v)):
            result = result - weight * near
        return result

    def smooth(self, source):
        centre = 0.5 * (EIGEN_TOP + EIGEN_LOW)
        radius = 0.5 * (EIGEN_TOP - EIGEN_LOW)
        ratio_start = centre / radius
        factor = 1.0 / ratio_start
        update = source * self.inverse * (1.0 / centre)
        smoothed = update
        for _ in range(1, CHEB):
            defect = source - self.apply(smoothed)
            factor_next = 1.0 / (2.0 * ratio_start - factor)
            update = factor_next * factor * update + (2.0 * factor_next / radius) * (
                defect * self.inverse
            )
            smoothed = smoothed + update
            factor = factor_next
        return smoothed


def to_lanes(column, start):
    n = column.shape[0]
    want = lax.rem(iota((n, LANES), 1) - start + 8 * LANES, LANES)
    hit = want == iota((n, LANES), 0)
    return jnp.sum(jnp.where(hit, column, 0.0), axis=0, keepdims=True)


def to_column(row, start, n):
    want = lax.rem(iota((n, LANES), 1) - start + 8 * LANES, LANES)
    hit = want == iota((n, LANES), 0)
    return jnp.sum(jnp.where(hit, row, 0.0), axis=1, keepdims=True)


def project_one(own, v, rows_ref, e):
    rows, columns = v.shape
    p = own * v
    q = p[:, :LANES]
    for k in range(1, columns // LANES):
        q = q + p[:, k * LANES : (k + 1) * LANES]
    s = q[:8]
    for k in range(1, rows // 8):
        s = s + q[8 * k : 8 * k + 8]
    rows_ref[e : e + 1, :] = jnp.sum(s, axis=0, keepdims=True)


def project(e_ref, v, rows_ref):
    for e in range(e_ref.shape[0]):
        project_one(e_ref[e], v, rows_ref, e)
    return jnp.sum(rows_ref[...], axis=1, keepdims=True)


def coarse(c_ref, gathered_ref, nev, stride):
    dofs = c_ref.shape[1]
    lane = iota((1, LANES), 1)
    total = None
    for r in range(dofs // LANES):
        low = r * LANES // nev
        high = (r * LANES + LANES - 1) // nev
        flat = gathered_ref[low * stride : low * stride + 1, :]
        for d in range(low + 1, high + 1):
            row = gathered_ref[d * stride : d * stride + 1, :]
            flat = jnp.where(lane >= d * nev - r * LANES, row, flat)
        term = c_ref[:, r * LANES : (r + 1) * LANES] * flat
        total = term if total is None else total + term
    return jnp.sum(total, axis=1, keepdims=True)


def prolong(e_ref, y, rows_ref):
    nev = e_ref.shape[0]
    rows_ref[...] = jnp.broadcast_to(y, (nev, LANES))
    reps = e_ref.shape[2] // LANES
    result = None
    for e in range(nev):
        weight = jnp.concatenate([rows_ref[e : e + 1, :]] * reps, axis=1)
        term = weight * e_ref[e]
        result = term if result is None else result + term
    return result


def total_of(v):
    return jnp.sum(jnp.sum(v, axis=0, keepdims=True), axis=1, keepdims=True)


def fill(out_ref, message):
    size = message.shape[0]
    count = out_ref.shape[0] // size
    batch = min(8, count)
    for i in range(batch):
        out_ref[i * size : (i + 1) * size, :] = message
    pattern = out_ref[: batch * size, :]
    for k in range(1, count // batch):
        out_ref[k * batch * size : (k + 1) * batch * size, :] = pattern


def group_place():
    return (lax.axis_index("zl") * lax.axis_size("xy") + lax.axis_index("xy")) * 2 + lax.axis_index(
        "core"
    )


def column_place():
    return lax.axis_index("xy") * 2 + lax.axis_index("core")


def lane_start(place, nev):
    return lax.rem(place * nev, LANES)


def opening_kernel(
    kinds_hbm, r_hbm, map_hbm, e_hbm, c_hbm,
    perm_ref, over_ref, facing_ref, out_ref, r_ref, e_ref, c_ref,
    kinds_ref, map_ref, rows_ref, block_ref, sems,
):
    nev, rows, columns = e_ref.shape
    steps = sems.shape[0] - 4
    chunk = nev // steps
    small = [
        pltpu.make_async_copy(source, target, sems.at[k])
        for k, (source, target) in enumerate(
            ((kinds_hbm, kinds_ref), (map_hbm, map_ref), (r_hbm, r_ref))
        )
    ]
    parts = [
        pltpu.make_async_copy(
            e_hbm.at[pl.ds(k * chunk, chunk)], e_ref.at[pl.ds(k * chunk, chunk)], sems.at[4 + k]
        )
        for k in range(steps)
    ]
    matrix = pltpu.make_async_copy(c_hbm, c_ref, sems.at[3])
    for copy in parts[:2] + small + parts[2:] + [matrix]:
        copy.start()
    for copy in small:
        copy.wait()
    classes = map_ref[...]
    perm = jnp.full(classes.shape, kinds_ref[0])
    for k in range(1, kinds_ref.shape[0]):
        perm = jnp.where(classes == k, kinds_ref[k], perm)
    perm_ref[...] = perm
    upper = lax.axis_index("zl") == 0
    over = jnp.where(upper, perm[:1], perm[-1:])
    within = jnp.where(upper, perm[-1:], perm[:1])
    over_ref[...] = jnp.zeros_like(over_ref)
    for k in range(columns // LANES):
        over_ref[k : k + 1, :] = over[:, k * LANES : (k + 1) * LANES]
    r = r_ref[...]
    first = lax.axis_index("core") == 0
    block = pl.multiple_of(jnp.where(first, 0, columns - LANES), LANES)
    turn = jnp.where(first, 0, 1)
    lane = iota((rows, LANES), 1)
    facing = jnp.zeros((rows, LANES), jnp.float32)
    for k in range(steps):
        parts[k].wait()
        for e in range(k * chunk, (k + 1) * chunk):
            project_one(e_ref[e], r, rows_ref, e)
            edge = pltpu.roll(e_ref[e, :, pl.ds(block, LANES)], e + turn, 1)
            facing = jnp.where(lane == e, edge, facing)
    facing_ref[...] = facing
    c = jnp.sum(rows_ref[...], axis=1, keepdims=True)
    start = lane_start(group_place(), nev)
    size = block_ref.shape[0]
    block_ref[:1, :] = (
        to_lanes(c, start)
        + to_lanes(perm[:, :1], start + nev)
        + to_lanes(perm[:, -1:], start + nev + rows)
    )
    for k in range(size - 1):
        block_ref[k + 1 : k + 2, :] = within[:, k * LANES : (k + 1) * LANES]
    fill(out_ref, block_ref[...])
    matrix.wait()


def beside_columns(got_ref, stride, nev, rows):
    place, b, b_count = group_place(), column_place(), lax.axis_size("xy") * 2
    last = got_ref.shape[0] // stride - 1
    before, after = jnp.maximum(place - 1, 0), jnp.minimum(place + 1, last)
    left = to_column(
        got_ref[pl.ds(before * stride, 1), :], lane_start(before, nev) + nev + rows, rows
    )
    right = to_column(got_ref[pl.ds(after * stride, 1), :], lane_start(after, nev) + nev, rows)
    return jnp.where(b > 0, left, 0.0), jnp.where(b < b_count - 1, right, 0.0)


def first_kernel(
    got_ref, over_ref, perm_ref, r_ref, e_ref, c_ref,
    z_ref, coef_ref, z_over_ref, z_in_ref, y_in_ref, rows_ref,
):
    nev, rows, columns = e_ref.shape
    size = columns // LANES + 1
    upper = lax.axis_index("zl") == 0
    first = lax.axis_index("core") == 0
    left, right = beside_columns(got_ref, size, nev, rows)
    across = lax.axis_size("xy") * 2
    partner = (group_place() + jnp.where(upper, across, -across)) * size
    over = jnp.concatenate([over_ref[k : k + 1, :] for k in range(size - 1)], axis=1)
    within = jnp.concatenate(
        [got_ref[pl.ds(partner + 1 + k, 1), :] for k in range(size - 1)], axis=1
    )
    halo = (jnp.where(upper, over, within), jnp.where(upper, within, over), left, right)
    perm = perm_ref[...]
    edges = edges_of(perm.shape)
    faces = []
    for edge, near, outside in zip(edges, shifts(perm), halo):
        faces.append(harmonic(perm, jnp.where(edge, outside, near)))
    diagonal = REACTION + faces[0] + faces[1] + faces[2] + faces[3]
    coef = faces + [diagonal, 1.0 / diagonal]
    for k in range(6):
        coef_ref[k] = coef[k]
    stencil = Stencil(coef)
    y = coarse(c_ref, got_ref, nev, size)
    z = stencil.smooth(r_ref[...]) + prolong(e_ref, y, rows_ref)
    z_ref[...] = z
    top, low = (faces[0] * z)[:1], (faces[1] * z)[-1:]
    z_over_ref[...] = jnp.where(upper, top, low)
    z_in_ref[...] = jnp.where(upper, low, top)
    lefts, rights = to_lanes((faces[2] * z)[:, :1], 0), to_lanes((faces[3] * z)[:, -1:], 0)
    y_in_ref[...] = jnp.broadcast_to(jnp.where(first, rights, lefts), y_in_ref.shape)


def second_kernel(
    z_in_ref, y_in_ref, z_over_ref, facing_ref, z_ref, coef_ref, e_ref, q_ref, out_ref, rows_ref
):
    nev, rows, _ = e_ref.shape
    upper = lax.axis_index("zl") == 0
    first = lax.axis_index("core") == 0
    stencil = Stencil(coef_ref)
    over, within = z_over_ref[...], z_in_ref[...]
    y_in = to_column(y_in_ref[:1, :], 0, rows)
    halo = (
        jnp.where(upper, over, within),
        jnp.where(upper, within, over),
        jnp.where(first, 0.0, y_in),
        jnp.where(first, y_in, 0.0),
    )
    z = z_ref[...]
    q = stencil.apply(z)
    for edge, outside in zip(stencil.edges, halo):
        q = q - jnp.where(edge, outside, 0.0)
    q_ref[...] = q
    left, right = (stencil.faces[2] * z)[:, :1], (stencil.faces[3] * z)[:, -1:]
    edge = jnp.where(first, left, right)
    start = lane_start(group_place(), nev)
    own = to_lanes(project(e_ref, q, rows_ref), start) + to_lanes(edge, start + nev)
    added = jnp.sum(facing_ref[...] * edge, axis=0, keepdims=True)
    step = jnp.where(first, LANES - nev, nev)
    added = pltpu.roll(added, lax.rem(start + step, LANES), 1)
    sub = iota((8, LANES), 0)
    pair = jnp.where(lax.rem(sub, 2) == 0, own, -added)
    for k in range(out_ref.shape[0] // 8):
        out_ref[8 * k : 8 * k + 8, :] = pair


def third_kernel(
    got_ref, q_ref, z_ref, r_ref, coef_ref, e_ref, c_ref,
    q_out_ref, w_ref, v_ref, out_ref, rows_ref, block_ref, group_ref,
):
    nev, rows, columns = e_ref.shape
    half = columns // LANES
    stencil = Stencil(coef_ref)
    z, r = z_ref[...], r_ref[...]
    first = lax.axis_index("core") == 0
    place, b, count = group_place(), column_place(), group_ref.shape[0]
    near = jnp.where(first, jnp.maximum(place - 1, 0), jnp.minimum(place + 1, count - 1))
    edge = to_column(got_ref[pl.ds(2 * near, 1), :], lane_start(near, nev) + nev, rows)
    left = jnp.where(first & (b > 0), edge, 0.0)
    right = jnp.where((~first) & (b < lax.axis_size("xy") * 2 - 1), edge, 0.0)
    q = q_ref[...] - jnp.where(stencil.edges[2], left, 0.0)
    q = q - jnp.where(stencil.edges[3], right, 0.0)
    q_out_ref[...] = q
    added = got_ref[pl.ds(1, count, stride=2), :]
    group_ref[...] = (
        got_ref[pl.ds(0, count, stride=2), :]
        + pltpu.roll(added, 1, 0)
        + pltpu.roll(added, count - 1, 0)
    )
    y = coarse(c_ref, group_ref, nev, 1)
    w = stencil.smooth(q) + prolong(e_ref, y, rows_ref)
    v = stencil.apply(w)
    w_ref[...] = w
    v_ref[...] = v
    low = (stencil.faces[1] * w)[-1:]
    for k in range(half):
        block_ref[k : k + 1, :] = low[:, k * LANES : (k + 1) * LANES]
        block_ref[half + k : half + k + 1, :] = w[:1, k * LANES : (k + 1) * LANES]
    last = to_lanes(w[:, :1], 0) + to_lanes((stencil.faces[3] * w)[:, -1:], rows)
    lane = iota((1, LANES), 1)
    for k, product in enumerate((r * z, z * q, r * w, q * w, w * v)):
        last = jnp.where(lane == 2 * rows + k, total_of(product), last)
    size = block_ref.shape[0]
    block_ref[size - 1 : size, :] = last
    fill(out_ref, block_ref[...])


def fourth_kernel(got_ref, v_ref, coef_ref, v_out_ref, out_ref, block_ref):
    rows, columns = v_ref.shape
    half = columns // LANES
    size = 2 * half + 1
    count = got_ref.shape[0] // size
    z_count = count // 2
    z = lax.axis_index("zh") * 2 + lax.axis_index("zl")
    core = lax.axis_index("core")
    flat = jnp.zeros((half, LANES), jnp.float32)
    for i in range(count - 2):
        at, below = i * size, (i + 2) * size
        flat = flat + got_ref[at : at + half, :] * got_ref[below + half : below + 2 * half, :]
    west = got_ref[pl.ds(2 * half, z_count, stride=2 * size), :]
    east = got_ref[pl.ds(2 * half + size, z_count, stride=2 * size), :]
    facing = jnp.where(iota((z_count, LANES), 1) < rows, pltpu.roll(west, LANES - rows, 1) * east, 0.0)
    between = total_of(flat) + total_of(facing)
    lane = iota((1, LANES), 1)
    sums = jnp.sum(west + east, axis=0, keepdims=True)
    sums = jnp.where(lane == 2 * rows + 4, sums - 2.0 * between, sums)
    pack = LANES // rows
    zr = z_count // pack
    wide = iota((zr, LANES), 1)
    lefts = jnp.zeros((zr, LANES), jnp.float32)
    rights = lefts
    for j in range(pack):
        a = got_ref[pl.ds(2 * half + 2 * size * j, zr, stride=2 * size * pack), :]
        d = got_ref[pl.ds(2 * half + size + 2 * size * j, zr, stride=2 * size * pack), :]
        a = jnp.where(wide < rows, a, 0.0)
        d = jnp.where((wide >= rows) & (wide < 2 * rows), d, 0.0)
        if j > 0:
            a = pltpu.roll(a, rows * j, 1)
        if j != 1:
            d = pltpu.roll(d, (rows * (j - 1)) % LANES, 1)
        lefts, rights = lefts + a, rights + d
    block_ref[:zr, :] = lefts
    block_ref[zr : 2 * zr, :] = rights
    block_ref[2 * zr : 2 * zr + 1, :] = sums
    fill(out_ref, block_ref[...])

    above = jnp.maximum(2 * z - 2 + core, 0) * size
    below = jnp.minimum(2 * z + 2 + core, count - 1) * size + half
    up = jnp.concatenate([got_ref[pl.ds(above + k, 1), :] for k in range(half)], axis=1)
    down = jnp.concatenate([got_ref[pl.ds(below + k, 1), :] for k in range(half)], axis=1)
    up = jnp.where(z > 0, up, 0.0)
    down = jnp.where(z < z_count - 1, down, 0.0) * coef_ref[1, rows - 1 : rows, :]
    partner = got_ref[pl.ds((2 * z + 1 - core) * size + 2 * half, 1), :]
    left, right = to_column(partner, rows, rows), to_column(partner, 0, rows)
    edges = edges_of((rows, columns))
    v = v_ref[...]
    v = v - jnp.where(edges[0], up, 0.0) - jnp.where(edges[1], down, 0.0)
    v = v - jnp.where(edges[2], jnp.where(core == 1, left, 0.0), 0.0)
    v = v - jnp.where(edges[3], jnp.where(core == 0, right, 0.0) * coef_ref[3], 0.0)
    v_out_ref[...] = v


def closing_kernel(got_ref, v_ref, z_ref, w_ref, q_ref, r_ref, coef_ref, x_ref, res_ref):
    rows, columns = v_ref.shape
    pack = LANES // rows
    zr = lax.axis_size("zh") * 2 // pack
    size = 2 * zr + 1
    count = got_ref.shape[0] // size
    z = lax.axis_index("zh") * 2 + lax.axis_index("zl")
    xy, core = lax.axis_index("xy"), lax.axis_index("core")
    sums = got_ref[2 * zr : 2 * zr + 1, :]
    flat = jnp.zeros((zr, LANES), jnp.float32)
    for i in range(1, count):
        at = i * size
        sums = sums + got_ref[at + 2 * zr : at + 2 * zr + 1, :]
        flat = flat + got_ref[at - size + zr : at - size + 2 * zr, :] * got_ref[at : at + zr, :]
    across = total_of(flat)
    lane = iota((1, LANES), 1)
    rz, zq, rw, qw, wv = (
        jnp.sum(jnp.where(lane == 2 * rows + k, sums, 0.0), axis=1, keepdims=True)
        for k in range(5)
    )
    wv = wv - 2.0 * across
    step = rz / zq
    rz_new = rz - step * ((rw + zq) - step * qw)
    grow = 1.0 + rz_new / rz
    curve = grow * grow * zq - 2.0 * grow * step * qw + step * step * wv
    step_next = rz_new / curve
    on_z = step + step_next * grow
    on_w = step_next * step

    left_of, right_of = jnp.maximum(xy - 1, 0), jnp.minimum(xy + 1, count - 1)
    row = z // pack
    position = lax.rem(z, pack) * rows
    left = to_column(got_ref[pl.ds(left_of * size + zr + row, 1), :], position, rows)
    right = to_column(got_ref[pl.ds(right_of * size + row, 1), :], position, rows)
    left = jnp.where((core == 0) & (xy > 0), left, 0.0)
    right = jnp.where((core == 1) & (xy < count - 1), right, 0.0)
    edges = edges_of((rows, columns))
    v = v_ref[...]
    v = v - jnp.where(edges[2], left, 0.0) - jnp.where(edges[3], right * coef_ref[3], 0.0)
    x_ref[...] = on_z * z_ref[...] - on_w * w_ref[...]
    res_ref[...] = r_ref[...] - on_z * q_ref[...] + on_w * v


def call(kernel, name, args, outs, scratch=(), by_hand=False):
    whole = pl.BlockSpec(memory_space=pltpu.VMEM)
    scratch = [pltpu.VMEM(x, jnp.float32) if isinstance(x, tuple) else x for x in scratch]
    return pl.pallas_call(
        kernel,
        out_shape=[jax.ShapeDtypeStruct(shape, jnp.float32) for shape in outs],
        in_specs=[pl.BlockSpec(memory_space=pl.ANY) if by_hand else whole] * len(args),
        out_specs=[whole] * len(outs),
        scratch_shapes=scratch,
        compiler_params=pltpu.CompilerParams(vmem_limit_bytes=VMEM_LIMIT),
        name=name,
    )(*args)


def exchanged(x, axes, rows):
    flat = x.reshape(x.shape[0] // rows, rows * LANES)
    return lax.all_to_all(flat, axes, 0, 0, tiled=True).reshape(x.shape)


def swap_in(x, axis):
    return lax.ppermute(x, axis, [(0, 1), (1, 0)])


def swap_over(x, axes):
    count = lax.axis_size(axes)
    pairs = [(i, i + 1) for i in range(1, count - 1, 2)]
    return lax.ppermute(x, axes, pairs + [(j, i) for i, j in pairs])


def local(right_side, class_map, class_perm, eigenvectors, coarse_inverse):
    rows, columns = right_side.shape
    nev = eigenvectors.shape[0]
    field = (rows, columns)
    group = 2 * lax.axis_size(COLS)
    z_count, chips = lax.axis_size(ROWS), lax.axis_size("xy")
    size = 2 * (columns // LANES) + 1
    size_next = 2 * (z_count * rows // LANES) + 1
    per_vector = (nev, LANES)

    size_first = columns // LANES + 1
    given = (class_perm, right_side, class_map, eigenvectors, coarse_inverse)
    perm, over, facing, message, r, vectors, matrix = call(
        opening_kernel, "opening",
        tuple(pltpu.with_memory_space_constraint(x, pltpu.HBM) for x in given),
        [field, (rows + 8, LANES), (rows, LANES), (size_first * group, LANES),
         field, eigenvectors.shape, coarse_inverse.shape],
        [pltpu.SMEM(class_perm.shape, jnp.float32), pltpu.VMEM(field, jnp.int32), per_vector,
         (size_first, LANES), pltpu.SemaphoreType.DMA((4 + PIECES,))],
        by_hand=True,
    )
    over, facing = swap_over(over, ROWS), swap_over(facing, COLS)
    got = exchanged(message, GROUP, size_first)
    z0, coef, z_over, z_in, y_in = call(
        first_kernel, "first", (got, over, perm, r, vectors, matrix),
        [field, (6,) + field, (1, columns), (1, columns), (8, LANES)], [per_vector],
    )
    z_in, y_in = swap_in(z_in, "zl"), swap_in(y_in, "core")
    z_over = swap_over(z_over, ROWS)
    q0, message = call(
        second_kernel, "second", (z_in, y_in, z_over, facing, z0, coef, vectors),
        [field, (2 * group, LANES)], [per_vector],
    )
    got = exchanged(message, GROUP, 2)
    q0, w, v, message = call(
        third_kernel, "third", (got, q0, z0, r, coef, vectors, matrix),
        [field, field, field, (2 * z_count * size, LANES)],
        [per_vector, (size, LANES), (group, LANES)],
    )
    got = exchanged(message, STACK, size)
    v, message = call(
        fourth_kernel, "fourth", (got, v, coef),
        [field, (chips * size_next, LANES)], [(size_next, LANES)],
    )
    got = exchanged(message, PLANE, size_next)
    return tuple(call(closing_kernel, "closing", (got, v, z0, w, q0, r, coef), [field, field]))


def solution(mesh):
    n_gx, n_gy = mesh.devices.shape
    fine = Mesh(mesh.devices.reshape(n_gx // 2, 2, n_gy // 2, 2), FINE)
    in_specs = (P(ROWS, COLS), P(ROWS, COLS), P(), P(None, ROWS, COLS), P(FINE, None))
    out_specs = (P(ROWS, COLS), P(ROWS, COLS))
    return jax.shard_map(local, mesh=fine, in_specs=in_specs, out_specs=out_specs, check_vma=False)
```

```python
import jax
import jax.numpy as jnp
from jax import lax
from jax.experimental import pallas as pl
from jax.experimental.pallas import tpu as pltpu
from jax.sharding import Mesh, PartitionSpec as P

CHEB = 4
REACTION = 0.05
EIGEN_TOP = 2.0
EIGEN_LOW = 0.1
LANES = 128

ROWS = ("zh", "zl")
COLS = ("xy", "core")
GROUP = ("zl", "xy", "core")
STACK = ("zh", "zl", "core")
PLANE = ("xy",)
FINE = ("zh", "zl", "xy", "core")
VMEM_LIMIT = 24 * 1024 * 1024
PIECES = 5


def iota(shape, dim):
    return lax.broadcasted_iota(jnp.int32, shape, dim)


def harmonic(centre, beside):
    return jnp.where(beside > 0.0, 2.0 * centre * beside / (centre + beside), centre)


def shifts(v):
    rows, columns = v.shape
    return (
        pltpu.roll(v, 1, 0),
        pltpu.roll(v, rows - 1, 0),
        pltpu.roll(v, 1, 1),
        pltpu.roll(v, columns - 1, 1),
    )


def edges_of(shape):
    row, column = iota(shape, 0), iota(shape, 1)
    return (row == 0, row == shape[0] - 1, column == 0, column == shape[1] - 1)


class Stencil:
    def __init__(self, coef):
        self.faces = tuple(coef[k] for k in range(4))
        self.diagonal, self.inverse = coef[4], coef[5]
        self.edges = edges_of(self.diagonal.shape)
        self.inner = tuple(
            jnp.where(edge, 0.0, face) for edge, face in zip(self.edges, self.faces)
        )

    def apply(self, v):
        result = self.diagonal * v
        for weight, near in zip(self.inner, shifts(v)):
            result = result - weight * near
        return result

    def smooth(self, source):
        centre = 0.5 * (EIGEN_TOP + EIGEN_LOW)
        radius = 0.5 * (EIGEN_TOP - EIGEN_LOW)
        ratio_start = centre / radius
        factor = 1.0 / ratio_start
        update = source * self.inverse * (1.0 / centre)
        smoothed = update
        for _ in range(1, CHEB):
            defect = source - self.apply(smoothed)
            factor_next = 1.0 / (2.0 * ratio_start - factor)
            update = factor_next * factor * update + (2.0 * factor_next / radius) * (
                defect * self.inverse
            )
            smoothed = smoothed + update
            factor = factor_next
        return smoothed


def to_lanes(column, start):
    n = column.shape[0]
    want = lax.rem(iota((n, LANES), 1) - start + 8 * LANES, LANES)
    hit = want == iota((n, LANES), 0)
    return jnp.sum(jnp.where(hit, column, 0.0), axis=0, keepdims=True)


def to_column(row, start, n):
    want = lax.rem(iota((n, LANES), 1) - start + 8 * LANES, LANES)
    hit = want == iota((n, LANES), 0)
    return jnp.sum(jnp.where(hit, row, 0.0), axis=1, keepdims=True)


def project_one(own, v, rows_ref, e):
    rows, columns = v.shape
    p = own * v
    q = p[:, :LANES]
    for k in range(1, columns // LANES):
        q = q + p[:, k * LANES : (k + 1) * LANES]
    s = q[:8]
    for k in range(1, rows // 8):
        s = s + q[8 * k : 8 * k + 8]
    rows_ref[e : e + 1, :] = jnp.sum(s, axis=0, keepdims=True)


def project(e_ref, v, rows_ref):
    for e in range(e_ref.shape[0]):
        project_one(e_ref[e], v, rows_ref, e)
    return jnp.sum(rows_ref[...], axis=1, keepdims=True)


def coarse(c_ref, gathered_ref, nev, stride):
    dofs = c_ref.shape[1]
    lane = iota((1, LANES), 1)
    total = None
    for r in range(dofs // LANES):
        low = r * LANES // nev
        high = (r * LANES + LANES - 1) // nev
        flat = gathered_ref[low * stride : low * stride + 1, :]
        for d in range(low + 1, high + 1):
            row = gathered_ref[d * stride : d * stride + 1, :]
            flat = jnp.where(lane >= d * nev - r * LANES, row, flat)
        term = c_ref[:, r * LANES : (r + 1) * LANES] * flat
        total = term if total is None else total + term
    return jnp.sum(total, axis=1, keepdims=True)


def prolong(e_ref, y, rows_ref):
    nev = e_ref.shape[0]
    rows_ref[...] = jnp.broadcast_to(y, (nev, LANES))
    reps = e_ref.shape[2] // LANES
    result = None
    for e in range(nev):
        weight = jnp.concatenate([rows_ref[e : e + 1, :]] * reps, axis=1)
        term = weight * e_ref[e]
        result = term if result is None else result + term
    return result


def total_of(v):
    return jnp.sum(jnp.sum(v, axis=0, keepdims=True), axis=1, keepdims=True)


def fill(out_ref, message):
    size = message.shape[0]
    count = out_ref.shape[0] // size
    batch = min(8, count)
    for i in range(batch):
        out_ref[i * size : (i + 1) * size, :] = message
    pattern = out_ref[: batch * size, :]
    for k in range(1, count // batch):
        out_ref[k * batch * size : (k + 1) * batch * size, :] = pattern


def group_place():
    return (lax.axis_index("zl") * lax.axis_size("xy") + lax.axis_index("xy")) * 2 + lax.axis_index(
        "core"
    )


def column_place():
    return lax.axis_index("xy") * 2 + lax.axis_index("core")


def lane_start(place, nev):
    return lax.rem(place * nev, LANES)


def opening_kernel(
    kinds_hbm, r_hbm, map_hbm, e_hbm, c_hbm,
    perm_ref, over_ref, facing_ref, inside_ref, out_ref, r_ref, e_ref, c_ref,
    kinds_ref, map_ref, rows_ref, block_ref, sems,
):
    nev, rows, columns = e_ref.shape
    steps = sems.shape[0] - 4
    chunk = nev // steps
    small = [
        pltpu.make_async_copy(source, target, sems.at[k])
        for k, (source, target) in enumerate(
            ((kinds_hbm, kinds_ref), (map_hbm, map_ref), (r_hbm, r_ref))
        )
    ]
    parts = [
        pltpu.make_async_copy(
            e_hbm.at[pl.ds(k * chunk, chunk)], e_ref.at[pl.ds(k * chunk, chunk)], sems.at[4 + k]
        )
        for k in range(steps)
    ]
    matrix = pltpu.make_async_copy(c_hbm, c_ref, sems.at[3])
    for copy in parts[:2] + small + parts[2:] + [matrix]:
        copy.start()
    for copy in small:
        copy.wait()
    classes = map_ref[...]
    perm = jnp.full(classes.shape, kinds_ref[0])
    for k in range(1, kinds_ref.shape[0]):
        perm = jnp.where(classes == k, kinds_ref[k], perm)
    perm_ref[...] = perm
    upper = lax.axis_index("zl") == 0
    over = jnp.where(upper, perm[:1], perm[-1:])
    within = jnp.where(upper, perm[-1:], perm[:1])
    over_ref[...] = jnp.zeros_like(over_ref)
    for k in range(columns // LANES):
        over_ref[k : k + 1, :] = over[:, k * LANES : (k + 1) * LANES]
    r = r_ref[...]
    first = lax.axis_index("core") == 0
    block = pl.multiple_of(jnp.where(first, 0, columns - LANES), LANES)
    other = pl.multiple_of(jnp.where(first, columns - LANES, 0), LANES)
    turn = jnp.where(first, 0, 1)
    lane = iota((rows, LANES), 1)
    facing = jnp.zeros((rows, LANES), jnp.float32)
    inside = facing
    for k in range(steps):
        parts[k].wait()
        for e in range(k * chunk, (k + 1) * chunk):
            project_one(e_ref[e], r, rows_ref, e)
            edge = pltpu.roll(e_ref[e, :, pl.ds(block, LANES)], e + turn, 1)
            facing = jnp.where(lane == e, edge, facing)
            edge = pltpu.roll(e_ref[e, :, pl.ds(other, LANES)], e + 1 - turn, 1)
            inside = jnp.where(lane == e, edge, inside)
    facing_ref[...] = facing
    inside_ref[...] = inside
    c = jnp.sum(rows_ref[...], axis=1, keepdims=True)
    start = lane_start(group_place(), nev)
    size = block_ref.shape[0]
    block_ref[:1, :] = (
        to_lanes(c, start)
        + to_lanes(perm[:, :1], start + nev)
        + to_lanes(perm[:, -1:], start + nev + rows)
    )
    for k in range(size - 1):
        block_ref[k + 1 : k + 2, :] = within[:, k * LANES : (k + 1) * LANES]
    fill(out_ref, block_ref[...])
    matrix.wait()


def beside_columns(got_ref, stride, nev, rows):
    place, b, b_count = group_place(), column_place(), lax.axis_size("xy") * 2
    last = got_ref.shape[0] // stride - 1
    before, after = jnp.maximum(place - 1, 0), jnp.minimum(place + 1, last)
    left = to_column(
        got_ref[pl.ds(before * stride, 1), :], lane_start(before, nev) + nev + rows, rows
    )
    right = to_column(got_ref[pl.ds(after * stride, 1), :], lane_start(after, nev) + nev, rows)
    return jnp.where(b > 0, left, 0.0), jnp.where(b < b_count - 1, right, 0.0)


def first_kernel(
    got_ref, over_ref, perm_ref, r_ref, e_ref, c_ref,
    z_ref, coef_ref, z_over_ref, z_in_ref, rows_ref,
):
    nev, rows, columns = e_ref.shape
    size = columns // LANES + 1
    upper = lax.axis_index("zl") == 0
    left, right = beside_columns(got_ref, size, nev, rows)
    across = lax.axis_size("xy") * 2
    partner = (group_place() + jnp.where(upper, across, -across)) * size
    over = jnp.concatenate([over_ref[k : k + 1, :] for k in range(size - 1)], axis=1)
    within = jnp.concatenate(
        [got_ref[pl.ds(partner + 1 + k, 1), :] for k in range(size - 1)], axis=1
    )
    halo = (jnp.where(upper, over, within), jnp.where(upper, within, over), left, right)
    perm = perm_ref[...]
    edges = edges_of(perm.shape)
    faces = []
    for edge, near, outside in zip(edges, shifts(perm), halo):
        faces.append(harmonic(perm, jnp.where(edge, outside, near)))
    diagonal = REACTION + faces[0] + faces[1] + faces[2] + faces[3]
    coef = faces + [diagonal, 1.0 / diagonal]
    for k in range(6):
        coef_ref[k] = coef[k]
    stencil = Stencil(coef)
    y = coarse(c_ref, got_ref, nev, size)
    z = stencil.smooth(r_ref[...]) + prolong(e_ref, y, rows_ref)
    z_ref[...] = z
    top, low = (faces[0] * z)[:1], (faces[1] * z)[-1:]
    z_over_ref[...] = jnp.where(upper, top, low)
    z_in_ref[...] = jnp.where(upper, low, top)


def second_kernel(
    z_over_ref, z_in_ref, facing_ref, inside_ref, z_ref, coef_ref, e_ref, q_ref, out_ref, rows_ref
):
    nev, rows, _ = e_ref.shape
    upper = lax.axis_index("zl") == 0
    first = lax.axis_index("core") == 0
    stencil = Stencil(coef_ref)
    over, within = z_over_ref[...], z_in_ref[...]
    z = z_ref[...]
    q = stencil.apply(z)
    q = q - jnp.where(stencil.edges[0], jnp.where(upper, over, within), 0.0)
    q = q - jnp.where(stencil.edges[1], jnp.where(upper, within, over), 0.0)
    q_ref[...] = q
    left, right = (stencil.faces[2] * z)[:, :1], (stencil.faces[3] * z)[:, -1:]
    start = lane_start(group_place(), nev)
    own = to_lanes(project(e_ref, q, rows_ref), start)
    own = own + to_lanes(left, start + nev) + to_lanes(right, start + nev + rows)
    facing, inside = facing_ref[...], inside_ref[...]
    to_left = jnp.sum(jnp.where(first, facing, inside) * left, axis=0, keepdims=True)
    to_right = jnp.sum(jnp.where(first, inside, facing) * right, axis=0, keepdims=True)
    added = pltpu.roll(to_left, lax.rem(start - nev + LANES, LANES), 1)
    added = added + pltpu.roll(to_right, lax.rem(start + nev, LANES), 1)
    sub = iota((8, LANES), 0)
    pair = jnp.where(lax.rem(sub, 2) == 0, own, -added)
    for k in range(out_ref.shape[0] // 8):
        out_ref[8 * k : 8 * k + 8, :] = pair


def third_kernel(
    got_ref, q_ref, z_ref, r_ref, coef_ref, e_ref, c_ref,
    q_out_ref, w_ref, v_ref, out_ref, rows_ref, block_ref, group_ref,
):
    nev, rows, columns = e_ref.shape
    half = columns // LANES
    stencil = Stencil(coef_ref)
    z, r = z_ref[...], r_ref[...]
    count = group_ref.shape[0]
    left, right = beside_columns(got_ref, 2, nev, rows)
    q = q_ref[...] - jnp.where(stencil.edges[2], left, 0.0)
    q = q - jnp.where(stencil.edges[3], right, 0.0)
    q_out_ref[...] = q
    added = got_ref[pl.ds(1, count, stride=2), :]
    group_ref[...] = (
        got_ref[pl.ds(0, count, stride=2), :]
        + pltpu.roll(added, 1, 0)
        + pltpu.roll(added, count - 1, 0)
    )
    y = coarse(c_ref, group_ref, nev, 1)
    w = stencil.smooth(q) + prolong(e_ref, y, rows_ref)
    v = stencil.apply(w)
    w_ref[...] = w
    v_ref[...] = v
    low = (stencil.faces[1] * w)[-1:]
    for k in range(half):
        block_ref[k : k + 1, :] = low[:, k * LANES : (k + 1) * LANES]
        block_ref[half + k : half + k + 1, :] = w[:1, k * LANES : (k + 1) * LANES]
    last = to_lanes(w[:, :1], 0) + to_lanes((stencil.faces[3] * w)[:, -1:], rows)
    lane = iota((1, LANES), 1)
    for k, product in enumerate((r * z, z * q, r * w, q * w, w * v)):
        last = jnp.where(lane == 2 * rows + k, total_of(product), last)
    size = block_ref.shape[0]
    block_ref[size - 1 : size, :] = last
    fill(out_ref, block_ref[...])


def fourth_kernel(got_ref, v_ref, coef_ref, v_out_ref, out_ref, block_ref):
    rows, columns = v_ref.shape
    half = columns // LANES
    size = 2 * half + 1
    count = got_ref.shape[0] // size
    z_count = count // 2
    z = lax.axis_index("zh") * 2 + lax.axis_index("zl")
    core = lax.axis_index("core")
    flat = jnp.zeros((half, LANES), jnp.float32)
    for i in range(count - 2):
        at, below = i * size, (i + 2) * size
        flat = flat + got_ref[at : at + half, :] * got_ref[below + half : below + 2 * half, :]
    west = got_ref[pl.ds(2 * half, z_count, stride=2 * size), :]
    east = got_ref[pl.ds(2 * half + size, z_count, stride=2 * size), :]
    facing = jnp.where(iota((z_count, LANES), 1) < rows, pltpu.roll(west, LANES - rows, 1) * east, 0.0)
    between = total_of(flat) + total_of(facing)
    lane = iota((1, LANES), 1)
    sums = jnp.sum(west + east, axis=0, keepdims=True)
    sums = jnp.where(lane == 2 * rows + 4, sums - 2.0 * between, sums)
    pack = LANES // rows
    zr = z_count // pack
    wide = iota((zr, LANES), 1)
    lefts = jnp.zeros((zr, LANES), jnp.float32)
    rights = lefts
    for j in range(pack):
        a = got_ref[pl.ds(2 * half + 2 * size * j, zr, stride=2 * size * pack), :]
        d = got_ref[pl.ds(2 * half + size + 2 * size * j, zr, stride=2 * size * pack), :]
        a = jnp.where(wide < rows, a, 0.0)
        d = jnp.where((wide >= rows) & (wide < 2 * rows), d, 0.0)
        if j > 0:
            a = pltpu.roll(a, rows * j, 1)
        if j != 1:
            d = pltpu.roll(d, (rows * (j - 1)) % LANES, 1)
        lefts, rights = lefts + a, rights + d
    block_ref[:zr, :] = lefts
    block_ref[zr : 2 * zr, :] = rights
    block_ref[2 * zr : 2 * zr + 1, :] = sums
    fill(out_ref, block_ref[...])

    above = jnp.maximum(2 * z - 2 + core, 0) * size
    below = jnp.minimum(2 * z + 2 + core, count - 1) * size + half
    up = jnp.concatenate([got_ref[pl.ds(above + k, 1), :] for k in range(half)], axis=1)
    down = jnp.concatenate([got_ref[pl.ds(below + k, 1), :] for k in range(half)], axis=1)
    up = jnp.where(z > 0, up, 0.0)
    down = jnp.where(z < z_count - 1, down, 0.0) * coef_ref[1, rows - 1 : rows, :]
    partner = got_ref[pl.ds((2 * z + 1 - core) * size + 2 * half, 1), :]
    left, right = to_column(partner, rows, rows), to_column(partner, 0, rows)
    edges = edges_of((rows, columns))
    v = v_ref[...]
    v = v - jnp.where(edges[0], up, 0.0) - jnp.where(edges[1], down, 0.0)
    v = v - jnp.where(edges[2], jnp.where(core == 1, left, 0.0), 0.0)
    v = v - jnp.where(edges[3], jnp.where(core == 0, right, 0.0) * coef_ref[3], 0.0)
    v_out_ref[...] = v


def closing_kernel(got_ref, v_ref, z_ref, w_ref, q_ref, r_ref, coef_ref, x_ref, res_ref):
    rows, columns = v_ref.shape
    pack = LANES // rows
    zr = lax.axis_size("zh") * 2 // pack
    size = 2 * zr + 1
    count = got_ref.shape[0] // size
    z = lax.axis_index("zh") * 2 + lax.axis_index("zl")
    xy, core = lax.axis_index("xy"), lax.axis_index("core")
    sums = got_ref[2 * zr : 2 * zr + 1, :]
    flat = jnp.zeros((zr, LANES), jnp.float32)
    for i in range(1, count):
        at = i * size
        sums = sums + got_ref[at + 2 * zr : at + 2 * zr + 1, :]
        flat = flat + got_ref[at - size + zr : at - size + 2 * zr, :] * got_ref[at : at + zr, :]
    across = total_of(flat)
    lane = iota((1, LANES), 1)
    rz, zq, rw, qw, wv = (
        jnp.sum(jnp.where(lane == 2 * rows + k, sums, 0.0), axis=1, keepdims=True)
        for k in range(5)
    )
    wv = wv - 2.0 * across
    step = rz / zq
    rz_new = rz - step * ((rw + zq) - step * qw)
    grow = 1.0 + rz_new / rz
    curve = grow * grow * zq - 2.0 * grow * step * qw + step * step * wv
    step_next = rz_new / curve
    on_z = step + step_next * grow
    on_w = step_next * step

    left_of, right_of = jnp.maximum(xy - 1, 0), jnp.minimum(xy + 1, count - 1)
    row = z // pack
    position = lax.rem(z, pack) * rows
    left = to_column(got_ref[pl.ds(left_of * size + zr + row, 1), :], position, rows)
    right = to_column(got_ref[pl.ds(right_of * size + row, 1), :], position, rows)
    left = jnp.where((core == 0) & (xy > 0), left, 0.0)
    right = jnp.where((core == 1) & (xy < count - 1), right, 0.0)
    edges = edges_of((rows, columns))
    v = v_ref[...]
    v = v - jnp.where(edges[2], left, 0.0) - jnp.where(edges[3], right * coef_ref[3], 0.0)
    x_ref[...] = on_z * z_ref[...] - on_w * w_ref[...]
    res_ref[...] = r_ref[...] - on_z * q_ref[...] + on_w * v


def call(kernel, name, args, outs, scratch=(), by_hand=False):
    whole = pl.BlockSpec(memory_space=pltpu.VMEM)
    scratch = [pltpu.VMEM(x, jnp.float32) if isinstance(x, tuple) else x for x in scratch]
    return pl.pallas_call(
        kernel,
        out_shape=[jax.ShapeDtypeStruct(shape, jnp.float32) for shape in outs],
        in_specs=[pl.BlockSpec(memory_space=pl.ANY) if by_hand else whole] * len(args),
        out_specs=[whole] * len(outs),
        scratch_shapes=scratch,
        compiler_params=pltpu.CompilerParams(vmem_limit_bytes=VMEM_LIMIT),
        name=name,
    )(*args)


def exchanged(x, axes, rows):
    flat = x.reshape(x.shape[0] // rows, rows * LANES)
    return lax.all_to_all(flat, axes, 0, 0, tiled=True).reshape(x.shape)


def swap_in(x, axis):
    return lax.ppermute(x, axis, [(0, 1), (1, 0)])


def swap_over(x, axes):
    count = lax.axis_size(axes)
    pairs = [(i, i + 1) for i in range(1, count - 1, 2)]
    return lax.ppermute(x, axes, pairs + [(j, i) for i, j in pairs])


def local(right_side, class_map, class_perm, eigenvectors, coarse_inverse):
    rows, columns = right_side.shape
    nev = eigenvectors.shape[0]
    field = (rows, columns)
    group = 2 * lax.axis_size(COLS)
    z_count, chips = lax.axis_size(ROWS), lax.axis_size("xy")
    size = 2 * (columns // LANES) + 1
    size_next = 2 * (z_count * rows // LANES) + 1
    per_vector = (nev, LANES)

    size_first = columns // LANES + 1
    given = (class_perm, right_side, class_map, eigenvectors, coarse_inverse)
    perm, over, facing, inside, message, r, vectors, matrix = call(
        opening_kernel, "opening",
        tuple(pltpu.with_memory_space_constraint(x, pltpu.HBM) for x in given),
        [field, (rows + 8, LANES), (rows, LANES), (rows, LANES), (size_first * group, LANES),
         field, eigenvectors.shape, coarse_inverse.shape],
        [pltpu.SMEM(class_perm.shape, jnp.float32), pltpu.VMEM(field, jnp.int32), per_vector,
         (size_first, LANES), pltpu.SemaphoreType.DMA((4 + PIECES,))],
        by_hand=True,
    )
    over, facing = swap_over(over, ROWS), swap_over(facing, COLS)
    inside = swap_in(inside, "core")
    got = exchanged(message, GROUP, size_first)
    z0, coef, z_over, z_in = call(
        first_kernel, "first", (got, over, perm, r, vectors, matrix),
        [field, (6,) + field, (1, columns), (1, columns)], [per_vector],
    )
    z_over, z_in = swap_over(z_over, ROWS), swap_in(z_in, "zl")
    q0, message = call(
        second_kernel, "second", (z_over, z_in, facing, inside, z0, coef, vectors),
        [field, (2 * group, LANES)], [per_vector],
    )
    got = exchanged(message, GROUP, 2)
    q0, w, v, message = call(
        third_kernel, "third", (got, q0, z0, r, coef, vectors, matrix),
        [field, field, field, (2 * z_count * size, LANES)],
        [per_vector, (size, LANES), (group, LANES)],
    )
    got = exchanged(message, STACK, size)
    v, message = call(
        fourth_kernel, "fourth", (got, v, coef),
        [field, (chips * size_next, LANES)], [(size_next, LANES)],
    )
    got = exchanged(message, PLANE, size_next)
    return tuple(call(closing_kernel, "closing", (got, v, z0, w, q0, r, coef), [field, field]))


def solution(mesh):
    n_gx, n_gy = mesh.devices.shape
    fine = Mesh(mesh.devices.reshape(n_gx // 2, 2, n_gy // 2, 2), FINE)
    in_specs = (P(ROWS, COLS), P(ROWS, COLS), P(), P(None, ROWS, COLS), P(FINE, None))
    out_specs = (P(ROWS, COLS), P(ROWS, COLS))
    return jax.shard_map(local, mesh=fine, in_specs=in_specs, out_specs=out_specs, check_vma=False)
```

```python
import jax
import jax.numpy as jnp
from jax import lax
from jax.experimental import pallas as pl
from jax.experimental.pallas import tpu as pltpu
from jax.sharding import Mesh, PartitionSpec as P

CHEB = 4
REACTION = 0.05
EIGEN_TOP = 2.0
EIGEN_LOW = 0.1
LANES = 128

ROWS = ("zh", "zl")
COLS = ("xy", "core")
GROUP = ("zl", "xy", "core")
STACK = ("zh", "zl", "core")
PLANE = ("xy",)
FINE = ("zh", "zl", "xy", "core")
VMEM_LIMIT = 24 * 1024 * 1024
PIECES = 5


def iota(shape, dim):
    return lax.broadcasted_iota(jnp.int32, shape, dim)


def harmonic(centre, beside):
    return jnp.where(beside > 0.0, 2.0 * centre * beside / (centre + beside), centre)


def shifts(v):
    rows, columns = v.shape
    return (
        pltpu.roll(v, 1, 0),
        pltpu.roll(v, rows - 1, 0),
        pltpu.roll(v, 1, 1),
        pltpu.roll(v, columns - 1, 1),
    )


def edges_of(shape):
    row, column = iota(shape, 0), iota(shape, 1)
    return (row == 0, row == shape[0] - 1, column == 0, column == shape[1] - 1)


class Stencil:
    def __init__(self, coef):
        self.faces = tuple(coef[k] for k in range(4))
        self.diagonal, self.inverse = coef[4], coef[5]
        self.edges = edges_of(self.diagonal.shape)
        self.inner = tuple(
            jnp.where(edge, 0.0, face) for edge, face in zip(self.edges, self.faces)
        )

    def apply(self, v):
        result = self.diagonal * v
        for weight, near in zip(self.inner, shifts(v)):
            result = result - weight * near
        return result

    def smooth(self, source):
        centre = 0.5 * (EIGEN_TOP + EIGEN_LOW)
        radius = 0.5 * (EIGEN_TOP - EIGEN_LOW)
        ratio_start = centre / radius
        factor = 1.0 / ratio_start
        update = source * self.inverse * (1.0 / centre)
        smoothed = update
        for _ in range(1, CHEB):
            defect = source - self.apply(smoothed)
            factor_next = 1.0 / (2.0 * ratio_start - factor)
            update = factor_next * factor * update + (2.0 * factor_next / radius) * (
                defect * self.inverse
            )
            smoothed = smoothed + update
            factor = factor_next
        return smoothed


def to_lanes(column, start):
    n = column.shape[0]
    want = lax.rem(iota((n, LANES), 1) - start + 8 * LANES, LANES)
    hit = want == iota((n, LANES), 0)
    return jnp.sum(jnp.where(hit, column, 0.0), axis=0, keepdims=True)


def to_column(row, start, n):
    want = lax.rem(iota((n, LANES), 1) - start + 8 * LANES, LANES)
    hit = want == iota((n, LANES), 0)
    return jnp.sum(jnp.where(hit, row, 0.0), axis=1, keepdims=True)


def project_one(own, v, rows_ref, e):
    rows, columns = v.shape
    p = own * v
    q = p[:, :LANES]
    for k in range(1, columns // LANES):
        q = q + p[:, k * LANES : (k + 1) * LANES]
    s = q[:8]
    for k in range(1, rows // 8):
        s = s + q[8 * k : 8 * k + 8]
    rows_ref[e : e + 1, :] = jnp.sum(s, axis=0, keepdims=True)


def project(e_ref, v, rows_ref):
    for e in range(e_ref.shape[0]):
        project_one(e_ref[e], v, rows_ref, e)
    return jnp.sum(rows_ref[...], axis=1, keepdims=True)


def coarse(c_ref, gathered_ref, nev, stride):
    dofs = c_ref.shape[1]
    lane = iota((1, LANES), 1)
    total = None
    for r in range(dofs // LANES):
        low = r * LANES // nev
        high = (r * LANES + LANES - 1) // nev
        flat = gathered_ref[low * stride : low * stride + 1, :]
        for d in range(low + 1, high + 1):
            row = gathered_ref[d * stride : d * stride + 1, :]
            flat = jnp.where(lane >= d * nev - r * LANES, row, flat)
        term = c_ref[:, r * LANES : (r + 1) * LANES] * flat
        total = term if total is None else total + term
    return jnp.sum(total, axis=1, keepdims=True)


def prolong(e_ref, y, rows_ref):
    nev = e_ref.shape[0]
    rows_ref[...] = jnp.broadcast_to(y, (nev, LANES))
    reps = e_ref.shape[2] // LANES
    result = None
    for e in range(nev):
        weight = jnp.concatenate([rows_ref[e : e + 1, :]] * reps, axis=1)
        term = weight * e_ref[e]
        result = term if result is None else result + term
    return result


def total_of(v):
    return jnp.sum(jnp.sum(v, axis=0, keepdims=True), axis=1, keepdims=True)


def fill(out_ref, message):
    size = message.shape[0]
    count = out_ref.shape[0] // size
    batch = min(8, count)
    for i in range(batch):
        out_ref[i * size : (i + 1) * size, :] = message
    pattern = out_ref[: batch * size, :]
    for k in range(1, count // batch):
        out_ref[k * batch * size : (k + 1) * batch * size, :] = pattern


def group_place():
    return (lax.axis_index("zl") * lax.axis_size("xy") + lax.axis_index("xy")) * 2 + lax.axis_index(
        "core"
    )


def column_place():
    return lax.axis_index("xy") * 2 + lax.axis_index("core")


def lane_start(place, nev):
    return lax.rem(place * nev, LANES)


def opening_kernel(
    kinds_hbm, r_hbm, map_hbm, e_hbm, c_hbm,
    perm_ref, over_ref, facing_ref, row_ref, out_ref, r_ref, e_ref, c_ref,
    kinds_ref, map_ref, rows_ref, block_ref, sems,
):
    nev, rows, columns = e_ref.shape
    steps = sems.shape[0] - 4
    chunk = nev // steps
    small = [
        pltpu.make_async_copy(source, target, sems.at[k])
        for k, (source, target) in enumerate(
            ((kinds_hbm, kinds_ref), (map_hbm, map_ref), (r_hbm, r_ref))
        )
    ]
    parts = [
        pltpu.make_async_copy(
            e_hbm.at[pl.ds(k * chunk, chunk)], e_ref.at[pl.ds(k * chunk, chunk)], sems.at[4 + k]
        )
        for k in range(steps)
    ]
    matrix = pltpu.make_async_copy(c_hbm, c_ref, sems.at[3])
    for copy in parts[:2] + small + parts[2:] + [matrix]:
        copy.start()
    for copy in small:
        copy.wait()
    classes = map_ref[...]
    perm = jnp.full(classes.shape, kinds_ref[0])
    for k in range(1, kinds_ref.shape[0]):
        perm = jnp.where(classes == k, kinds_ref[k], perm)
    perm_ref[...] = perm
    upper = lax.axis_index("zl") == 0
    over = jnp.where(upper, perm[:1], perm[-1:])
    within = jnp.where(upper, perm[-1:], perm[:1])
    over_ref[...] = jnp.zeros_like(over_ref)
    for k in range(columns // LANES):
        over_ref[k : k + 1, :] = over[:, k * LANES : (k + 1) * LANES]
    r = r_ref[...]
    first = lax.axis_index("core") == 0
    block = pl.multiple_of(jnp.where(first, 0, columns - LANES), LANES)
    turn = jnp.where(first, 0, 1)
    lane = iota((rows, LANES), 1)
    facing = jnp.zeros((rows, LANES), jnp.float32)
    for k in range(steps):
        parts[k].wait()
        for e in range(k * chunk, (k + 1) * chunk):
            own = e_ref[e]
            project_one(own, r, rows_ref, e)
            row_ref[e : e + 1, :] = jnp.where(upper, own[rows - 1 :], own[:1])
            edge = pltpu.roll(e_ref[e, :, pl.ds(block, LANES)], e + turn, 1)
            facing = jnp.where(lane == e, edge, facing)
    facing_ref[...] = facing
    c = jnp.sum(rows_ref[...], axis=1, keepdims=True)
    start = lane_start(group_place(), nev)
    size = block_ref.shape[0]
    block_ref[:1, :] = (
        to_lanes(c, start)
        + to_lanes(perm[:, :1], start + nev)
        + to_lanes(perm[:, -1:], start + nev + rows)
    )
    for k in range(size - 1):
        block_ref[k + 1 : k + 2, :] = within[:, k * LANES : (k + 1) * LANES]
    fill(out_ref, block_ref[...])
    matrix.wait()


def beside_columns(got_ref, stride, nev, rows):
    place, b, b_count = group_place(), column_place(), lax.axis_size("xy") * 2
    last = got_ref.shape[0] // stride - 1
    before, after = jnp.maximum(place - 1, 0), jnp.minimum(place + 1, last)
    left = to_column(
        got_ref[pl.ds(before * stride, 1), :], lane_start(before, nev) + nev + rows, rows
    )
    right = to_column(got_ref[pl.ds(after * stride, 1), :], lane_start(after, nev) + nev, rows)
    return jnp.where(b > 0, left, 0.0), jnp.where(b < b_count - 1, right, 0.0)


def first_kernel(
    got_ref, over_ref, perm_ref, r_ref, e_ref, c_ref,
    z_ref, coef_ref, z_over_ref, y_in_ref, rows_ref,
):
    nev, rows, columns = e_ref.shape
    size = columns // LANES + 1
    upper = lax.axis_index("zl") == 0
    first = lax.axis_index("core") == 0
    left, right = beside_columns(got_ref, size, nev, rows)
    across = lax.axis_size("xy") * 2
    partner = (group_place() + jnp.where(upper, across, -across)) * size
    over = jnp.concatenate([over_ref[k : k + 1, :] for k in range(size - 1)], axis=1)
    within = jnp.concatenate(
        [got_ref[pl.ds(partner + 1 + k, 1), :] for k in range(size - 1)], axis=1
    )
    halo = (jnp.where(upper, over, within), jnp.where(upper, within, over), left, right)
    perm = perm_ref[...]
    edges = edges_of(perm.shape)
    faces = []
    for edge, near, outside in zip(edges, shifts(perm), halo):
        faces.append(harmonic(perm, jnp.where(edge, outside, near)))
    diagonal = REACTION + faces[0] + faces[1] + faces[2] + faces[3]
    coef = faces + [diagonal, 1.0 / diagonal]
    for k in range(6):
        coef_ref[k] = coef[k]
    stencil = Stencil(coef)
    y = coarse(c_ref, got_ref, nev, size)
    z = stencil.smooth(r_ref[...]) + prolong(e_ref, y, rows_ref)
    z_ref[...] = z
    top, low = (faces[0] * z)[:1], (faces[1] * z)[-1:]
    z_over_ref[...] = jnp.where(upper, top, low)
    lefts, rights = to_lanes((faces[2] * z)[:, :1], 0), to_lanes((faces[3] * z)[:, -1:], 0)
    y_in_ref[...] = jnp.where(first, rights, lefts)


def second_kernel(
    z_over_ref, y_in_ref, facing_ref, row_ref, z_ref, coef_ref, e_ref,
    q_ref, z_in_ref, out_ref, rows_ref,
):
    nev, rows, _ = e_ref.shape
    upper = lax.axis_index("zl") == 0
    first = lax.axis_index("core") == 0
    stencil = Stencil(coef_ref)
    over = z_over_ref[...]
    y_in = to_column(y_in_ref[...], 0, rows)
    halo = (
        jnp.where(upper, over, 0.0),
        jnp.where(upper, 0.0, over),
        jnp.where(first, 0.0, y_in),
        jnp.where(first, y_in, 0.0),
    )
    z = z_ref[...]
    q = stencil.apply(z)
    for edge, outside in zip(stencil.edges, halo):
        q = q - jnp.where(edge, outside, 0.0)
    q_ref[...] = q
    within = jnp.where(upper, (stencil.faces[1] * z)[-1:], (stencil.faces[0] * z)[:1])
    z_in_ref[...] = within
    left, right = (stencil.faces[2] * z)[:, :1], (stencil.faces[3] * z)[:, -1:]
    edge = jnp.where(first, left, right)
    start = lane_start(group_place(), nev)
    own = to_lanes(project(e_ref, q, rows_ref), start) + to_lanes(edge, start + nev)
    added = jnp.sum(facing_ref[...] * edge, axis=0, keepdims=True)
    step = jnp.where(first, LANES - nev, nev)
    added = pltpu.roll(added, lax.rem(start + step, LANES), 1)
    across = lax.axis_size("xy") * 2
    partner = group_place() + jnp.where(upper, across, -across)
    below = jnp.sum(row_ref[...] * within, axis=1, keepdims=True)
    added = added + to_lanes(below, lane_start(partner, nev))
    sub = iota((8, LANES), 0)
    pair = jnp.where(lax.rem(sub, 2) == 0, own, -added)
    for k in range(out_ref.shape[0] // 8):
        out_ref[8 * k : 8 * k + 8, :] = pair


def third_kernel(
    got_ref, z_in_ref, q_ref, z_ref, r_ref, coef_ref, e_ref, c_ref,
    q_out_ref, w_ref, v_ref, out_ref, rows_ref, block_ref, group_ref,
):
    nev, rows, columns = e_ref.shape
    half = columns // LANES
    stencil = Stencil(coef_ref)
    z, r = z_ref[...], r_ref[...]
    first = lax.axis_index("core") == 0
    place, b, count = group_place(), column_place(), group_ref.shape[0]
    near = jnp.where(first, jnp.maximum(place - 1, 0), jnp.minimum(place + 1, count - 1))
    edge = to_column(got_ref[pl.ds(2 * near, 1), :], lane_start(near, nev) + nev, rows)
    left = jnp.where(first & (b > 0), edge, 0.0)
    right = jnp.where((~first) & (b < lax.axis_size("xy") * 2 - 1), edge, 0.0)
    q = q_ref[...] - jnp.where(stencil.edges[2], left, 0.0)
    q = q - jnp.where(stencil.edges[3], right, 0.0)
    upper = lax.axis_index("zl") == 0
    within = z_in_ref[...]
    q = q - jnp.where(stencil.edges[0], jnp.where(upper, 0.0, within), 0.0)
    q = q - jnp.where(stencil.edges[1], jnp.where(upper, within, 0.0), 0.0)
    q_out_ref[...] = q
    added = got_ref[pl.ds(1, count, stride=2), :]
    group_ref[...] = (
        got_ref[pl.ds(0, count, stride=2), :]
        + pltpu.roll(added, 1, 0)
        + pltpu.roll(added, count - 1, 0)
        + pltpu.roll(added, count // 2, 0)
    )
    y = coarse(c_ref, group_ref, nev, 1)
    w = stencil.smooth(q) + prolong(e_ref, y, rows_ref)
    v = stencil.apply(w)
    w_ref[...] = w
    v_ref[...] = v
    low = (stencil.faces[1] * w)[-1:]
    for k in range(half):
        block_ref[k : k + 1, :] = low[:, k * LANES : (k + 1) * LANES]
        block_ref[half + k : half + k + 1, :] = w[:1, k * LANES : (k + 1) * LANES]
    last = to_lanes(w[:, :1], 0) + to_lanes((stencil.faces[3] * w)[:, -1:], rows)
    lane = iota((1, LANES), 1)
    for k, product in enumerate((r * z, z * q, r * w, q * w, w * v)):
        last = jnp.where(lane == 2 * rows + k, total_of(product), last)
    size = block_ref.shape[0]
    block_ref[size - 1 : size, :] = last
    fill(out_ref, block_ref[...])


def fourth_kernel(got_ref, v_ref, coef_ref, v_out_ref, out_ref, block_ref):
    rows, columns = v_ref.shape
    half = columns // LANES
    size = 2 * half + 1
    count = got_ref.shape[0] // size
    z_count = count // 2
    z = lax.axis_index("zh") * 2 + lax.axis_index("zl")
    core = lax.axis_index("core")
    flat = jnp.zeros((half, LANES), jnp.float32)
    for i in range(count - 2):
        at, below = i * size, (i + 2) * size
        flat = flat + got_ref[at : at + half, :] * got_ref[below + half : below + 2 * half, :]
    west = got_ref[pl.ds(2 * half, z_count, stride=2 * size), :]
    east = got_ref[pl.ds(2 * half + size, z_count, stride=2 * size), :]
    facing = jnp.where(iota((z_count, LANES), 1) < rows, pltpu.roll(west, LANES - rows, 1) * east, 0.0)
    between = total_of(flat) + total_of(facing)
    lane = iota((1, LANES), 1)
    sums = jnp.sum(west + east, axis=0, keepdims=True)
    sums = jnp.where(lane == 2 * rows + 4, sums - 2.0 * between, sums)
    pack = LANES // rows
    zr = z_count // pack
    wide = iota((zr, LANES), 1)
    lefts = jnp.zeros((zr, LANES), jnp.float32)
    rights = lefts
    for j in range(pack):
        a = got_ref[pl.ds(2 * half + 2 * size * j, zr, stride=2 * size * pack), :]
        d = got_ref[pl.ds(2 * half + size + 2 * size * j, zr, stride=2 * size * pack), :]
        a = jnp.where(wide < rows, a, 0.0)
        d = jnp.where((wide >= rows) & (wide < 2 * rows), d, 0.0)
        if j > 0:
            a = pltpu.roll(a, rows * j, 1)
        if j != 1:
            d = pltpu.roll(d, (rows * (j - 1)) % LANES, 1)
        lefts, rights = lefts + a, rights + d
    block_ref[:zr, :] = lefts
    block_ref[zr : 2 * zr, :] = rights
    block_ref[2 * zr : 2 * zr + 1, :] = sums
    fill(out_ref, block_ref[...])

    above = jnp.maximum(2 * z - 2 + core, 0) * size
    below = jnp.minimum(2 * z + 2 + core, count - 1) * size + half
    up = jnp.concatenate([got_ref[pl.ds(above + k, 1), :] for k in range(half)], axis=1)
    down = jnp.concatenate([got_ref[pl.ds(below + k, 1), :] for k in range(half)], axis=1)
    up = jnp.where(z > 0, up, 0.0)
    down = jnp.where(z < z_count - 1, down, 0.0) * coef_ref[1, rows - 1 : rows, :]
    partner = got_ref[pl.ds((2 * z + 1 - core) * size + 2 * half, 1), :]
    left, right = to_column(partner, rows, rows), to_column(partner, 0, rows)
    edges = edges_of((rows, columns))
    v = v_ref[...]
    v = v - jnp.where(edges[0], up, 0.0) - jnp.where(edges[1], down, 0.0)
    v = v - jnp.where(edges[2], jnp.where(core == 1, left, 0.0), 0.0)
    v = v - jnp.where(edges[3], jnp.where(core == 0, right, 0.0) * coef_ref[3], 0.0)
    v_out_ref[...] = v


def closing_kernel(got_ref, v_ref, z_ref, w_ref, q_ref, r_ref, coef_ref, x_ref, res_ref):
    rows, columns = v_ref.shape
    pack = LANES // rows
    zr = lax.axis_size("zh") * 2 // pack
    size = 2 * zr + 1
    count = got_ref.shape[0] // size
    z = lax.axis_index("zh") * 2 + lax.axis_index("zl")
    xy, core = lax.axis_index("xy"), lax.axis_index("core")
    sums = got_ref[2 * zr : 2 * zr + 1, :]
    flat = jnp.zeros((zr, LANES), jnp.float32)
    for i in range(1, count):
        at = i * size
        sums = sums + got_ref[at + 2 * zr : at + 2 * zr + 1, :]
        flat = flat + got_ref[at - size + zr : at - size + 2 * zr, :] * got_ref[at : at + zr, :]
    across = total_of(flat)
    lane = iota((1, LANES), 1)
    rz, zq, rw, qw, wv = (
        jnp.sum(jnp.where(lane == 2 * rows + k, sums, 0.0), axis=1, keepdims=True)
        for k in range(5)
    )
    wv = wv - 2.0 * across
    step = rz / zq
    rz_new = rz - step * ((rw + zq) - step * qw)
    grow = 1.0 + rz_new / rz
    curve = grow * grow * zq - 2.0 * grow * step * qw + step * step * wv
    step_next = rz_new / curve
    on_z = step + step_next * grow
    on_w = step_next * step

    left_of, right_of = jnp.maximum(xy - 1, 0), jnp.minimum(xy + 1, count - 1)
    row = z // pack
    position = lax.rem(z, pack) * rows
    left = to_column(got_ref[pl.ds(left_of * size + zr + row, 1), :], position, rows)
    right = to_column(got_ref[pl.ds(right_of * size + row, 1), :], position, rows)
    left = jnp.where((core == 0) & (xy > 0), left, 0.0)
    right = jnp.where((core == 1) & (xy < count - 1), right, 0.0)
    edges = edges_of((rows, columns))
    v = v_ref[...]
    v = v - jnp.where(edges[2], left, 0.0) - jnp.where(edges[3], right * coef_ref[3], 0.0)
    x_ref[...] = on_z * z_ref[...] - on_w * w_ref[...]
    res_ref[...] = r_ref[...] - on_z * q_ref[...] + on_w * v


def call(kernel, name, args, outs, scratch=(), by_hand=False):
    whole = pl.BlockSpec(memory_space=pltpu.VMEM)
    scratch = [pltpu.VMEM(x, jnp.float32) if isinstance(x, tuple) else x for x in scratch]
    return pl.pallas_call(
        kernel,
        out_shape=[jax.ShapeDtypeStruct(shape, jnp.float32) for shape in outs],
        in_specs=[pl.BlockSpec(memory_space=pl.ANY) if by_hand else whole] * len(args),
        out_specs=[whole] * len(outs),
        scratch_shapes=scratch,
        compiler_params=pltpu.CompilerParams(vmem_limit_bytes=VMEM_LIMIT),
        name=name,
    )(*args)


def exchanged(x, axes, rows):
    flat = x.reshape(x.shape[0] // rows, rows * LANES)
    return lax.all_to_all(flat, axes, 0, 0, tiled=True).reshape(x.shape)


def swap_in(x, axis):
    return lax.ppermute(x, axis, [(0, 1), (1, 0)])


def swap_over(x, axes):
    count = lax.axis_size(axes)
    pairs = [(i, i + 1) for i in range(1, count - 1, 2)]
    return lax.ppermute(x, axes, pairs + [(j, i) for i, j in pairs])


def local(right_side, class_map, class_perm, eigenvectors, coarse_inverse):
    rows, columns = right_side.shape
    nev = eigenvectors.shape[0]
    field = (rows, columns)
    group = 2 * lax.axis_size(COLS)
    z_count, chips = lax.axis_size(ROWS), lax.axis_size("xy")
    size = 2 * (columns // LANES) + 1
    size_next = 2 * (z_count * rows // LANES) + 1
    per_vector = (nev, LANES)

    size_first = columns // LANES + 1
    given = (class_perm, right_side, class_map, eigenvectors, coarse_inverse)
    perm, over, facing, row, message, r, vectors, matrix = call(
        opening_kernel, "opening",
        tuple(pltpu.with_memory_space_constraint(x, pltpu.HBM) for x in given),
        [field, (2 * nev + 8, LANES), (rows, LANES), (nev, columns), (size_first * group, LANES),
         field, eigenvectors.shape, coarse_inverse.shape],
        [pltpu.SMEM(class_perm.shape, jnp.float32), pltpu.VMEM(field, jnp.int32), per_vector,
         (size_first, LANES), pltpu.SemaphoreType.DMA((4 + PIECES,))],
        by_hand=True,
    )
    over, row = swap_over(over, ROWS), swap_in(row, "zl")
    facing = swap_over(facing, COLS)
    got = exchanged(message, GROUP, size_first)
    z0, coef, z_over, y_in = call(
        first_kernel, "first", (got, over, perm, r, vectors, matrix),
        [field, (6,) + field, (1, columns), (1, LANES)], [per_vector],
    )
    z_over, y_in = swap_over(z_over, ROWS), swap_in(y_in, "core")
    q0, z_in, message = call(
        second_kernel, "second", (z_over, y_in, facing, row, z0, coef, vectors),
        [field, (1, columns), (2 * group, LANES)], [per_vector],
    )
    z_in = swap_in(z_in, "zl")
    got = exchanged(message, GROUP, 2)
    q0, w, v, message = call(
        third_kernel, "third", (got, z_in, q0, z0, r, coef, vectors, matrix),
        [field, field, field, (2 * z_count * size, LANES)],
        [per_vector, (size, LANES), (group, LANES)],
    )
    got = exchanged(message, STACK, size)
    v, message = call(
        fourth_kernel, "fourth", (got, v, coef),
        [field, (chips * size_next, LANES)], [(size_next, LANES)],
    )
    got = exchanged(message, PLANE, size_next)
    return tuple(call(closing_kernel, "closing", (got, v, z0, w, q0, r, coef), [field, field]))


def solution(mesh):
    n_gx, n_gy = mesh.devices.shape
    fine = Mesh(mesh.devices.reshape(n_gx // 2, 2, n_gy // 2, 2), FINE)
    in_specs = (P(ROWS, COLS), P(ROWS, COLS), P(), P(None, ROWS, COLS), P(FINE, None))
    out_specs = (P(ROWS, COLS), P(ROWS, COLS))
    return jax.shard_map(local, mesh=fine, in_specs=in_specs, out_specs=out_specs, check_vma=False)
```

```python
import jax
import jax.numpy as jnp
from jax import lax
from jax.experimental import pallas as pl
from jax.experimental.pallas import tpu as pltpu
from jax.sharding import Mesh, PartitionSpec as P

CHEB = 4
REACTION = 0.05
EIGEN_TOP = 2.0
EIGEN_LOW = 0.1
LANES = 128

ROWS = ("zh", "zl")
COLS = ("xy", "core")
GROUP = ("zl", "xy", "core")
STACK = ("zh", "zl", "core")
PLANE = ("xy",)
FINE = ("zh", "zl", "xy", "core")
VMEM_LIMIT = 24 * 1024 * 1024
PIECES = 5


def iota(shape, dim):
    return lax.broadcasted_iota(jnp.int32, shape, dim)


def harmonic(centre, beside):
    return jnp.where(beside > 0.0, 2.0 * centre * beside / (centre + beside), centre)


def shifts(v):
    rows, columns = v.shape
    return (
        pltpu.roll(v, 1, 0),
        pltpu.roll(v, rows - 1, 0),
        pltpu.roll(v, 1, 1),
        pltpu.roll(v, columns - 1, 1),
    )


def edges_of(shape):
    row, column = iota(shape, 0), iota(shape, 1)
    return (row == 0, row == shape[0] - 1, column == 0, column == shape[1] - 1)


class Stencil:
    def __init__(self, coef):
        self.faces = tuple(coef[k] for k in range(4))
        self.diagonal, self.inverse = coef[4], coef[5]
        self.edges = edges_of(self.diagonal.shape)
        self.inner = tuple(
            jnp.where(edge, 0.0, face) for edge, face in zip(self.edges, self.faces)
        )

    def apply(self, v):
        result = self.diagonal * v
        for weight, near in zip(self.inner, shifts(v)):
            result = result - weight * near
        return result

    def smooth(self, source):
        centre = 0.5 * (EIGEN_TOP + EIGEN_LOW)
        radius = 0.5 * (EIGEN_TOP - EIGEN_LOW)
        ratio_start = centre / radius
        factor = 1.0 / ratio_start
        update = source * self.inverse * (1.0 / centre)
        smoothed = update
        for _ in range(1, CHEB):
            defect = source - self.apply(smoothed)
            factor_next = 1.0 / (2.0 * ratio_start - factor)
            update = factor_next * factor * update + (2.0 * factor_next / radius) * (
                defect * self.inverse
            )
            smoothed = smoothed + update
            factor = factor_next
        return smoothed


def to_lanes(column, start):
    n = column.shape[0]
    want = lax.rem(iota((n, LANES), 1) - start + 8 * LANES, LANES)
    hit = want == iota((n, LANES), 0)
    return jnp.sum(jnp.where(hit, column, 0.0), axis=0, keepdims=True)


def to_column(row, start, n):
    want = lax.rem(iota((n, LANES), 1) - start + 8 * LANES, LANES)
    hit = want == iota((n, LANES), 0)
    return jnp.sum(jnp.where(hit, row, 0.0), axis=1, keepdims=True)


def project_one(own, v, rows_ref, e):
    rows, columns = v.shape
    p = own * v
    q = p[:, :LANES]
    for k in range(1, columns // LANES):
        q = q + p[:, k * LANES : (k + 1) * LANES]
    s = q[:8]
    for k in range(1, rows // 8):
        s = s + q[8 * k : 8 * k + 8]
    rows_ref[e : e + 1, :] = jnp.sum(s, axis=0, keepdims=True)


def project(e_ref, v, rows_ref):
    for e in range(e_ref.shape[0]):
        project_one(e_ref[e], v, rows_ref, e)
    return jnp.sum(rows_ref[...], axis=1, keepdims=True)


def coarse(c_ref, gathered_ref, nev, stride):
    dofs = c_ref.shape[1]
    lane = iota((1, LANES), 1)
    total = None
    for r in range(dofs // LANES):
        low = r * LANES // nev
        high = (r * LANES + LANES - 1) // nev
        flat = gathered_ref[low * stride : low * stride + 1, :]
        for d in range(low + 1, high + 1):
            row = gathered_ref[d * stride : d * stride + 1, :]
            flat = jnp.where(lane >= d * nev - r * LANES, row, flat)
        term = c_ref[:, r * LANES : (r + 1) * LANES] * flat
        total = term if total is None else total + term
    return jnp.sum(total, axis=1, keepdims=True)


def prolong(e_ref, y, rows_ref):
    nev = e_ref.shape[0]
    rows_ref[...] = jnp.broadcast_to(y, (nev, LANES))
    reps = e_ref.shape[2] // LANES
    result = None
    for e in range(nev):
        weight = jnp.concatenate([rows_ref[e : e + 1, :]] * reps, axis=1)
        term = weight * e_ref[e]
        result = term if result is None else result + term
    return result


def total_of(v):
    return jnp.sum(jnp.sum(v, axis=0, keepdims=True), axis=1, keepdims=True)


def fill(out_ref, message):
    size = message.shape[0]
    count = out_ref.shape[0] // size
    batch = min(8, count)
    for i in range(batch):
        out_ref[i * size : (i + 1) * size, :] = message
    pattern = out_ref[: batch * size, :]
    for k in range(1, count // batch):
        out_ref[k * batch * size : (k + 1) * batch * size, :] = pattern


def group_place():
    return (lax.axis_index("zl") * lax.axis_size("xy") + lax.axis_index("xy")) * 2 + lax.axis_index(
        "core"
    )


def column_place():
    return lax.axis_index("xy") * 2 + lax.axis_index("core")


def lane_start(place, nev):
    return lax.rem(place * nev, LANES)


def opening_kernel(
    kinds_hbm, r_hbm, map_hbm, e_hbm, c_hbm,
    perm_ref, over_ref, facing_ref, inside_ref, out_ref, r_ref, e_ref, c_ref,
    kinds_ref, map_ref, rows_ref, block_ref, sems,
):
    nev, rows, columns = e_ref.shape
    steps = sems.shape[0] - 4
    chunk = nev // steps
    small = [
        pltpu.make_async_copy(source, target, sems.at[k])
        for k, (source, target) in enumerate(
            ((kinds_hbm, kinds_ref), (map_hbm, map_ref), (r_hbm, r_ref))
        )
    ]
    parts = [
        pltpu.make_async_copy(
            e_hbm.at[pl.ds(k * chunk, chunk)], e_ref.at[pl.ds(k * chunk, chunk)], sems.at[4 + k]
        )
        for k in range(steps)
    ]
    matrix = pltpu.make_async_copy(c_hbm, c_ref, sems.at[3])
    for copy in parts[:2] + small + parts[2:] + [matrix]:
        copy.start()
    for copy in small:
        copy.wait()
    classes = map_ref[...]
    perm = jnp.full(classes.shape, kinds_ref[0])
    for k in range(1, kinds_ref.shape[0]):
        perm = jnp.where(classes == k, kinds_ref[k], perm)
    perm_ref[...] = perm
    upper = lax.axis_index("zl") == 0
    over = jnp.where(upper, perm[:1], perm[-1:])
    within = jnp.where(upper, perm[-1:], perm[:1])
    over_ref[...] = jnp.zeros_like(over_ref)
    for k in range(columns // LANES):
        over_ref[k : k + 1, :] = over[:, k * LANES : (k + 1) * LANES]
    r = r_ref[...]
    first = lax.axis_index("core") == 0
    block = pl.multiple_of(jnp.where(first, 0, columns - LANES), LANES)
    other = pl.multiple_of(jnp.where(first, columns - LANES, 0), LANES)
    turn = jnp.where(first, 0, 1)
    lane = iota((rows, LANES), 1)
    facing = jnp.zeros((rows, LANES), jnp.float32)
    inside = facing
    for k in range(steps):
        parts[k].wait()
        for e in range(k * chunk, (k + 1) * chunk):
            project_one(e_ref[e], r, rows_ref, e)
            edge = pltpu.roll(e_ref[e, :, pl.ds(block, LANES)], e + turn, 1)
            facing = jnp.where(lane == e, edge, facing)
            edge = pltpu.roll(e_ref[e, :, pl.ds(other, LANES)], e + 1 - turn, 1)
            inside = jnp.where(lane == e, edge, inside)
    facing_ref[...] = facing
    inside_ref[...] = inside
    c = jnp.sum(rows_ref[...], axis=1, keepdims=True)
    start = lane_start(group_place(), nev)
    size = block_ref.shape[0]
    block_ref[:1, :] = (
        to_lanes(c, start)
        + to_lanes(perm[:, :1], start + nev)
        + to_lanes(perm[:, -1:], start + nev + rows)
    )
    for k in range(size - 1):
        block_ref[k + 1 : k + 2, :] = within[:, k * LANES : (k + 1) * LANES]
    fill(out_ref, block_ref[...])
    matrix.wait()


def beside_columns(got_ref, stride, nev, rows):
    place, b, b_count = group_place(), column_place(), lax.axis_size("xy") * 2
    last = got_ref.shape[0] // stride - 1
    before, after = jnp.maximum(place - 1, 0), jnp.minimum(place + 1, last)
    left = to_column(
        got_ref[pl.ds(before * stride, 1), :], lane_start(before, nev) + nev + rows, rows
    )
    right = to_column(got_ref[pl.ds(after * stride, 1), :], lane_start(after, nev) + nev, rows)
    return jnp.where(b > 0, left, 0.0), jnp.where(b < b_count - 1, right, 0.0)


def first_kernel(
    got_ref, over_ref, perm_ref, r_ref, e_ref, c_ref,
    z_ref, coef_ref, z_over_ref, z_in_ref, rows_ref,
):
    nev, rows, columns = e_ref.shape
    size = columns // LANES + 1
    upper = lax.axis_index("zl") == 0
    left, right = beside_columns(got_ref, size, nev, rows)
    across = lax.axis_size("xy") * 2
    partner = (group_place() + jnp.where(upper, across, -across)) * size
    over = jnp.concatenate([over_ref[k : k + 1, :] for k in range(size - 1)], axis=1)
    within = jnp.concatenate(
        [got_ref[pl.ds(partner + 1 + k, 1), :] for k in range(size - 1)], axis=1
    )
    halo = (jnp.where(upper, over, within), jnp.where(upper, within, over), left, right)
    perm = perm_ref[...]
    edges = edges_of(perm.shape)
    faces = []
    for edge, near, outside in zip(edges, shifts(perm), halo):
        faces.append(harmonic(perm, jnp.where(edge, outside, near)))
    diagonal = REACTION + faces[0] + faces[1] + faces[2] + faces[3]
    coef = faces + [diagonal, 1.0 / diagonal]
    for k in range(6):
        coef_ref[k] = coef[k]
    stencil = Stencil(coef)
    y = coarse(c_ref, got_ref, nev, size)
    z = stencil.smooth(r_ref[...]) + prolong(e_ref, y, rows_ref)
    z_ref[...] = z
    top, low = (faces[0] * z)[:1], (faces[1] * z)[-1:]
    z_over_ref[...] = jnp.where(upper, top, low)
    z_in_ref[...] = jnp.where(upper, low, top)


def second_kernel(
    z_in_ref, z_over_ref, facing_ref, inside_ref, z_ref, coef_ref, e_ref, q_ref, out_ref, rows_ref
):
    nev, rows, _ = e_ref.shape
    upper = lax.axis_index("zl") == 0
    first = lax.axis_index("core") == 0
    stencil = Stencil(coef_ref)
    over, within = z_over_ref[...], z_in_ref[...]
    z = z_ref[...]
    q = stencil.apply(z)
    q = q - jnp.where(stencil.edges[0], jnp.where(upper, over, within), 0.0)
    q = q - jnp.where(stencil.edges[1], jnp.where(upper, within, over), 0.0)
    q_ref[...] = q
    left, right = (stencil.faces[2] * z)[:, :1], (stencil.faces[3] * z)[:, -1:]
    start = lane_start(group_place(), nev)
    own = to_lanes(project(e_ref, q, rows_ref), start)
    own = own + to_lanes(left, start + nev) + to_lanes(right, start + nev + rows)
    facing, inside = facing_ref[...], inside_ref[...]
    to_left = jnp.sum(jnp.where(first, facing, inside) * left, axis=0, keepdims=True)
    to_right = jnp.sum(jnp.where(first, inside, facing) * right, axis=0, keepdims=True)
    added = pltpu.roll(to_left, lax.rem(start - nev + LANES, LANES), 1)
    added = added + pltpu.roll(to_right, lax.rem(start + nev, LANES), 1)
    sub = iota((8, LANES), 0)
    pair = jnp.where(lax.rem(sub, 2) == 0, own, -added)
    for k in range(out_ref.shape[0] // 8):
        out_ref[8 * k : 8 * k + 8, :] = pair


def third_kernel(
    got_ref, q_ref, z_ref, r_ref, coef_ref, e_ref, c_ref,
    q_out_ref, w_ref, v_ref, out_ref, rows_ref, block_ref, group_ref,
):
    nev, rows, columns = e_ref.shape
    half = columns // LANES
    stencil = Stencil(coef_ref)
    z, r = z_ref[...], r_ref[...]
    count = group_ref.shape[0]
    left, right = beside_columns(got_ref, 2, nev, rows)
    q = q_ref[...] - jnp.where(stencil.edges[2], left, 0.0)
    q = q - jnp.where(stencil.edges[3], right, 0.0)
    q_out_ref[...] = q
    added = got_ref[pl.ds(1, count, stride=2), :]
    group_ref[...] = (
        got_ref[pl.ds(0, count, stride=2), :]
        + pltpu.roll(added, 1, 0)
        + pltpu.roll(added, count - 1, 0)
    )
    y = coarse(c_ref, group_ref, nev, 1)
    w = stencil.smooth(q) + prolong(e_ref, y, rows_ref)
    v = stencil.apply(w)
    w_ref[...] = w
    v_ref[...] = v
    low = (stencil.faces[1] * w)[-1:]
    for k in range(half):
        block_ref[k : k + 1, :] = low[:, k * LANES : (k + 1) * LANES]
        block_ref[half + k : half + k + 1, :] = w[:1, k * LANES : (k + 1) * LANES]
    last = to_lanes(w[:, :1], 0) + to_lanes((stencil.faces[3] * w)[:, -1:], rows)
    lane = iota((1, LANES), 1)
    for k, product in enumerate((r * z, z * q, r * w, q * w, w * v)):
        last = jnp.where(lane == 2 * rows + k, total_of(product), last)
    size = block_ref.shape[0]
    block_ref[size - 1 : size, :] = last
    fill(out_ref, block_ref[...])


def fourth_kernel(got_ref, v_ref, coef_ref, v_out_ref, out_ref, block_ref):
    rows, columns = v_ref.shape
    half = columns // LANES
    size = 2 * half + 1
    count = got_ref.shape[0] // size
    z_count = count // 2
    z = lax.axis_index("zh") * 2 + lax.axis_index("zl")
    core = lax.axis_index("core")
    flat = jnp.zeros((half, LANES), jnp.float32)
    for i in range(count - 2):
        at, below = i * size, (i + 2) * size
        flat = flat + got_ref[at : at + half, :] * got_ref[below + half : below + 2 * half, :]
    west = got_ref[pl.ds(2 * half, z_count, stride=2 * size), :]
    east = got_ref[pl.ds(2 * half + size, z_count, stride=2 * size), :]
    facing = jnp.where(iota((z_count, LANES), 1) < rows, pltpu.roll(west, LANES - rows, 1) * east, 0.0)
    between = total_of(flat) + total_of(facing)
    lane = iota((1, LANES), 1)
    sums = jnp.sum(west + east, axis=0, keepdims=True)
    sums = jnp.where(lane == 2 * rows + 4, sums - 2.0 * between, sums)
    pack = LANES // rows
    zr = z_count // pack
    wide = iota((zr, LANES), 1)
    lefts = jnp.zeros((zr, LANES), jnp.float32)
    rights = lefts
    for j in range(pack):
        a = got_ref[pl.ds(2 * half + 2 * size * j, zr, stride=2 * size * pack), :]
        d = got_ref[pl.ds(2 * half + size + 2 * size * j, zr, stride=2 * size * pack), :]
        a = jnp.where(wide < rows, a, 0.0)
        d = jnp.where((wide >= rows) & (wide < 2 * rows), d, 0.0)
        if j > 0:
            a = pltpu.roll(a, rows * j, 1)
        if j != 1:
            d = pltpu.roll(d, (rows * (j - 1)) % LANES, 1)
        lefts, rights = lefts + a, rights + d
    block_ref[:zr, :] = lefts
    block_ref[zr : 2 * zr, :] = rights
    block_ref[2 * zr : 2 * zr + 1, :] = sums
    fill(out_ref, block_ref[...])

    above = jnp.maximum(2 * z - 2 + core, 0) * size
    below = jnp.minimum(2 * z + 2 + core, count - 1) * size + half
    up = jnp.concatenate([got_ref[pl.ds(above + k, 1), :] for k in range(half)], axis=1)
    down = jnp.concatenate([got_ref[pl.ds(below + k, 1), :] for k in range(half)], axis=1)
    up = jnp.where(z > 0, up, 0.0)
    down = jnp.where(z < z_count - 1, down, 0.0) * coef_ref[1, rows - 1 : rows, :]
    partner = got_ref[pl.ds((2 * z + 1 - core) * size + 2 * half, 1), :]
    left, right = to_column(partner, rows, rows), to_column(partner, 0, rows)
    edges = edges_of((rows, columns))
    v = v_ref[...]
    v = v - jnp.where(edges[0], up, 0.0) - jnp.where(edges[1], down, 0.0)
    v = v - jnp.where(edges[2], jnp.where(core == 1, left, 0.0), 0.0)
    v = v - jnp.where(edges[3], jnp.where(core == 0, right, 0.0) * coef_ref[3], 0.0)
    v_out_ref[...] = v


def closing_kernel(got_ref, v_ref, z_ref, w_ref, q_ref, r_ref, coef_ref, x_ref, res_ref):
    rows, columns = v_ref.shape
    pack = LANES // rows
    zr = lax.axis_size("zh") * 2 // pack
    size = 2 * zr + 1
    count = got_ref.shape[0] // size
    z = lax.axis_index("zh") * 2 + lax.axis_index("zl")
    xy, core = lax.axis_index("xy"), lax.axis_index("core")
    sums = got_ref[2 * zr : 2 * zr + 1, :]
    flat = jnp.zeros((zr, LANES), jnp.float32)
    for i in range(1, count):
        at = i * size
        sums = sums + got_ref[at + 2 * zr : at + 2 * zr + 1, :]
        flat = flat + got_ref[at - size + zr : at - size + 2 * zr, :] * got_ref[at : at + zr, :]
    across = total_of(flat)
    lane = iota((1, LANES), 1)
    rz, zq, rw, qw, wv = (
        jnp.sum(jnp.where(lane == 2 * rows + k, sums, 0.0), axis=1, keepdims=True)
        for k in range(5)
    )
    wv = wv - 2.0 * across
    step = rz / zq
    rz_new = rz - step * ((rw + zq) - step * qw)
    grow = 1.0 + rz_new / rz
    curve = grow * grow * zq - 2.0 * grow * step * qw + step * step * wv
    step_next = rz_new / curve
    on_z = step + step_next * grow
    on_w = step_next * step

    left_of, right_of = jnp.maximum(xy - 1, 0), jnp.minimum(xy + 1, count - 1)
    row = z // pack
    position = lax.rem(z, pack) * rows
    left = to_column(got_ref[pl.ds(left_of * size + zr + row, 1), :], position, rows)
    right = to_column(got_ref[pl.ds(right_of * size + row, 1), :], position, rows)
    left = jnp.where((core == 0) & (xy > 0), left, 0.0)
    right = jnp.where((core == 1) & (xy < count - 1), right, 0.0)
    edges = edges_of((rows, columns))
    v = v_ref[...]
    v = v - jnp.where(edges[2], left, 0.0) - jnp.where(edges[3], right * coef_ref[3], 0.0)
    x_ref[...] = on_z * z_ref[...] - on_w * w_ref[...]
    res_ref[...] = r_ref[...] - on_z * q_ref[...] + on_w * v


def call(kernel, name, args, outs, scratch=(), by_hand=False):
    whole = pl.BlockSpec(memory_space=pltpu.VMEM)
    scratch = [pltpu.VMEM(x, jnp.float32) if isinstance(x, tuple) else x for x in scratch]
    return pl.pallas_call(
        kernel,
        out_shape=[jax.ShapeDtypeStruct(shape, jnp.float32) for shape in outs],
        in_specs=[pl.BlockSpec(memory_space=pl.ANY) if by_hand else whole] * len(args),
        out_specs=[whole] * len(outs),
        scratch_shapes=scratch,
        compiler_params=pltpu.CompilerParams(vmem_limit_bytes=VMEM_LIMIT),
        name=name,
    )(*args)


def exchanged(x, axes, rows):
    flat = x.reshape(x.shape[0] // rows, rows * LANES)
    return lax.all_to_all(flat, axes, 0, 0, tiled=True).reshape(x.shape)


def swap_in(x, axis):
    return lax.ppermute(x, axis, [(0, 1), (1, 0)])


def swap_over(x, axes):
    count = lax.axis_size(axes)
    pairs = [(i, i + 1) for i in range(1, count - 1, 2)]
    return lax.ppermute(x, axes, pairs + [(j, i) for i, j in pairs])


def local(right_side, class_map, class_perm, eigenvectors, coarse_inverse):
    rows, columns = right_side.shape
    nev = eigenvectors.shape[0]
    field = (rows, columns)
    group = 2 * lax.axis_size(COLS)
    z_count, chips = lax.axis_size(ROWS), lax.axis_size("xy")
    size = 2 * (columns // LANES) + 1
    size_next = 2 * (z_count * rows // LANES) + 1
    per_vector = (nev, LANES)

    size_first = columns // LANES + 1
    given = (class_perm, right_side, class_map, eigenvectors, coarse_inverse)
    perm, over, facing, inside, message, r, vectors, matrix = call(
        opening_kernel, "opening",
        tuple(pltpu.with_memory_space_constraint(x, pltpu.HBM) for x in given),
        [field, (rows + 8, LANES), (rows, LANES), (rows, LANES), (size_first * group, LANES),
         field, eigenvectors.shape, coarse_inverse.shape],
        [pltpu.SMEM(class_perm.shape, jnp.float32), pltpu.VMEM(field, jnp.int32), per_vector,
         (size_first, LANES), pltpu.SemaphoreType.DMA((4 + PIECES,))],
        by_hand=True,
    )
    over, facing = swap_over(over, ROWS), swap_over(facing, COLS)
    inside = swap_in(inside, "core")
    got = exchanged(message, GROUP, size_first)
    z0, coef, z_over, z_in = call(
        first_kernel, "first", (got, over, perm, r, vectors, matrix),
        [field, (6,) + field, (1, columns), (1, columns)], [per_vector],
    )
    z_over, z_in = swap_over(z_over, ROWS), swap_in(z_in, "zl")
    q0, message = call(
        second_kernel, "second", (z_in, z_over, facing, inside, z0, coef, vectors),
        [field, (2 * group, LANES)], [per_vector],
    )
    got = exchanged(message, GROUP, 2)
    q0, w, v, message = call(
        third_kernel, "third", (got, q0, z0, r, coef, vectors, matrix),
        [field, field, field, (2 * z_count * size, LANES)],
        [per_vector, (size, LANES), (group, LANES)],
    )
    got = exchanged(message, STACK, size)
    v, message = call(
        fourth_kernel, "fourth", (got, v, coef),
        [field, (chips * size_next, LANES)], [(size_next, LANES)],
    )
    got = exchanged(message, PLANE, size_next)
    return tuple(call(closing_kernel, "closing", (got, v, z0, w, q0, r, coef), [field, field]))


def solution(mesh):
    n_gx, n_gy = mesh.devices.shape
    fine = Mesh(mesh.devices.reshape(n_gx // 2, 2, n_gy // 2, 2), FINE)
    in_specs = (P(ROWS, COLS), P(ROWS, COLS), P(), P(None, ROWS, COLS), P(FINE, None))
    out_specs = (P(ROWS, COLS), P(ROWS, COLS))
    return jax.shard_map(local, mesh=fine, in_specs=in_specs, out_specs=out_specs, check_vma=False)
```

```python
import jax
import jax.numpy as jnp
from jax import lax
from jax.experimental import pallas as pl
from jax.experimental.pallas import tpu as pltpu
from jax.sharding import Mesh, PartitionSpec as P

CHEB = 4
REACTION = 0.05
EIGEN_TOP = 2.0
EIGEN_LOW = 0.1
LANES = 128

ROWS = ("zh", "zl")
COLS = ("xy", "core")
GROUP = ("zl", "xy", "core")
STACK = ("zh", "zl", "core")
PLANE = ("xy",)
FINE = ("zh", "zl", "xy", "core")
VMEM_LIMIT = 24 * 1024 * 1024
PIECES = 5


def iota(shape, dim):
    return lax.broadcasted_iota(jnp.int32, shape, dim)


def harmonic(centre, beside):
    return jnp.where(beside > 0.0, 2.0 * centre * beside / (centre + beside), centre)


def shifts(v):
    rows, columns = v.shape
    return (
        pltpu.roll(v, 1, 0),
        pltpu.roll(v, rows - 1, 0),
        pltpu.roll(v, 1, 1),
        pltpu.roll(v, columns - 1, 1),
    )


def edges_of(shape):
    row, column = iota(shape, 0), iota(shape, 1)
    return (row == 0, row == shape[0] - 1, column == 0, column == shape[1] - 1)


class Stencil:
    def __init__(self, coef):
        self.faces = tuple(coef[k] for k in range(4))
        self.diagonal, self.inverse = coef[4], coef[5]
        self.edges = edges_of(self.diagonal.shape)
        self.inner = tuple(
            jnp.where(edge, 0.0, face) for edge, face in zip(self.edges, self.faces)
        )

    def apply(self, v):
        result = self.diagonal * v
        for weight, near in zip(self.inner, shifts(v)):
            result = result - weight * near
        return result

    def smooth(self, source):
        centre = 0.5 * (EIGEN_TOP + EIGEN_LOW)
        radius = 0.5 * (EIGEN_TOP - EIGEN_LOW)
        ratio_start = centre / radius
        factor = 1.0 / ratio_start
        update = source * self.inverse * (1.0 / centre)
        smoothed = update
        for _ in range(1, CHEB):
            defect = source - self.apply(smoothed)
            factor_next = 1.0 / (2.0 * ratio_start - factor)
            update = factor_next * factor * update + (2.0 * factor_next / radius) * (
                defect * self.inverse
            )
            smoothed = smoothed + update
            factor = factor_next
        return smoothed


def to_lanes(column, start):
    n = column.shape[0]
    want = lax.rem(iota((n, LANES), 1) - start + 8 * LANES, LANES)
    hit = want == iota((n, LANES), 0)
    return jnp.sum(jnp.where(hit, column, 0.0), axis=0, keepdims=True)


def to_column(row, start, n):
    want = lax.rem(iota((n, LANES), 1) - start + 8 * LANES, LANES)
    hit = want == iota((n, LANES), 0)
    return jnp.sum(jnp.where(hit, row, 0.0), axis=1, keepdims=True)


def project_one(own, v, rows_ref, e):
    rows, columns = v.shape
    p = own * v
    q = p[:, :LANES]
    for k in range(1, columns // LANES):
        q = q + p[:, k * LANES : (k + 1) * LANES]
    s = q[:8]
    for k in range(1, rows // 8):
        s = s + q[8 * k : 8 * k + 8]
    rows_ref[e : e + 1, :] = jnp.sum(s, axis=0, keepdims=True)


def project(e_ref, v, rows_ref):
    for e in range(e_ref.shape[0]):
        project_one(e_ref[e], v, rows_ref, e)
    return jnp.sum(rows_ref[...], axis=1, keepdims=True)


def coarse(c_ref, gathered_ref, nev, stride):
    dofs = c_ref.shape[1]
    lane = iota((1, LANES), 1)
    total = None
    for r in range(dofs // LANES):
        low = r * LANES // nev
        high = (r * LANES + LANES - 1) // nev
        flat = gathered_ref[low * stride : low * stride + 1, :]
        for d in range(low + 1, high + 1):
            row = gathered_ref[d * stride : d * stride + 1, :]
            flat = jnp.where(lane >= d * nev - r * LANES, row, flat)
        term = c_ref[:, r * LANES : (r + 1) * LANES] * flat
        total = term if total is None else total + term
    return jnp.sum(total, axis=1, keepdims=True)


def prolong(e_ref, y, rows_ref):
    nev = e_ref.shape[0]
    rows_ref[...] = jnp.broadcast_to(y, (nev, LANES))
    reps = e_ref.shape[2] // LANES
    result = None
    for e in range(nev):
        weight = jnp.concatenate([rows_ref[e : e + 1, :]] * reps, axis=1)
        term = weight * e_ref[e]
        result = term if result is None else result + term
    return result


def total_of(v):
    return jnp.sum(jnp.sum(v, axis=0, keepdims=True), axis=1, keepdims=True)


def fill(out_ref, message):
    size = message.shape[0]
    count = out_ref.shape[0] // size
    batch = min(8, count)
    for i in range(batch):
        out_ref[i * size : (i + 1) * size, :] = message
    pattern = out_ref[: batch * size, :]
    for k in range(1, count // batch):
        out_ref[k * batch * size : (k + 1) * batch * size, :] = pattern


def group_place():
    return (lax.axis_index("zl") * lax.axis_size("xy") + lax.axis_index("xy")) * 2 + lax.axis_index(
        "core"
    )


def column_place():
    return lax.axis_index("xy") * 2 + lax.axis_index("core")


def lane_start(place, nev):
    return lax.rem(place * nev, LANES)


def opening_kernel(
    kinds_hbm, r_hbm, map_hbm, e_hbm, c_hbm,
    perm_ref, over_ref, facing_ref, inside_ref, out_ref, r_ref, e_ref, c_ref,
    kinds_ref, map_ref, rows_ref, block_ref, sems,
):
    nev, rows, columns = e_ref.shape
    steps = sems.shape[0] - 4
    chunk = nev // steps
    small = [
        pltpu.make_async_copy(source, target, sems.at[k])
        for k, (source, target) in enumerate(
            ((kinds_hbm, kinds_ref), (map_hbm, map_ref), (r_hbm, r_ref))
        )
    ]
    parts = [
        pltpu.make_async_copy(
            e_hbm.at[pl.ds(k * chunk, chunk)], e_ref.at[pl.ds(k * chunk, chunk)], sems.at[4 + k]
        )
        for k in range(steps)
    ]
    matrix = pltpu.make_async_copy(c_hbm, c_ref, sems.at[3])
    for copy in parts[:2] + small + parts[2:] + [matrix]:
        copy.start()
    for copy in small:
        copy.wait()
    classes = map_ref[...]
    perm = jnp.full(classes.shape, kinds_ref[0])
    for k in range(1, kinds_ref.shape[0]):
        perm = jnp.where(classes == k, kinds_ref[k], perm)
    perm_ref[...] = perm
    upper = lax.axis_index("zl") == 0
    over = jnp.where(upper, perm[:1], perm[-1:])
    within = jnp.where(upper, perm[-1:], perm[:1])
    over_ref[...] = jnp.zeros_like(over_ref)
    for k in range(columns // LANES):
        over_ref[k : k + 1, :] = over[:, k * LANES : (k + 1) * LANES]
    r = r_ref[...]
    first = lax.axis_index("core") == 0
    lane = iota((rows, LANES), 1)
    lefts = jnp.zeros((rows, LANES), jnp.float32)
    rights = lefts
    for k in range(steps):
        parts[k].wait()
        for e in range(k * chunk, (k + 1) * chunk):
            own = e_ref[e]
            project_one(own, r, rows_ref, e)
            both = jnp.where(lane < LANES // 2, own[:, :LANES], own[:, columns - LANES :])
            both = pltpu.roll(both, e, 1) if e > 0 else both
            lefts = jnp.where(lane == e, both, lefts)
            rights = jnp.where(lane == (e - 1) % LANES, both, rights)
    rights = pltpu.roll(rights, 1, 1)
    facing_ref[...] = jnp.where(first, lefts, rights)
    inside_ref[...] = jnp.where(first, rights, lefts)
    c = jnp.sum(rows_ref[...], axis=1, keepdims=True)
    start = lane_start(group_place(), nev)
    size = block_ref.shape[0]
    block_ref[:1, :] = (
        to_lanes(c, start)
        + to_lanes(perm[:, :1], start + nev)
        + to_lanes(perm[:, -1:], start + nev + rows)
    )
    for k in range(size - 1):
        block_ref[k + 1 : k + 2, :] = within[:, k * LANES : (k + 1) * LANES]
    fill(out_ref, block_ref[...])
    matrix.wait()


def beside_columns(got_ref, stride, nev, rows):
    place, b, b_count = group_place(), column_place(), lax.axis_size("xy") * 2
    last = got_ref.shape[0] // stride - 1
    before, after = jnp.maximum(place - 1, 0), jnp.minimum(place + 1, last)
    left = to_column(
        got_ref[pl.ds(before * stride, 1), :], lane_start(before, nev) + nev + rows, rows
    )
    right = to_column(got_ref[pl.ds(after * stride, 1), :], lane_start(after, nev) + nev, rows)
    return jnp.where(b > 0, left, 0.0), jnp.where(b < b_count - 1, right, 0.0)


def first_kernel(
    got_ref, over_ref, perm_ref, r_ref, e_ref, c_ref,
    z_ref, coef_ref, z_over_ref, z_in_ref, rows_ref,
):
    nev, rows, columns = e_ref.shape
    size = columns // LANES + 1
    upper = lax.axis_index("zl") == 0
    left, right = beside_columns(got_ref, size, nev, rows)
    across = lax.axis_size("xy") * 2
    partner = (group_place() + jnp.where(upper, across, -across)) * size
    over = jnp.concatenate([over_ref[k : k + 1, :] for k in range(size - 1)], axis=1)
    within = jnp.concatenate(
        [got_ref[pl.ds(partner + 1 + k, 1), :] for k in range(size - 1)], axis=1
    )
    halo = (jnp.where(upper, over, within), jnp.where(upper, within, over), left, right)
    perm = perm_ref[...]
    edges = edges_of(perm.shape)
    faces = []
    for edge, near, outside in zip(edges, shifts(perm), halo):
        faces.append(harmonic(perm, jnp.where(edge, outside, near)))
    diagonal = REACTION + faces[0] + faces[1] + faces[2] + faces[3]
    coef = faces + [diagonal, 1.0 / diagonal]
    for k in range(6):
        coef_ref[k] = coef[k]
    stencil = Stencil(coef)
    y = coarse(c_ref, got_ref, nev, size)
    z = stencil.smooth(r_ref[...]) + prolong(e_ref, y, rows_ref)
    z_ref[...] = z
    top, low = (faces[0] * z)[:1], (faces[1] * z)[-1:]
    z_over_ref[...] = jnp.where(upper, top, low)
    z_in_ref[...] = jnp.where(upper, low, top)


def second_kernel(
    z_in_ref, z_over_ref, facing_ref, inside_ref, z_ref, coef_ref, e_ref, q_ref, out_ref, rows_ref
):
    nev, rows, _ = e_ref.shape
    upper = lax.axis_index("zl") == 0
    first = lax.axis_index("core") == 0
    stencil = Stencil(coef_ref)
    over, within = z_over_ref[...], z_in_ref[...]
    z = z_ref[...]
    q = stencil.apply(z)
    q = q - jnp.where(stencil.edges[0], jnp.where(upper, over, within), 0.0)
    q = q - jnp.where(stencil.edges[1], jnp.where(upper, within, over), 0.0)
    q_ref[...] = q
    left, right = (stencil.faces[2] * z)[:, :1], (stencil.faces[3] * z)[:, -1:]
    start = lane_start(group_place(), nev)
    own = to_lanes(project(e_ref, q, rows_ref), start)
    own = own + to_lanes(left, start + nev) + to_lanes(right, start + nev + rows)
    facing, inside = facing_ref[...], inside_ref[...]
    to_left = jnp.sum(jnp.where(first, facing, inside) * left, axis=0, keepdims=True)
    to_right = jnp.sum(jnp.where(first, inside, facing) * right, axis=0, keepdims=True)
    added = pltpu.roll(to_left, lax.rem(start - nev + LANES, LANES), 1)
    added = added + pltpu.roll(to_right, lax.rem(start + nev, LANES), 1)
    sub = iota((8, LANES), 0)
    pair = jnp.where(lax.rem(sub, 2) == 0, own, -added)
    for k in range(out_ref.shape[0] // 8):
        out_ref[8 * k : 8 * k + 8, :] = pair


def third_kernel(
    got_ref, q_ref, z_ref, r_ref, coef_ref, e_ref, c_ref,
    q_out_ref, w_ref, v_ref, out_ref, rows_ref, block_ref, group_ref,
):
    nev, rows, columns = e_ref.shape
    half = columns // LANES
    stencil = Stencil(coef_ref)
    z, r = z_ref[...], r_ref[...]
    count = group_ref.shape[0]
    left, right = beside_columns(got_ref, 2, nev, rows)
    q = q_ref[...] - jnp.where(stencil.edges[2], left, 0.0)
    q = q - jnp.where(stencil.edges[3], right, 0.0)
    q_out_ref[...] = q
    added = got_ref[pl.ds(1, count, stride=2), :]
    group_ref[...] = (
        got_ref[pl.ds(0, count, stride=2), :]
        + pltpu.roll(added, 1, 0)
        + pltpu.roll(added, count - 1, 0)
    )
    y = coarse(c_ref, group_ref, nev, 1)
    w = stencil.smooth(q) + prolong(e_ref, y, rows_ref)
    v = stencil.apply(w)
    w_ref[...] = w
    v_ref[...] = v
    low = (stencil.faces[1] * w)[-1:]
    for k in range(half):
        block_ref[k : k + 1, :] = low[:, k * LANES : (k + 1) * LANES]
        block_ref[half + k : half + k + 1, :] = w[:1, k * LANES : (k + 1) * LANES]
    last = to_lanes(w[:, :1], 0) + to_lanes((stencil.faces[3] * w)[:, -1:], rows)
    lane = iota((1, LANES), 1)
    for k, product in enumerate((r * z, z * q, r * w, q * w, w * v)):
        last = jnp.where(lane == 2 * rows + k, total_of(product), last)
    size = block_ref.shape[0]
    block_ref[size - 1 : size, :] = last
    fill(out_ref, block_ref[...])


def fourth_kernel(got_ref, v_ref, coef_ref, v_out_ref, out_ref, block_ref):
    rows, columns = v_ref.shape
    half = columns // LANES
    size = 2 * half + 1
    count = got_ref.shape[0] // size
    z_count = count // 2
    z = lax.axis_index("zh") * 2 + lax.axis_index("zl")
    core = lax.axis_index("core")
    flat = jnp.zeros((half, LANES), jnp.float32)
    for i in range(count - 2):
        at, below = i * size, (i + 2) * size
        flat = flat + got_ref[at : at + half, :] * got_ref[below + half : below + 2 * half, :]
    west = got_ref[pl.ds(2 * half, z_count, stride=2 * size), :]
    east = got_ref[pl.ds(2 * half + size, z_count, stride=2 * size), :]
    facing = jnp.where(iota((z_count, LANES), 1) < rows, pltpu.roll(west, LANES - rows, 1) * east, 0.0)
    between = total_of(flat) + total_of(facing)
    lane = iota((1, LANES), 1)
    sums = jnp.sum(west + east, axis=0, keepdims=True)
    sums = jnp.where(lane == 2 * rows + 4, sums - 2.0 * between, sums)
    pack = LANES // rows
    zr = z_count // pack
    wide = iota((zr, LANES), 1)
    lefts = jnp.zeros((zr, LANES), jnp.float32)
    rights = lefts
    for j in range(pack):
        a = got_ref[pl.ds(2 * half + 2 * size * j, zr, stride=2 * size * pack), :]
        d = got_ref[pl.ds(2 * half + size + 2 * size * j, zr, stride=2 * size * pack), :]
        a = jnp.where(wide < rows, a, 0.0)
        d = jnp.where((wide >= rows) & (wide < 2 * rows), d, 0.0)
        if j > 0:
            a = pltpu.roll(a, rows * j, 1)
        if j != 1:
            d = pltpu.roll(d, (rows * (j - 1)) % LANES, 1)
        lefts, rights = lefts + a, rights + d
    block_ref[:zr, :] = lefts
    block_ref[zr : 2 * zr, :] = rights
    block_ref[2 * zr : 2 * zr + 1, :] = sums
    fill(out_ref, block_ref[...])

    above = jnp.maximum(2 * z - 2 + core, 0) * size
    below = jnp.minimum(2 * z + 2 + core, count - 1) * size + half
    up = jnp.concatenate([got_ref[pl.ds(above + k, 1), :] for k in range(half)], axis=1)
    down = jnp.concatenate([got_ref[pl.ds(below + k, 1), :] for k in range(half)], axis=1)
    up = jnp.where(z > 0, up, 0.0)
    down = jnp.where(z < z_count - 1, down, 0.0) * coef_ref[1, rows - 1 : rows, :]
    partner = got_ref[pl.ds((2 * z + 1 - core) * size + 2 * half, 1), :]
    left, right = to_column(partner, rows, rows), to_column(partner, 0, rows)
    edges = edges_of((rows, columns))
    v = v_ref[...]
    v = v - jnp.where(edges[0], up, 0.0) - jnp.where(edges[1], down, 0.0)
    v = v - jnp.where(edges[2], jnp.where(core == 1, left, 0.0), 0.0)
    v = v - jnp.where(edges[3], jnp.where(core == 0, right, 0.0) * coef_ref[3], 0.0)
    v_out_ref[...] = v


def closing_kernel(got_ref, v_ref, z_ref, w_ref, q_ref, r_ref, coef_ref, x_ref, res_ref):
    rows, columns = v_ref.shape
    pack = LANES // rows
    zr = lax.axis_size("zh") * 2 // pack
    size = 2 * zr + 1
    count = got_ref.shape[0] // size
    z = lax.axis_index("zh") * 2 + lax.axis_index("zl")
    xy, core = lax.axis_index("xy"), lax.axis_index("core")
    sums = got_ref[2 * zr : 2 * zr + 1, :]
    flat = jnp.zeros((zr, LANES), jnp.float32)
    for i in range(1, count):
        at = i * size
        sums = sums + got_ref[at + 2 * zr : at + 2 * zr + 1, :]
        flat = flat + got_ref[at - size + zr : at - size + 2 * zr, :] * got_ref[at : at + zr, :]
    across = total_of(flat)
    lane = iota((1, LANES), 1)
    rz, zq, rw, qw, wv = (
        jnp.sum(jnp.where(lane == 2 * rows + k, sums, 0.0), axis=1, keepdims=True)
        for k in range(5)
    )
    wv = wv - 2.0 * across
    step = rz / zq
    rz_new = rz - step * ((rw + zq) - step * qw)
    grow = 1.0 + rz_new / rz
    curve = grow * grow * zq - 2.0 * grow * step * qw + step * step * wv
    step_next = rz_new / curve
    on_z = step + step_next * grow
    on_w = step_next * step

    left_of, right_of = jnp.maximum(xy - 1, 0), jnp.minimum(xy + 1, count - 1)
    row = z // pack
    position = lax.rem(z, pack) * rows
    left = to_column(got_ref[pl.ds(left_of * size + zr + row, 1), :], position, rows)
    right = to_column(got_ref[pl.ds(right_of * size + row, 1), :], position, rows)
    left = jnp.where((core == 0) & (xy > 0), left, 0.0)
    right = jnp.where((core == 1) & (xy < count - 1), right, 0.0)
    edges = edges_of((rows, columns))
    v = v_ref[...]
    v = v - jnp.where(edges[2], left, 0.0) - jnp.where(edges[3], right * coef_ref[3], 0.0)
    x_ref[...] = on_z * z_ref[...] - on_w * w_ref[...]
    res_ref[...] = r_ref[...] - on_z * q_ref[...] + on_w * v


def call(kernel, name, args, outs, scratch=(), by_hand=False):
    whole = pl.BlockSpec(memory_space=pltpu.VMEM)
    scratch = [pltpu.VMEM(x, jnp.float32) if isinstance(x, tuple) else x for x in scratch]
    return pl.pallas_call(
        kernel,
        out_shape=[jax.ShapeDtypeStruct(shape, jnp.float32) for shape in outs],
        in_specs=[pl.BlockSpec(memory_space=pl.ANY) if by_hand else whole] * len(args),
        out_specs=[whole] * len(outs),
        scratch_shapes=scratch,
        compiler_params=pltpu.CompilerParams(vmem_limit_bytes=VMEM_LIMIT),
        name=name,
    )(*args)


def exchanged(x, axes, rows):
    flat = x.reshape(x.shape[0] // rows, rows * LANES)
    return lax.all_to_all(flat, axes, 0, 0, tiled=True).reshape(x.shape)


def swap_in(x, axis):
    return lax.ppermute(x, axis, [(0, 1), (1, 0)])


def swap_over(x, axes):
    count = lax.axis_size(axes)
    pairs = [(i, i + 1) for i in range(1, count - 1, 2)]
    return lax.ppermute(x, axes, pairs + [(j, i) for i, j in pairs])


def local(right_side, class_map, class_perm, eigenvectors, coarse_inverse):
    rows, columns = right_side.shape
    nev = eigenvectors.shape[0]
    field = (rows, columns)
    group = 2 * lax.axis_size(COLS)
    z_count, chips = lax.axis_size(ROWS), lax.axis_size("xy")
    size = 2 * (columns // LANES) + 1
    size_next = 2 * (z_count * rows // LANES) + 1
    per_vector = (nev, LANES)

    size_first = columns // LANES + 1
    given = (class_perm, right_side, class_map, eigenvectors, coarse_inverse)
    perm, over, facing, inside, message, r, vectors, matrix = call(
        opening_kernel, "opening",
        tuple(pltpu.with_memory_space_constraint(x, pltpu.HBM) for x in given),
        [field, (rows + 8, LANES), (rows, LANES), (rows, LANES), (size_first * group, LANES),
         field, eigenvectors.shape, coarse_inverse.shape],
        [pltpu.SMEM(class_perm.shape, jnp.float32), pltpu.VMEM(field, jnp.int32), per_vector,
         (size_first, LANES), pltpu.SemaphoreType.DMA((4 + PIECES,))],
        by_hand=True,
    )
    over, facing = swap_over(over, ROWS), swap_over(facing, COLS)
    inside = swap_in(inside, "core")
    got = exchanged(message, GROUP, size_first)
    z0, coef, z_over, z_in = call(
        first_kernel, "first", (got, over, perm, r, vectors, matrix),
        [field, (6,) + field, (1, columns), (1, columns)], [per_vector],
    )
    z_over, z_in = swap_over(z_over, ROWS), swap_in(z_in, "zl")
    q0, message = call(
        second_kernel, "second", (z_in, z_over, facing, inside, z0, coef, vectors),
        [field, (2 * group, LANES)], [per_vector],
    )
    got = exchanged(message, GROUP, 2)
    q0, w, v, message = call(
        third_kernel, "third", (got, q0, z0, r, coef, vectors, matrix),
        [field, field, field, (2 * z_count * size, LANES)],
        [per_vector, (size, LANES), (group, LANES)],
    )
    got = exchanged(message, STACK, size)
    v, message = call(
        fourth_kernel, "fourth", (got, v, coef),
        [field, (chips * size_next, LANES)], [(size_next, LANES)],
    )
    got = exchanged(message, PLANE, size_next)
    return tuple(call(closing_kernel, "closing", (got, v, z0, w, q0, r, coef), [field, field]))


def solution(mesh):
    n_gx, n_gy = mesh.devices.shape
    fine = Mesh(mesh.devices.reshape(n_gx // 2, 2, n_gy // 2, 2), FINE)
    in_specs = (P(ROWS, COLS), P(ROWS, COLS), P(), P(None, ROWS, COLS), P(FINE, None))
    out_specs = (P(ROWS, COLS), P(ROWS, COLS))
    return jax.shard_map(local, mesh=fine, in_specs=in_specs, out_specs=out_specs, check_vma=False)
```
